128 devices in a mesh: lon: 8 (over x, y_lo), lat: 16 (over z, y_hi, core).
Axes of the slice: x: 4, y: 4 (y_hi: 2, y_lo: 2; y = y_hi * 2 + y_lo), z: 4, core: 2. Of those that a mesh axis runs over, the one named last changes fastest.
Arguments:
- adj_final: float32 [36, 30, 64, 1024], P(None, None, 'lat', 'lon'), may hold values from -6 to 6
- saved: bfloat16 [3, 36, 30, 64, 1024], P(None, None, None, 'lat', 'lon'), may hold values from 0.099609375 to 10
- beta: float32 [36, 30], replicated, may hold values from 0 to 0.6
- sea_mask: int32 [64, 1024], P('lat', 'lon'), may hold values 0 or 1
- ice_mask: int32 [64, 1024], P('lat', 'lon'), may hold values 0 or 1
- obs_count: int32 [128, 128], P(('lon', 'lat')), may hold values from 0 to 4, as said below
- obs_cell: int32 [128, 512], P(('lon', 'lat')), may hold values from 0 to 65535, as said below
- obs_value: float32 [128, 512], P(('lon', 'lat')), may hold values from -3000 to 3000
Outputs:
- adj_start: float32 [36, 30, 64, 1024], P(None, None, 'lat', 'lon')
The draws below stay inside these ranges and needn't reach their ends.
Inputs may be any that keep to these rules, and one draw needn't show every extreme that they name: `obs_count`: each entry is at most 4; in every row some entry equals 4, and one column equals 4 in every row. `obs_cell`: row s lists its observations grouped by tile in device order: the first obs_count[s,0] entries lie in the tile of device 0, the next obs_count[s,1] in that of device 1, and so on, where the device of lon index a and lat index b is number a times the lat axis size plus b and holds rows b * 4 to (b + 1) * 4 - 1 and longitudes a 128 to (a + 1) * 128 - 1. Entries after these are ignored.
All inputs are finite; a program needn't handle non-finite values. No bound on the sum of `sea_mask` or of `ice_mask` on one device may be relied on, other than what follows from the above.
Results may differ from the reference program's by a relative error of at most 0.0003.
Values sent between devices are 32-bit elements; how exact they have to be, the bound alone decides.
No kernel may reach another device: no remote copies, remote signals or barrier semaphores. Data moves between devices by JAX's collectives and lax.ppermute only.
A program may use at most 192 MiB of HBM per device.

```python
import math
import jax
import jax.numpy as jnp
from jax import lax

NDIR = 36
NFREQ = 30
LON_DEV = 128
LAT_DEV = 4
STEPS = 2
CAP = 4
NLAT = 64
NLON = 1024
SLOTS = 512
N_LON = 8
N_LAT = 16
DEVICES = 128


def obs_layout(key):
    first_key, second_key, third_key, fourth_key = jax.random.split(key, 4)
    base = jax.random.randint(first_key, (DEVICES, DEVICES), 0, CAP + 1)
    keeper = (jax.random.randint(second_key, (DEVICES, DEVICES), 0, 4) < 3).astype(jnp.int32)
    counts = base * keeper
    hottest = jax.random.randint(third_key, (), 0, DEVICES)
    shuffled = jax.random.permutation(fourth_key, DEVICES)
    columns = jnp.arange(DEVICES)
    filled = (columns[None, :] == hottest) | (columns[None, :] == shuffled[:, None])
    return jnp.where(filled, CAP, counts).astype(jnp.int32)


def draw_obs_count(key, part):
    return obs_layout(key)


def draw_obs_cell(key, part):
    counts = obs_layout(key)
    key = jax.random.fold_in(key, 5)
    row_key, col_key = jax.random.split(key)
    ends = jnp.cumsum(counts, axis=1)
    slot_ids = jnp.arange(SLOTS)
    owner = jnp.sum((slot_ids[None, :, None] >= ends[:, None, :]).astype(jnp.int32), axis=2)
    owner = jnp.minimum(owner, DEVICES - 1)
    lon_owner = owner // N_LAT
    lat_owner = owner % N_LAT
    row_pick = lat_owner * LAT_DEV + jax.random.randint(row_key, (DEVICES, SLOTS), 0, LAT_DEV)
    col_pick = lon_owner * LON_DEV + jax.random.randint(col_key, (DEVICES, SLOTS), 0, LON_DEV)
    return (row_pick * (LON_DEV * N_LON) + col_pick).astype(jnp.int32)


def with_ends(array, stream_key, least, high):
    index_at = [jax.random.randint(jax.random.fold_in(stream_key, axis), (), 0, length) for axis, length in enumerate(array.shape)]
    main_axis = array.shape.index(max(array.shape))
    beside = index_at[:main_axis] + [(index_at[main_axis] + 1) % array.shape[main_axis]] + index_at[main_axis + 1:]
    return array.at[tuple(index_at)].set(least).at[tuple(beside)].set(high)


def steps_of(rng, shape, shards, smallest, largest):
    factor_of = 1.0
    for dim, shards_of in shards:
        steps = jax.random.uniform(jax.random.fold_in(jax.random.fold_in(rng, 6), dim), (shards_of,), jnp.float32, smallest / len(shards), largest / len(shards))
        factor_of = factor_of * jnp.repeat(jnp.exp(steps), shape[dim] // shards_of).reshape((-1,) + (1,) * (len(shape) - 1 - dim))
    return factor_of


def scatter_about(key, dims, width, reach, shards=(), held_as=jnp.bfloat16):
    drawn = width * jax.random.normal(key, dims, jnp.float32)
    if shards:
        drawn = drawn * steps_of(key, dims, shards, -0.22, 0.18)
    return jnp.clip(drawn, -reach, reach).astype(held_as)


def setup_inputs(seed: int = 0) -> dict:
    key_list = jax.random.split(jax.random.key(seed), 9)
    adj_final = scatter_about(key_list[0], (NDIR, NFREQ, NLAT, NLON), 1.0, 6.0, ((2, 16), (3, 8)), jnp.float32)
    saved = jnp.clip(jnp.exp(math.log(10.0) - 4.609084 * jax.random.uniform(key_list[1], (STEPS + 1, NDIR, NFREQ, NLAT, NLON), jnp.float32) ** steps_of(key_list[1], (STEPS + 1, NDIR, NFREQ, NLAT, NLON), ((3, 16), (4, 8)), -0.2, 0.2)), 0.099609375, 10.0).astype(jnp.bfloat16)
    beta = jnp.clip(jax.random.uniform(key_list[2], (NDIR, NFREQ), jnp.float32, 0.0, 0.6), 0.0, 0.6)
    sea_mask = with_ends((jax.random.randint(key_list[3], (NLAT, NLON), 0, 5) < 4).astype(jnp.int32), jax.random.fold_in(key_list[3], 1), 0, 1)
    ice_mask = with_ends((jax.random.randint(key_list[4], (NLAT, NLON), 0, 8) < 1).astype(jnp.int32), jax.random.fold_in(key_list[4], 1), 0, 1)
    obs_count = draw_obs_count(jax.random.fold_in(key_list[8], 71), 0)
    obs_cell = draw_obs_cell(jax.random.fold_in(key_list[8], 71), 0)
    obs_value = scatter_about(key_list[7], (DEVICES, SLOTS), 500.0, 3000.0, ((0, 128),), jnp.float32)
    return {"adj_final": adj_final, "saved": saved, "beta": beta, "sea_mask": sea_mask, "ice_mask": ice_mask, "obs_count": obs_count, "obs_cell": obs_cell, "obs_value": obs_value}


def geometry(directions, frequencies, rows, total_rows):
    angles = (jnp.arange(directions, dtype=jnp.float32) + 0.5) * (2.0 * math.pi / directions)
    speeds = jnp.power(jnp.float32(1.1), -jnp.arange(frequencies, dtype=jnp.float32))
    latitude = (rows.astype(jnp.float32) + 0.5 - total_rows / 2.0) * (100.0 / total_rows)
    stretch = math.cos(50.0 * math.pi / 180.0) / jnp.cos(latitude * (math.pi / 180.0))
    ax_part = 0.7 * speeds[None, :, None, None] * jnp.abs(jnp.cos(angles))[:, None, None, None] * stretch[None, None, :, None]
    ay_part = 0.6 * speeds[None, :, None, None] * jnp.abs(jnp.sin(angles))[:, None, None, None]
    growth = jnp.power(jnp.float32(1.1), jnp.arange(frequencies, dtype=jnp.float32))
    weights = (growth / (directions * jnp.sum(growth)))[None, :, None, None]
    east_ward = (jnp.cos(angles) > 0)[:, None, None, None]
    north_ward = (jnp.sin(angles) > 0)[:, None, None, None]
    return (ax_part, ay_part, weights, east_ward, north_ward)

def reference(adj_final, saved, beta, sea_mask, ice_mask, obs_count, obs_cell, obs_value):
    directions, frequencies = (NDIR, NFREQ)
    ax_part, ay_part, weights, east_ward, north_ward = geometry(directions, frequencies, jnp.arange(NLAT), NLAT)
    totals = lax.optimization_barrier(jnp.sum(obs_count, axis=1))
    valid = jnp.arange(SLOTS)[None, :] < totals[:, None]
    force = jnp.zeros((NLAT * NLON,), jnp.float32).at[obs_cell.reshape(-1)].add(jnp.where(valid, obs_value, jnp.float32(0.0)).reshape(-1)).reshape(NLAT, NLON)
    sea = sea_mask.astype(jnp.float32)
    rate = 1.0 - ice_mask.astype(jnp.float32)
    final = saved[STEPS].astype(jnp.float32)
    moment = lax.optimization_barrier(jnp.sum(weights * final, axis=(0, 1)))
    lam = adj_final + sea * force * 2.0 * weights / jnp.sqrt(moment)
    beta_full = beta[:, :, None, None]
    zero_row = jnp.zeros((directions, frequencies, 1, NLON), jnp.float32)
    for step_index in reversed(range(STEPS)):
        adjoint = sea * lam
        east_side = jnp.roll(adjoint, -1, axis=3)
        west_side = jnp.roll(adjoint, 1, axis=3)
        north_side = jnp.concatenate([adjoint[:, :, 1:], zero_row], axis=2)
        south_side = jnp.concatenate([zero_row, adjoint[:, :, :-1]], axis=2)
        moved = (1.0 - ax_part - ay_part) * adjoint + ax_part * jnp.where(east_ward, east_side, west_side) + ay_part * jnp.where(north_ward, north_side, south_side)
        spectrum = saved[step_index].astype(jnp.float32)
        energy = lax.optimization_barrier(jnp.sum(weights * spectrum, axis=(0, 1)))
        coupling = lax.optimization_barrier(jnp.sum(spectrum * moved, axis=(0, 1)))
        lam = moved * (1.0 + rate * (beta_full - 0.2 * energy)) - rate * 0.2 * weights * coupling
    return lam
```

```python
import math

import jax
import jax.numpy as jnp
import numpy as np
from jax import lax
from jax.experimental import pallas as pl
from jax.experimental.pallas import tpu as pltpu
from jax.sharding import PartitionSpec as P

STEPS = 2
CAP = 4
NDIR = 36
NFREQ = 30
PAIRS = NFREQ // 2
LAT = 4
LON = 128
ROWS = NDIR * NFREQ * LAT
HALF = NDIR * NFREQ // 2
HALO = 552
SOUTH0 = 536
N_LAT = 16
N_LON = 8
MIB = 2**20
F32 = jnp.float32

VMEM = pl.BlockSpec(memory_space=pltpu.VMEM)
SMEM = pl.BlockSpec(memory_space=pltpu.SMEM)

SEGMENTS = (
    (0, 4, True, True, True),
    (4, 5, True, True, False),
    (5, 9, True, False, False),
    (9, 13, False, False, False),
    (13, 14, False, False, True),
    (14, 18, False, True, True),
)


def constant_tables():
    angle = (np.arange(NDIR) + 0.5) * (2.0 * math.pi / NDIR)
    per_direction = np.stack([0.7 * np.abs(np.cos(angle)), 0.6 * np.abs(np.sin(angle))])
    j = np.arange(NFREQ)
    speed = 1.1 ** (-j.astype(np.float64))
    growth = 1.1 ** j.astype(np.float64)
    weight = growth / (NDIR * growth.sum())
    rows = np.arange(N_LAT * LAT)
    latitude = (rows + 0.5 - N_LAT * LAT / 2.0) * (100.0 / (N_LAT * LAT))
    stretch = math.cos(50.0 * math.pi / 180.0) / np.cos(latitude * (math.pi / 180.0))
    stretch = np.tile(stretch.reshape(N_LAT, 1, LAT), (1, 2, 1)).reshape(-1)
    column = np.concatenate([np.repeat(speed, LAT), np.repeat(weight, LAT), stretch])
    table = np.tile(column[:, None], (1, LON))
    return per_direction.astype(np.float32), table.astype(np.float32)


SPEED0, WEIGHT0, STRETCH0 = 0, NFREQ * LAT, 2 * NFREQ * LAT


def iotas():
    sub = lax.broadcasted_iota(jnp.int32, (8, LON), 0)
    lane = lax.broadcasted_iota(jnp.int32, (8, LON), 1)
    return sub, lane


def lon_slot(k, east):
    place = jnp.where(k < 9, k, k - 18) if east else k - 9
    return 8 * (place // 8), (place % 8) * PAIRS


def pack_edge(ref, k, east, edge_columns, lane):
    row, base = lon_slot(k, east)
    row = pl.multiple_of(row, 8)
    block = ref[pl.ds(row, 8), :]
    for jp, column in enumerate(edge_columns):
        block = jnp.where(lane == base + jp, column, block)
    ref[pl.ds(row, 8), :] = block


def extract_rows(src, r, first, dst, scale):
    def body(m, carry):
        for u in range(4):
            start = (first + 8 * (4 * m + u)) * LAT + r
            dst[pl.ds(pl.multiple_of(8 * (4 * m + u), 8), 8), :] = (
                src[pl.ds(start, 8, stride=LAT), :] * scale
            )
        return carry

    lax.fori_loop(0, 17, body, 0)


def send_rows(par, src, on_ref, off_ref, field, scale8):
    def put(dst, r, first):
        extract_rows(src, r, first, dst, scale8[r : r + 1, :])
        dst[pl.ds(544, 8), :] = jnp.broadcast_to(field[r : r + 1, :], (8, LON))

    @pl.when(par == 0)
    def _():
        put(on_ref, LAT - 1, SOUTH0)
        put(off_ref, 0, 0)

    @pl.when(par == 1)
    def _():
        put(on_ref, 0, 0)
        put(off_ref, LAT - 1, SOUTH0)


def take_rows(par, on_ref, off_ref, north_ref, south_ref):
    @pl.when(par == 0)
    def _():
        north_ref[...] = on_ref[...]
        south_ref[...] = off_ref[...]

    @pl.when(par == 1)
    def _():
        north_ref[...] = off_ref[...]
        south_ref[...] = on_ref[...]


def pick_observations(count_ref, cell_ref, value_ref, out_ref):
    sub = lax.broadcasted_iota(jnp.int32, (128, 128), 0)
    lane = lax.broadcasted_iota(jnp.int32, (128, 128), 1)
    counts = jnp.broadcast_to(count_ref[...].astype(F32), (128, 128))
    starts = jnp.sum(jnp.where(lane < sub, counts, 0.0), axis=1, keepdims=True)
    mine = jnp.sum(jnp.where(lane == sub, counts, 0.0), axis=1, keepdims=True)
    cell = cell_ref[...]
    local = (((cell >> 10) & (LAT - 1)) * LON + (cell & (LON - 1))).astype(F32)
    value = value_ref[...]
    slots = cell.shape[1]
    slot = lax.broadcasted_iota(jnp.int32, (128, slots), 1).astype(F32)
    listed = jnp.zeros((128, 128), F32)
    for i in range(CAP):
        hit = slot == starts + float(i)
        index_i = jnp.sum(jnp.where(hit, local, 0.0), axis=1, keepdims=True)
        value_i = jnp.sum(jnp.where(hit, value, 0.0), axis=1, keepdims=True)
        value_i = jnp.where(mine > float(i), value_i, 0.0)
        listed = jnp.where(lane == i, index_i, listed)
        listed = jnp.where(lane == CAP + i, value_i, listed)
    out = listed
    for place, shift in enumerate((127, 1, 128 - N_LAT, N_LAT)):
        moved = pltpu.roll(listed, shift, axis=0)
        out = out + pltpu.roll(moved, 8 * (place + 1), axis=1)
    out_ref[...] = out


def start_kernel(
    where_ref, adj_ref, final_ref, table_ref, sea_ref, count_ref, cell_ref, value_ref,
    on_ref, off_ref, west_ref, east_ref, obs_ref, field_ref, sea8_ref,
):
    par = where_ref[0] % 2
    sub, lane = iotas()
    sea = sea_ref[...].astype(F32)
    sea8 = jnp.concatenate([sea, sea], axis=0)
    sea8_ref[...] = sea8

    def moment_body(p, total):
        for q in range(PAIRS):
            both = final_ref[pl.ds(pl.multiple_of(p * 240 + 16 * q, 16), 16), :].astype(F32)
            for h in range(2):
                jp = (2 * q + h) % PAIRS
                total = total + table_ref[WEIGHT0 + 8 * jp : WEIGHT0 + 8 * jp + 8, :] * both[8 * h : 8 * h + 8, :]
        return total

    total = lax.fori_loop(0, NDIR // 2, moment_body, jnp.zeros((8, LON), F32))
    moment = total + pltpu.roll(total, 4, axis=0)
    field = sea8 * 2.0 / jnp.sqrt(moment)
    field_ref[...] = field
    send_rows(par, adj_ref, on_ref, off_ref, field_ref, sea8_ref)

    west_ref[...] = jnp.zeros_like(west_ref)
    east_ref[...] = jnp.zeros_like(east_ref)
    for lo, hi, north, first_east, second_east in SEGMENTS:

        def body(p, carry):
            for h, east in enumerate((first_east, second_east)):
                k = 2 * p + h
                columns = []
                for jp in range(PAIRS):
                    row = pl.multiple_of(p * 240 + 8 * (h * PAIRS + jp), 8)
                    x = adj_ref[pl.ds(row, 8), :] * sea8
                    columns.append(x[:, :1] if east else x[:, LON - 1 :])
                pack_edge(west_ref if east else east_ref, k, east, columns, lane)
            return carry

        lax.fori_loop(lo, hi, body, 0)
    west_ref[24:32, :] = jnp.broadcast_to(field[:, :1], (8, LON))
    east_ref[24:32, :] = jnp.broadcast_to(field[:, LON - 1 :], (8, LON))
    pick_observations(count_ref, cell_ref, value_ref, obs_ref)


def move(
    src_ref, dst_ref, spectrum_ref, table_ref, gx_ref, coef_ref, lon_east_ref, lon_west_ref,
    north_ref, south_ref, sub, lane, scale8=None, add_ref=None, row_add=None, lon_add=None,
):
    upper = sub >= LAT
    row_of = sub % LAT
    carry = (jnp.zeros((8, LON), F32), jnp.zeros((8, LON), F32))
    for lo, hi, north, first_east, second_east in SEGMENTS:

        def body(p, carry):
            coupling, energy = carry
            halo_ref = north_ref if north else south_ref
            both = None
            for h, east in enumerate((first_east, second_east)):
                k = 2 * p + h
                east_speed = coef_ref[0, k]
                north_speed = coef_ref[1, k]
                row, base = lon_slot(k, east)
                block = (lon_east_ref if east else lon_west_ref)[pl.ds(pl.multiple_of(row, 8), 8), :]
                block = pltpu.roll(block, (LON - base) % LON, axis=1)
                for jp in range(PAIRS):
                    n = h * PAIRS + jp
                    tab = slice(8 * jp, 8 * jp + 8)
                    place = pl.ds(pl.multiple_of(p * 240 + 8 * n, 8), 8)
                    if n % 2 == 0:
                        both = spectrum_ref[
                            pl.ds(pl.multiple_of(p * 240 + 8 * n, 16), 16), :
                        ].astype(F32)
                    spectrum = both[8 * (n % 2) : 8 * (n % 2) + 8, :]
                    mu = src_ref[place, :]
                    if scale8 is not None:
                        mu = mu * scale8 + add_ref[tab, :]
                    lon_halo = block[:, jp : jp + 1]
                    first = k * NFREQ + 2 * jp - (0 if north else SOUTH0)
                    row_halo = jnp.where(
                        upper, halo_ref[pl.ds(first + 1, 1), :], halo_ref[pl.ds(first, 1), :]
                    )
                    if lon_add is not None:
                        lon_halo = lon_halo + lon_add[0 if east else 1][tab, :]
                        row_halo = row_halo + row_add[0 if north else 1][tab, :]
                    if east:
                        along = jnp.where(lane == LON - 1, lon_halo, pltpu.roll(mu, LON - 1, axis=1))
                    else:
                        along = jnp.where(lane == 0, lon_halo, pltpu.roll(mu, 1, axis=1))
                    if north:
                        across = jnp.where(row_of == LAT - 1, row_halo, pltpu.roll(mu, 7, axis=0))
                    else:
                        across = jnp.where(row_of == 0, row_halo, pltpu.roll(mu, 1, axis=0))
                    ax = gx_ref[tab, :] * east_speed
                    ay = table_ref[tab, :] * north_speed
                    nu = mu + ax * (along - mu) + ay * (across - mu)
                    dst_ref[place, :] = nu
                    coupling = coupling + spectrum * nu
                    energy = energy + table_ref[WEIGHT0 + 8 * jp : WEIGHT0 + 8 * jp + 8, :] * spectrum
            return coupling, energy

        carry = lax.fori_loop(lo, hi, body, carry)
    coupling, energy = carry
    return coupling + pltpu.roll(coupling, 4, axis=0), energy + pltpu.roll(energy, 4, axis=0)


def set_speeds(where_ref, table_ref, gx_ref):
    place = pl.multiple_of(STRETCH0 + 8 * where_ref[0], 8)
    stretch = table_ref[pl.ds(place, 8), :]
    for jp in range(PAIRS):
        gx_ref[8 * jp : 8 * jp + 8, :] = table_ref[8 * jp : 8 * jp + 8, :] * stretch


def set_weighted(table_ref, field, dst_ref):
    for jp in range(PAIRS):
        tab = slice(8 * jp, 8 * jp + 8)
        dst_ref[tab, :] = table_ref[WEIGHT0 + 8 * jp : WEIGHT0 + 8 * jp + 8, :] * field


def rates(beta_ref, k, jp, upper):
    return jnp.where(upper, beta_ref[k, 2 * jp + 1], beta_ref[k, 2 * jp])


def middle_kernel(
    where_ref, coef_ref, beta_ref, adj_ref, spectrum_ref, table_ref, sea8_ref, ice_ref, field_ref,
    obs_ref, on_in, off_in, lon_east_ref, lon_west_ref,
    mu_ref, on_ref, off_ref, west_ref, east_ref,
    gx_ref, north_ref, south_ref, add_ref, add_n, add_s, add_e, add_w, one_ref,
):
    par = where_ref[0] % 2
    sub, lane = iotas()
    upper = sub >= LAT
    sea8 = sea8_ref[...]
    set_speeds(where_ref, table_ref, gx_ref)
    take_rows(par, on_in, off_in, north_ref, south_ref)

    wide = lax.broadcasted_iota(jnp.int32, (128, 128), 1).astype(F32)
    own = [jnp.zeros((128, 128), F32) for _ in range(LAT)]
    beside = [jnp.zeros((128, 128), F32) for _ in range(4)]
    for i in range(CAP):
        index = obs_ref[:, i : i + 1]
        value = obs_ref[:, CAP + i : CAP + i + 1]
        for r in range(LAT):
            own[r] = own[r] + jnp.where(index == wide + float(r * LON), value, 0.0)
        for place, target in enumerate(
            (wide, wide + float((LAT - 1) * LON), wide * LON, wide * LON + (LON - 1.0))
        ):
            index = obs_ref[:, 8 * place + 8 + i : 8 * place + 9 + i]
            value = obs_ref[:, 8 * place + 8 + CAP + i : 8 * place + 9 + CAP + i]
            beside[place] = beside[place] + jnp.where(index == target, value, 0.0)
    force = jnp.zeros((8, LON), F32)
    for r in range(LAT):
        force = jnp.where(sub % LAT == r, jnp.sum(own[r], axis=0, keepdims=True), force)
    lines = [jnp.sum(b, axis=0, keepdims=True) for b in beside]
    force_n, force_s = lines[0], lines[1]
    force_e, force_w = (
        jnp.sum(jnp.where(lane == sub % LAT, line, 0.0), axis=1, keepdims=True) for line in lines[2:]
    )
    set_weighted(table_ref, force * field_ref[...], add_ref)
    set_weighted(table_ref, force_n * north_ref[544:552, :], add_n)
    set_weighted(table_ref, force_s * south_ref[544:552, :], add_s)
    set_weighted(table_ref, force_e * lon_east_ref[24:32, :], add_e)
    set_weighted(table_ref, force_w * lon_west_ref[24:32, :], add_w)

    coupling, energy = move(
        adj_ref, mu_ref, spectrum_ref, table_ref, gx_ref, coef_ref, lon_east_ref, lon_west_ref,
        north_ref, south_ref, sub, lane, sea8, add_ref, (add_n, add_s), (add_e, add_w),
    )
    ice = ice_ref[...].astype(F32)
    rate = sea8 * (1.0 - jnp.concatenate([ice, ice], axis=0))
    base = sea8 - 0.2 * rate * energy
    set_weighted(table_ref, 0.2 * rate * coupling, add_ref)
    for lo, hi, north, first_east, second_east in SEGMENTS:

        def body(p, carry):
            for h, east in enumerate((first_east, second_east)):
                k = 2 * p + h
                columns = []
                for jp in range(PAIRS):
                    place = pl.ds(pl.multiple_of(p * 240 + 8 * (h * PAIRS + jp), 8), 8)
                    x = mu_ref[place, :] * (base + rate * rates(beta_ref, k, jp, upper))
                    x = x - add_ref[8 * jp : 8 * jp + 8, :]
                    mu_ref[place, :] = x
                    columns.append(x[:, :1] if east else x[:, LON - 1 :])
                pack_edge(west_ref if east else east_ref, k, east, columns, lane)
            return carry

        lax.fori_loop(lo, hi, body, 0)
    one_ref[...] = jnp.ones((8, LON), F32)
    send_rows(par, mu_ref, on_ref, off_ref, one_ref, one_ref)


def last_kernel(
    where_ref, coef_ref, beta_ref, mu_ref, spectrum_ref, table_ref, ice_ref,
    on_in, off_in, lon_east_ref, lon_west_ref,
    out_ref,
    gx_ref, north_ref, south_ref, add_ref,
):
    par = where_ref[0] % 2
    sub, lane = iotas()
    upper = sub >= LAT
    set_speeds(where_ref, table_ref, gx_ref)
    take_rows(par, on_in, off_in, north_ref, south_ref)
    coupling, energy = move(
        mu_ref, out_ref, spectrum_ref, table_ref, gx_ref, coef_ref, lon_east_ref, lon_west_ref,
        north_ref, south_ref, sub, lane,
    )
    ice = ice_ref[...].astype(F32)
    rate = 1.0 - jnp.concatenate([ice, ice], axis=0)
    base = 1.0 - 0.2 * rate * energy
    set_weighted(table_ref, 0.2 * rate * coupling, add_ref)

    def body(p, carry):
        for h in range(2):
            k = 2 * p + h
            for jp in range(PAIRS):
                place = pl.ds(pl.multiple_of(p * 240 + 8 * (h * PAIRS + jp), 8), 8)
                x = out_ref[place, :] * (base + rate * rates(beta_ref, k, jp, upper))
                out_ref[place, :] = x - add_ref[8 * jp : 8 * jp + 8, :]
        return carry

    lax.fori_loop(0, NDIR // 2, body, 0)


def params():
    return pltpu.CompilerParams(vmem_limit_bytes=40 * MIB)


def f32(*shape):
    return jax.ShapeDtypeStruct(shape, F32)


def level(step):
    return pl.BlockSpec((ROWS, LON), lambda i: (step, 0))


def whole(*shape):
    return pl.BlockSpec(shape, lambda i: tuple(0 for _ in shape))


def exchange(on, off, west, east):
    n_lon, n_lat = lax.axis_size("lon"), lax.axis_size("lat")
    near = [(i, i ^ 1) for i in range(n_lat)]
    far = [(i, ((i + 1) ^ 1) - 1) for i in range(1, n_lat - 1)]
    off = lax.ppermute(off, "lat", far)
    on = lax.ppermute(on, "lat", near)
    from_east = lax.ppermute(west, "lon", [(i, (i - 1) % n_lon) for i in range(n_lon)])
    from_west = lax.ppermute(east, "lon", [(i, (i + 1) % n_lon) for i in range(n_lon)])
    return on, off, from_east, from_west


def on_device(adj_final, saved, beta, sea_mask, ice_mask, obs_count, obs_cell, obs_value):
    per_direction, table = constant_tables()
    coef = jnp.asarray(per_direction)
    table = jnp.asarray(table)
    where = lax.axis_index("lat").astype(jnp.int32).reshape(1)
    adj = adj_final.reshape(ROWS, LON)
    saved = saved.reshape((STEPS + 1) * ROWS, LON)
    tiles = lambda rows: pltpu.VMEM((rows, LON), F32)
    tab_shape = table.shape

    on, off, west, east, obs, field, sea8 = pl.pallas_call(
        start_kernel,
        grid=(1,),
        out_shape=(f32(HALO, LON), f32(HALO, LON), f32(32, LON), f32(32, LON), f32(128, 128), f32(8, LON), f32(8, LON)),
        in_specs=[
            SMEM, whole(ROWS, LON), level(2), whole(*tab_shape), whole(LAT, LON),
            whole(1, 128), whole(*obs_cell.shape), whole(*obs_value.shape),
        ],
        out_specs=(
            whole(HALO, LON), whole(HALO, LON), whole(32, LON), whole(32, LON), whole(128, 128),
            whole(8, LON), whole(8, LON),
        ),
        compiler_params=params(),
        name="edges_and_observations",
    )(where, adj, saved, table, sea_mask, obs_count, obs_cell, obs_value)

    on, off, from_east, from_west = exchange(on, off, west, east)
    obs = lax.all_to_all(obs.reshape(128, 1, 128), ("lon", "lat"), split_axis=0, concat_axis=0, tiled=True)
    obs = obs.reshape(128, 128)

    mu, on, off, west, east = pl.pallas_call(
        middle_kernel,
        grid=(1,),
        out_shape=(f32(ROWS, LON), f32(HALO, LON), f32(HALO, LON), f32(32, LON), f32(32, LON)),
        in_specs=[
            SMEM, SMEM, SMEM, whole(ROWS, LON), level(1), whole(*tab_shape), whole(8, LON), whole(LAT, LON),
            whole(8, LON), whole(128, 128), whole(HALO, LON), whole(HALO, LON), whole(32, LON), whole(32, LON),
        ],
        out_specs=(
            whole(ROWS, LON), whole(HALO, LON), whole(HALO, LON), whole(32, LON), whole(32, LON),
        ),
        scratch_shapes=[tiles(120), tiles(HALO), tiles(HALO)] + [tiles(120)] * 5 + [tiles(8)],
        compiler_params=params(),
        name="first_step",
    )(where, coef, beta, adj, saved, table, sea8, ice_mask, field, obs, on, off, from_east, from_west)

    on, off, from_east, from_west = exchange(on, off, west, east)

    out = pl.pallas_call(
        last_kernel,
        grid=(1,),
        out_shape=f32(ROWS, LON),
        in_specs=[
            SMEM, SMEM, SMEM, whole(ROWS, LON), level(0), whole(*tab_shape), whole(LAT, LON),
            whole(HALO, LON), whole(HALO, LON), whole(32, LON), whole(32, LON),
        ],
        out_specs=whole(ROWS, LON),
        scratch_shapes=[tiles(120), tiles(HALO), tiles(HALO), tiles(120)],
        compiler_params=params(),
        name="last_step",
    )(where, coef, beta, mu, saved, table, ice_mask, on, off, from_east, from_west)
    return out.reshape(adj_final.shape)


def solution(mesh):
    return jax.shard_map(
        on_device,
        mesh=mesh,
        in_specs=(
            P(None, None, "lat", "lon"),
            P(None, None, None, "lat", "lon"),
            P(),
            P("lat", "lon"),
            P("lat", "lon"),
            P(("lon", "lat"), None),
            P(("lon", "lat"), None),
            P(("lon", "lat"), None),
        ),
        out_specs=P(None, None, "lat", "lon"),
        check_vma=False,
    )
```

```python
import math

import jax
import jax.numpy as jnp
import numpy as np
from jax import lax
from jax.experimental import pallas as pl
from jax.experimental.pallas import tpu as pltpu
from jax.sharding import PartitionSpec as P

STEPS = 2
CAP = 4
NDIR = 36
NFREQ = 30
QUAD = NDIR // 4
PAIRS = NFREQ // 2
LAT = 4
LON = 128
BLOCK = NFREQ * LAT
ROWS = NDIR * BLOCK
HALO = 552
SOUTH0 = 536
EDGE = 40
SPREAD = 2208
N_LAT = 16
N_LON = 8
MIB = 2**20
F32 = jnp.float32

HBM = pl.BlockSpec(memory_space=pltpu.HBM)
VMEM = pl.BlockSpec(memory_space=pltpu.VMEM)
SMEM = pl.BlockSpec(memory_space=pltpu.SMEM)

QUADRANTS = ((True, True), (True, False), (False, False), (False, True))

WEIGHT0 = 0
SPEED0 = BLOCK
COS0 = 2 * BLOCK
SIN0 = COS0 + 8 * QUAD
STRETCH0 = SIN0 + 8 * QUAD


def constant_table():
    angle = (np.arange(QUAD) + 0.5) * (2.0 * math.pi / NDIR)
    j = np.arange(NFREQ)
    speed = 1.1 ** (-j.astype(np.float64))
    growth = 1.1 ** j.astype(np.float64)
    weight = growth / (NDIR * growth.sum())
    rows = np.arange(N_LAT * LAT)
    latitude = (rows + 0.5 - N_LAT * LAT / 2.0) * (100.0 / (N_LAT * LAT))
    stretch = math.cos(50.0 * math.pi / 180.0) / np.cos(latitude * (math.pi / 180.0))
    stretch = np.tile(stretch.reshape(N_LAT, 1, LAT), (1, 2, 1)).reshape(-1)
    column = np.concatenate(
        [
            np.repeat(weight, LAT),
            np.repeat(speed, LAT),
            np.repeat(np.cos(angle), 8),
            np.repeat(np.sin(angle), 8),
            stretch,
        ]
    )
    return np.tile(column[:, None], (1, LON)).astype(np.float32)


def iotas():
    sub = lax.broadcasted_iota(jnp.int32, (8, LON), 0)
    lane = lax.broadcasted_iota(jnp.int32, (8, LON), 1)
    return sub, lane


def tab(jp):
    return slice(8 * jp, 8 * jp + 8)


def weights(table_ref, jp):
    return table_ref[WEIGHT0 + 8 * jp : WEIGHT0 + 8 * jp + 8, :]


def edge_block(quadrant, jp):
    first = 8 * (2 * (quadrant // 2) + jp // 8)
    return slice(first, first + 8)


def over_directions(body, carry):
    def two(v, carry):
        return body(2 * v + 1, 1, body(2 * v, 0, carry))

    carry = lax.fori_loop(0, QUAD // 2, two, carry)
    return body(QUAD - 1, (QUAD - 1) % 2, carry)


def spectrum_reader(ref, k, odd, level=0):
    first = level * ROWS + k * BLOCK - (8 if odd else 0)
    held = {}

    def read(jp):
        place, part = divmod(jp + odd, 2)
        if place not in held:
            held.clear()
            rows = pl.ds(pl.multiple_of(first + 16 * place, 16), 16)
            held[place] = ref[rows, :].astype(F32)
        return held[place][8 * part : 8 * part + 8, :]

    return read


def direction_rows(i, quadrant, jp=0, count=8):
    return pl.ds(pl.multiple_of((i + QUAD * quadrant) * BLOCK + 8 * jp, 8), count)


def extract_rows(src, r, first, dst, scale):
    def body(m, carry):
        for u in range(4):
            start = (first + 8 * (4 * m + u)) * LAT + r
            value = src[pl.ds(start, 8, stride=LAT), :]
            if scale is not None:
                value = value * scale
            dst[pl.ds(pl.multiple_of(8 * (4 * m + u), 8), 8), :] = value
        return carry

    lax.fori_loop(0, 17, body, 0)


def send_rows(par, src, on_ref, off_ref, field=None, scale8=None):
    def put(dst, r, first):
        extract_rows(src, r, first, dst, None if scale8 is None else scale8[r : r + 1, :])
        if field is not None:
            dst[pl.ds(544, 8), :] = jnp.broadcast_to(field[r : r + 1, :], (8, LON))

    @pl.when(par == 0)
    def _():
        put(on_ref, LAT - 1, SOUTH0)
        put(off_ref, 0, 0)

    @pl.when(par == 1)
    def _():
        put(on_ref, 0, 0)
        put(off_ref, LAT - 1, SOUTH0)


def spread_rows(par, on_ref, off_ref, north_ref, south_ref, field_ref=None):
    def spread(src, dst, r):
        def body(m, carry):
            for u in range(4):
                first = 8 * (4 * m + u)
                dst[pl.ds(first * LAT + r, 8, stride=LAT), :] = src[pl.ds(pl.multiple_of(first, 8), 8), :]
            return carry

        lax.fori_loop(0, 17, body, 0)

    for parity, (north, south) in enumerate(((on_ref, off_ref), (off_ref, on_ref))):

        @pl.when(par == parity)
        def _():
            spread(north, north_ref, LAT - 1)
            spread(south, south_ref, 0)
            if field_ref is not None:
                field_ref[0:8, :] = north[544:552, :]
                field_ref[8:16, :] = south[544:552, :]


def pack_edges(west_ref, east_ref, i, value_of, lane):
    relative = lane - 8 * i
    here = (relative >= 0) & (relative < 8)
    refs = [west_ref if east else east_ref for _, east in QUADRANTS]
    for lo, hi in ((0, 8), (8, PAIRS)):
        blocks = [None] * 4
        for jp in range(lo, hi):
            for q, (_, east) in enumerate(QUADRANTS):
                x = value_of(q, jp)
                shift = jp - lo + (0 if east else 1)
                x = pltpu.roll(x, shift, axis=1) if shift else x
                blocks[q] = x if jp == lo else jnp.where(lane == jp - lo, x, blocks[q])
        for q in range(4):
            place = edge_block(q, lo)
            moved = pltpu.roll(blocks[q], 8 * i, axis=1)
            refs[q][place, :] = jnp.where(here, moved, refs[q][place, :])


def pick_observations(count, cell, value, out_ref):
    sub = lax.broadcasted_iota(jnp.int32, (128, 128), 0)
    lane = lax.broadcasted_iota(jnp.int32, (128, 128), 1)
    counts = jnp.broadcast_to(count.astype(F32), (128, 128))
    starts = jnp.sum(jnp.where(lane < sub, counts, 0.0), axis=1, keepdims=True)
    mine = jnp.sum(jnp.where(lane == sub, counts, 0.0), axis=1, keepdims=True)
    local = (((cell >> 10) & (LAT - 1)) * LON + (cell & (LON - 1))).astype(F32)
    slots = cell.shape[1]
    slot = lax.broadcasted_iota(jnp.int32, (128, slots), 1).astype(F32)
    listed = jnp.zeros((128, 128), F32)
    for i in range(CAP):
        hit = slot == starts + float(i)
        index_i = jnp.sum(jnp.where(hit, local, 0.0), axis=1, keepdims=True)
        value_i = jnp.sum(jnp.where(hit, value, 0.0), axis=1, keepdims=True)
        value_i = jnp.where(mine > float(i), value_i, 0.0)
        listed = jnp.where(lane == i, index_i, listed)
        listed = jnp.where(lane == CAP + i, value_i, listed)
    out = listed
    for place, shift in enumerate((127, 1, 128 - N_LAT, N_LAT)):
        moved = pltpu.roll(listed, shift, axis=0)
        out = out + pltpu.roll(moved, 8 * (place + 1), axis=1)
    out_ref[...] = out


def fetch(sems, *pairs):
    copies = [pltpu.make_async_copy(src, dst, sems.at[n]) for n, (src, dst) in enumerate(pairs)]
    for copy in copies:
        copy.start()
    return copies


def start_kernel(
    where_ref, adj_hbm, saved_hbm, table_hbm, sea_hbm, count_hbm, cell_hbm, value_hbm,
    on_ref, off_ref, west_ref, east_ref, obs_ref, field_ref, sea8_ref, early_ref,
    adj_ref, final_ref, table_ref, sea_ref, count_ref, cell_ref, value_ref, sems,
):
    half = ROWS // 2
    final0 = STEPS * ROWS
    copies = fetch(
        sems,
        (count_hbm, count_ref),
        (cell_hbm, cell_ref),
        (value_hbm, value_ref),
        (sea_hbm, sea_ref),
        (table_hbm.at[pl.ds(0, BLOCK)], table_ref),
        (saved_hbm.at[pl.ds(final0, half)], final_ref.at[pl.ds(0, half)]),
        (saved_hbm.at[pl.ds(final0 + half, half)], final_ref.at[pl.ds(half, half)]),
        (adj_hbm.at[pl.ds(0, half)], adj_ref.at[pl.ds(0, half)]),
        (adj_hbm.at[pl.ds(half, half)], adj_ref.at[pl.ds(half, half)]),
        (saved_hbm.at[pl.ds(ROWS, ROWS)], early_ref.at[pl.ds(ROWS, ROWS)]),
        (saved_hbm.at[pl.ds(0, ROWS)], early_ref.at[pl.ds(0, ROWS)]),
    )
    par = where_ref[0] % 2
    sub, lane = iotas()
    for copy in copies[:3]:
        copy.wait()
    pick_observations(count_ref[...], cell_ref[...], value_ref[...], obs_ref)
    for copy in copies[3:7]:
        copy.wait()
    sea = sea_ref[...].astype(F32)
    sea8 = jnp.concatenate([sea, sea], axis=0)
    sea8_ref[...] = sea8

    def moment(i, odd, total):
        read = [spectrum_reader(final_ref, i + QUAD * q, (odd + q) % 2) for q in range(4)]
        for jp in range(PAIRS):
            both = (read[0](jp) + read[1](jp)) + (read[2](jp) + read[3](jp))
            total = total + weights(table_ref, jp) * both
        return total

    total = over_directions(moment, jnp.zeros((8, LON), F32))
    field = sea8 * 2.0 / jnp.sqrt(total + pltpu.roll(total, 4, axis=0))
    field_ref[...] = field
    for copy in copies[7:9]:
        copy.wait()
    send_rows(par, adj_ref, on_ref, off_ref, field_ref, sea8_ref)

    west_ref[...] = jnp.zeros_like(west_ref)
    east_ref[...] = jnp.zeros_like(east_ref)

    def pack(i, carry):
        pack_edges(west_ref, east_ref, i, lambda q, jp: adj_ref[direction_rows(i, q, jp), :], lane)
        return carry

    lax.fori_loop(0, QUAD, pack, 0)
    west_sea = jnp.broadcast_to(sea8[:, :1], (8, LON))
    east_sea = jnp.broadcast_to(sea8[:, LON - 1 :], (8, LON))
    for block in range(4):
        west_ref[tab(block), :] = west_ref[tab(block), :] * west_sea
        east_ref[tab(block), :] = east_ref[tab(block), :] * east_sea
    west_ref[32:40, :] = jnp.broadcast_to(field[:, :1], (8, LON))
    east_ref[32:40, :] = jnp.broadcast_to(field[:, LON - 1 :], (8, LON))
    for copy in copies[9:]:
        copy.wait()


def speeds_of(table_ref, stretch, i):
    cos_i = table_ref[pl.ds(pl.multiple_of(COS0 + 8 * i, 8), 8), :]
    sin_i = table_ref[pl.ds(pl.multiple_of(SIN0 + 8 * i, 8), 8), :]
    stretched = 0.7 * stretch
    return (cos_i * stretched, sin_i * stretched), (0.6 * sin_i, 0.6 * cos_i)


def turned_edges(lon_east_ref, lon_west_ref, i):
    turn = (LON - 8 * i) % LON
    out = {}
    for q, (_, east) in enumerate(QUADRANTS):
        for lo in (0, 8):
            ref = lon_east_ref if east else lon_west_ref
            out[q, lo] = pltpu.roll(ref[edge_block(q, lo), :], turn, axis=1)

    def edge(q, jp):
        shift = ((LON - 1 if QUADRANTS[q][1] else 0) - jp % 8) % LON
        block = out[q, 8 * (jp // 8)]
        return pltpu.roll(block, shift, axis=1) if shift else block

    return edge


def row_halo_of(north_ref, south_ref, i, q, jp):
    if QUADRANTS[q][0]:
        return north_ref[direction_rows(i, q, jp), :]
    row = (i + QUAD * q - NDIR // 2) * BLOCK + 8 * jp + 16
    return south_ref[pl.ds(pl.multiple_of(row, 8), 8), :]


def both_halves(total):
    return total + pltpu.roll(total, 4, axis=0)


def speed_of(table_ref, jp):
    return table_ref[SPEED0 + 8 * jp : SPEED0 + 8 * jp + 8, :]


def move(dst_ref, spectrum_ref, level, table_ref, stretch, sub, lane, value_of, lon_of, row_of):
    row = sub % LAT

    def body(i, odd, carry):
        coupling, energy = carry
        x_speed, y_speed = speeds_of(table_ref, stretch, i)
        read = [spectrum_reader(spectrum_ref, i + QUAD * q, (odd + q) % 2, level) for q in range(4)]
        lon_halo = lon_of(i)
        for jp in range(PAIRS):
            all_of = None
            for q, (north, east) in enumerate(QUADRANTS):
                spectrum = read[q](jp)
                mu = value_of(i, q, jp)
                turned = pltpu.roll(mu, LON - 1 if east else 1, axis=1)
                along = jnp.where(lane == (LON - 1 if east else 0), lon_halo(q, jp), turned)
                shifted = pltpu.roll(mu, 7 if north else 1, axis=0)
                across = jnp.where(row == (LAT - 1 if north else 0), row_of(i, q, jp), shifted)
                change = x_speed[q % 2] * (along - mu) + y_speed[q % 2] * (across - mu)
                nu = mu + speed_of(table_ref, jp) * change
                dst_ref[direction_rows(i, q, jp), :] = nu
                coupling = coupling + spectrum * nu
                all_of = spectrum if all_of is None else all_of + spectrum
            energy = energy + weights(table_ref, jp) * all_of
        return coupling, energy

    coupling, energy = over_directions(body, (jnp.zeros((8, LON), F32), jnp.zeros((8, LON), F32)))
    return both_halves(coupling), both_halves(energy)


def stretch_of(where_ref, table_ref):
    return table_ref[pl.ds(pl.multiple_of(STRETCH0 + 8 * where_ref[0], 8), 8), :]


def set_weighted(table_ref, field, dst_ref):
    for jp in range(PAIRS):
        dst_ref[tab(jp), :] = weights(table_ref, jp) * field


def rate_of(beta_ref, k, jp, upper):
    return jnp.where(upper, beta_ref[2 * jp + 1, k], beta_ref[2 * jp, k])


def sum_observations(obs_ref, sub, lane):
    wide = lax.broadcasted_iota(jnp.int32, (128, 128), 1).astype(F32)
    own = [jnp.zeros((128, 128), F32) for _ in range(LAT)]
    beside = [jnp.zeros((128, 128), F32) for _ in range(4)]
    for i in range(CAP):
        index = obs_ref[:, i : i + 1]
        value = obs_ref[:, CAP + i : CAP + i + 1]
        for r in range(LAT):
            own[r] = own[r] + jnp.where(index == wide + float(r * LON), value, 0.0)
        for place, target in enumerate(
            (wide, wide + float((LAT - 1) * LON), wide * LON, wide * LON + (LON - 1.0))
        ):
            index = obs_ref[:, 8 * place + 8 + i : 8 * place + 9 + i]
            value = obs_ref[:, 8 * place + 8 + CAP + i : 8 * place + 9 + CAP + i]
            beside[place] = beside[place] + jnp.where(index == target, value, 0.0)
    force = jnp.zeros((8, LON), F32)
    for r in range(LAT):
        force = jnp.where(sub % LAT == r, jnp.sum(own[r], axis=0, keepdims=True), force)
    lines = [jnp.sum(b, axis=0, keepdims=True) for b in beside]
    force_n, force_s = lines[0], lines[1]
    force_e, force_w = (
        jnp.sum(jnp.where(lane == sub % LAT, line, 0.0), axis=1, keepdims=True) for line in lines[2:]
    )
    return force, force_n, force_s, force_e, force_w


def middle_kernel(
    where_ref, beta_hbm, adj_ref, spectrum_ref, table_ref, sea8_ref, ice_ref, field_ref,
    obs_ref, on_in, off_in, lon_east_ref, lon_west_ref,
    mu_ref, on_ref, off_ref, west_ref, east_ref,
    beta_ref, north_ref, south_ref, fields_ref, add_ref, add_n, add_s, add_e, add_w, sems,
):
    copies = fetch(sems, (beta_hbm, beta_ref))
    par = where_ref[0] % 2
    sub, lane = iotas()
    sea8 = sea8_ref[...]
    stretch = stretch_of(where_ref, table_ref)
    force, force_n, force_s, force_e, force_w = sum_observations(obs_ref, sub, lane)
    spread_rows(par, on_in, off_in, north_ref, south_ref, fields_ref)
    set_weighted(table_ref, force * field_ref[...], add_ref)
    set_weighted(table_ref, force_n * fields_ref[0:8, :], add_n)
    set_weighted(table_ref, force_s * fields_ref[8:16, :], add_s)
    set_weighted(table_ref, force_e * lon_east_ref[32:40, :], add_e)
    set_weighted(table_ref, force_w * lon_west_ref[32:40, :], add_w)

    def lon_of(i):
        edge = turned_edges(lon_east_ref, lon_west_ref, i)
        return lambda q, jp: edge(q, jp) + (add_e if QUADRANTS[q][1] else add_w)[tab(jp), :]

    coupling, energy = move(
        mu_ref, spectrum_ref, 1, table_ref, stretch, sub, lane,
        lambda i, q, jp: adj_ref[direction_rows(i, q, jp), :] * sea8 + add_ref[tab(jp), :],
        lon_of,
        lambda i, q, jp: row_halo_of(north_ref, south_ref, i, q, jp)
        + (add_n if QUADRANTS[q][0] else add_s)[tab(jp), :],
    )
    upper = sub >= LAT
    ice = ice_ref[...].astype(F32)
    rate = sea8 * (1.0 - jnp.concatenate([ice, ice], axis=0))
    base = sea8 - 0.2 * rate * energy
    set_weighted(table_ref, 0.2 * rate * coupling, add_ref)
    west_ref[...] = jnp.zeros_like(west_ref)
    east_ref[...] = jnp.zeros_like(east_ref)
    copies[0].wait()

    def source(i, carry):
        def value_of(q, jp):
            beta = rate_of(beta_ref, i + QUAD * q, jp, upper)
            place = direction_rows(i, q, jp)
            x = mu_ref[place, :] * (base + rate * beta) - add_ref[tab(jp), :]
            mu_ref[place, :] = x
            return x

        pack_edges(west_ref, east_ref, i, value_of, lane)
        return carry

    lax.fori_loop(0, QUAD, source, 0)
    send_rows(par, mu_ref, on_ref, off_ref)


def inner_kernel(where_ref, mu_ref, spectrum_ref, table_ref, nu_ref, coupling_ref, energy_ref):
    sub, lane = iotas()
    coupling, energy = move(
        nu_ref, spectrum_ref, 0, table_ref, stretch_of(where_ref, table_ref), sub, lane,
        lambda i, q, jp: mu_ref[direction_rows(i, q, jp), :],
        lambda i: lambda q, jp: 0.0,
        lambda i, q, jp: 0.0,
    )
    coupling_ref[...] = coupling
    energy_ref[...] = energy


def last_kernel(
    where_ref, beta_hbm, nu_ref, spectrum_ref, table_ref, ice_ref, coupling_ref, energy_ref,
    on_in, off_in, lon_east_ref, lon_west_ref,
    out_hbm,
    beta_ref, north_ref, south_ref, add_ref, gain_ref, sems, out_sems,
):
    copies = fetch(sems, (beta_hbm, beta_ref))
    par = where_ref[0] % 2
    sub, lane = iotas()
    row = sub % LAT
    spread_rows(par, on_in, off_in, north_ref, south_ref)
    stretch = stretch_of(where_ref, table_ref)

    def gains(i, odd, coupling):
        x_speed, y_speed = speeds_of(table_ref, stretch, i)
        read = [spectrum_reader(spectrum_ref, i + QUAD * q, (odd + q) % 2) for q in range(4)]
        edge = turned_edges(lon_east_ref, lon_west_ref, i)
        for jp in range(PAIRS):
            for q, (north, east) in enumerate(QUADRANTS):
                along = jnp.where(lane == (LON - 1 if east else 0), edge(q, jp), 0.0)
                halo = row_halo_of(north_ref, south_ref, i, q, jp)
                across = jnp.where(row == (LAT - 1 if north else 0), halo, 0.0)
                gain = speed_of(table_ref, jp) * (x_speed[q % 2] * along + y_speed[q % 2] * across)
                gain_ref[direction_rows(i, q, jp), :] = gain
                coupling = coupling + read[q](jp) * gain
        return coupling

    gained = over_directions(gains, jnp.zeros((8, LON), F32))
    coupling = coupling_ref[...] + both_halves(gained)
    upper = sub >= LAT
    ice = ice_ref[...].astype(F32)
    rate = 1.0 - jnp.concatenate([ice, ice], axis=0)
    base = 1.0 - 0.2 * rate * energy_ref[...]
    set_weighted(table_ref, 0.2 * rate * coupling, add_ref)
    copies[0].wait()

    def chunk(g):
        rows = pl.ds(pl.multiple_of(g * 4 * BLOCK, 8), 4 * BLOCK)
        return pltpu.make_async_copy(gain_ref.at[rows], out_hbm.at[rows], out_sems.at[g])

    def body(g, carry):
        for jp in range(PAIRS):
            for h in range(4):
                beta = rate_of(beta_ref, 4 * g + h, jp, upper)
                place = pl.ds(pl.multiple_of((4 * g + h) * BLOCK + 8 * jp, 8), 8)
                x = (nu_ref[place, :] + gain_ref[place, :]) * (base + rate * beta)
                gain_ref[place, :] = x - add_ref[tab(jp), :]
        chunk(g).start()
        return carry

    lax.fori_loop(0, NDIR // 4, body, 0)
    for g in range(NDIR // 4):
        chunk(g).wait()


FIRST = 54


def params(limit=24):
    return pltpu.CompilerParams(vmem_limit_bytes=limit * MIB)


def f32(*shape):
    return jax.ShapeDtypeStruct(shape, F32)


def exchange(on, off, west, east):
    n_lon, n_lat = lax.axis_size("lon"), lax.axis_size("lat")
    near = [(i, i ^ 1) for i in range(n_lat)]
    far = [(i, ((i + 1) ^ 1) - 1) for i in range(1, n_lat - 1)]
    off = lax.ppermute(off, "lat", far)
    on = lax.ppermute(on, "lat", near)
    from_east = lax.ppermute(west, "lon", [(i, (i - 1) % n_lon) for i in range(n_lon)])
    from_west = lax.ppermute(east, "lon", [(i, (i + 1) % n_lon) for i in range(n_lon)])
    return on, off, from_east, from_west


def on_device(adj_final, saved, beta, sea_mask, ice_mask, obs_count, obs_cell, obs_value):
    table = jnp.asarray(constant_table())
    where = lax.axis_index("lat").astype(jnp.int32).reshape(1)
    adj = adj_final.reshape(ROWS, LON)
    saved = saved.reshape((STEPS + 1) * ROWS, LON)
    beta = beta.T
    tiles = lambda rows: pltpu.VMEM((rows, LON), F32)
    whole = lambda x: pltpu.VMEM(x.shape, x.dtype)
    level = pltpu.VMEM((ROWS, LON), jnp.bfloat16)
    payload = (f32(HALO, LON), f32(HALO, LON), f32(EDGE, LON), f32(EDGE, LON))
    dma = lambda *n: pltpu.SemaphoreType.DMA(n)

    on, off, west, east, obs, field, sea8, early = pl.pallas_call(
        start_kernel,
        out_shape=payload
        + (f32(128, 128), tiles(8), tiles(8))
        + (pltpu.VMEM((2 * ROWS, LON), jnp.bfloat16),),
        in_specs=[SMEM] + [HBM] * 7,
        out_specs=(VMEM,) * 8,
        scratch_shapes=[
            tiles(ROWS), level, tiles(BLOCK), whole(sea_mask), whole(obs_count), whole(obs_cell), whole(obs_value), dma(11),
        ],
        compiler_params=params(FIRST),
        name="edges_and_observations",
    )(where, adj, saved, table, sea_mask, obs_count, obs_cell, obs_value)

    on, off, from_east, from_west = exchange(on, off, west, east)
    obs = lax.all_to_all(obs.reshape(128, 1, 128), ("lon", "lat"), split_axis=0, concat_axis=0, tiled=True)
    obs = obs.reshape(128, 128)

    rates = pltpu.SMEM(beta.shape, F32)
    mu, on, off, west, east = pl.pallas_call(
        middle_kernel,
        out_shape=(f32(ROWS, LON),) + payload,
        in_specs=[SMEM, HBM] + [VMEM] * 11,
        out_specs=(VMEM,) * 5,
        scratch_shapes=[rates, tiles(SPREAD), tiles(SPREAD), tiles(16)] + [tiles(BLOCK)] * 5 + [dma(1)],
        compiler_params=params(),
        name="first_step",
    )(where, beta, adj, early, table, sea8, ice_mask, field, obs, on, off, from_east, from_west)

    on, off, from_east, from_west = exchange(on, off, west, east)

    nu, coupling, energy = pl.pallas_call(
        inner_kernel,
        out_shape=(f32(ROWS, LON), f32(8, LON), f32(8, LON)),
        in_specs=[SMEM] + [VMEM] * 3,
        out_specs=(VMEM,) * 3,
        compiler_params=params(),
        cost_estimate=pl.CostEstimate(flops=20_000_000, bytes_accessed=6_000_000, transcendentals=0),
        name="last_step_inside",
    )(where, mu, early, table)

    out = pl.pallas_call(
        last_kernel,
        out_shape=f32(ROWS, LON),
        in_specs=[SMEM, HBM] + [VMEM] * 10,
        out_specs=HBM,
        scratch_shapes=[rates, tiles(SPREAD), tiles(SPREAD), tiles(BLOCK), tiles(ROWS), dma(1), dma(NDIR // 4)],
        compiler_params=params(),
        name="last_step_edges",
    )(where, beta, nu, early, table, ice_mask, coupling, energy, on, off, from_east, from_west)
    return out.reshape(adj_final.shape)


def solution(mesh):
    return jax.shard_map(
        on_device,
        mesh=mesh,
        in_specs=(
            P(None, None, "lat", "lon"),
            P(None, None, None, "lat", "lon"),
            P(),
            P("lat", "lon"),
            P("lat", "lon"),
            P(("lon", "lat"), None),
            P(("lon", "lat"), None),
            P(("lon", "lat"), None),
        ),
        out_specs=P(None, None, "lat", "lon"),
        check_vma=False,
    )
```

```python
import functools
import math

import jax
import jax.numpy as jnp
import numpy as np
from jax import lax
from jax.experimental import pallas as pl
from jax.experimental.pallas import tpu as pltpu
from jax.sharding import PartitionSpec as P

STEPS = 2
CAP = 4
NDIR = 36
NFREQ = 30
QUAD = NDIR // 4
PAIRS = NFREQ // 2
LAT = 4
LON = 128
BLOCK = NFREQ * LAT
ROWS = NDIR * BLOCK
HALO = 552
SOUTH0 = 536
EDGE = 40
SPREAD = 2208
N_LAT = 16
N_LON = 8
MIB = 2**20
F32 = jnp.float32

HBM = pl.BlockSpec(memory_space=pltpu.HBM)
VMEM = pl.BlockSpec(memory_space=pltpu.VMEM)
SMEM = pl.BlockSpec(memory_space=pltpu.SMEM)

QUADRANTS = ((True, True), (True, False), (False, False), (False, True))

WEIGHT0 = 0
SPEED0 = BLOCK
COS0 = 2 * BLOCK
SIN0 = COS0 + 8 * QUAD
STRETCH0 = SIN0 + 8 * QUAD


def constant_table():
    angle = (np.arange(QUAD) + 0.5) * (2.0 * math.pi / NDIR)
    j = np.arange(NFREQ)
    speed = 1.1 ** (-j.astype(np.float64))
    growth = 1.1 ** j.astype(np.float64)
    weight = growth / (NDIR * growth.sum())
    rows = np.arange(N_LAT * LAT)
    latitude = (rows + 0.5 - N_LAT * LAT / 2.0) * (100.0 / (N_LAT * LAT))
    stretch = math.cos(50.0 * math.pi / 180.0) / np.cos(latitude * (math.pi / 180.0))
    stretch = np.tile(stretch.reshape(N_LAT, 1, LAT), (1, 2, 1)).reshape(-1)
    column = np.concatenate(
        [
            np.repeat(weight, LAT),
            np.repeat(speed, LAT),
            np.repeat(np.cos(angle), 8),
            np.repeat(np.sin(angle), 8),
            stretch,
        ]
    )
    return np.tile(column[:, None], (1, LON)).astype(np.float32)


def iotas():
    sub = lax.broadcasted_iota(jnp.int32, (8, LON), 0)
    lane = lax.broadcasted_iota(jnp.int32, (8, LON), 1)
    return sub, lane


def tab(jp):
    return slice(8 * jp, 8 * jp + 8)


def weights(table_ref, jp):
    return table_ref[WEIGHT0 + 8 * jp : WEIGHT0 + 8 * jp + 8, :]


def edge_block(quadrant, jp):
    first = 8 * (2 * (quadrant // 2) + jp // 8)
    return slice(first, first + 8)


def over_directions(body, carry):
    def two(v, carry):
        return body(2 * v + 1, 1, body(2 * v, 0, carry))

    carry = lax.fori_loop(0, QUAD // 2, two, carry)
    return body(QUAD - 1, (QUAD - 1) % 2, carry)


def spectrum_reader(ref, k, odd, level=0):
    first = level * ROWS + k * BLOCK - (8 if odd else 0)
    held = {}

    def read(jp):
        place, part = divmod(jp + odd, 2)
        if place not in held:
            held.clear()
            rows = pl.ds(pl.multiple_of(first + 16 * place, 16), 16)
            held[place] = ref[rows, :].astype(F32)
        return held[place][8 * part : 8 * part + 8, :]

    return read


def direction_rows(i, quadrant, jp=0, count=8):
    return pl.ds(pl.multiple_of((i + QUAD * quadrant) * BLOCK + 8 * jp, 8), count)


def extract_rows(src, r, first, dst, scale):
    def body(m, carry):
        for u in range(4):
            start = (first + 8 * (4 * m + u)) * LAT + r
            value = src[pl.ds(start, 8, stride=LAT), :]
            if scale is not None:
                value = value * scale
            dst[pl.ds(pl.multiple_of(8 * (4 * m + u), 8), 8), :] = value
        return carry

    lax.fori_loop(0, 17, body, 0)


def send_rows(par, src, on_ref, off_ref, field=None, scale8=None):
    def put(dst, r, first):
        extract_rows(src, r, first, dst, None if scale8 is None else scale8[r : r + 1, :])
        if field is not None:
            dst[pl.ds(544, 8), :] = jnp.broadcast_to(field[r : r + 1, :], (8, LON))

    @pl.when(par == 0)
    def _():
        put(on_ref, LAT - 1, SOUTH0)
        put(off_ref, 0, 0)

    @pl.when(par == 1)
    def _():
        put(on_ref, 0, 0)
        put(off_ref, LAT - 1, SOUTH0)


def spread_rows(par, on_ref, off_ref, north_ref, south_ref, field_ref=None):
    def spread(src, dst, r):
        def body(m, carry):
            for u in range(4):
                first = 8 * (4 * m + u)
                dst[pl.ds(first * LAT + r, 8, stride=LAT), :] = src[pl.ds(pl.multiple_of(first, 8), 8), :]
            return carry

        lax.fori_loop(0, 17, body, 0)

    for parity, (north, south) in enumerate(((on_ref, off_ref), (off_ref, on_ref))):

        @pl.when(par == parity)
        def _():
            spread(north, north_ref, LAT - 1)
            spread(south, south_ref, 0)
            if field_ref is not None:
                field_ref[0:8, :] = north[544:552, :]
                field_ref[8:16, :] = south[544:552, :]


def pack_edges(west_ref, east_ref, i, value_of, lane):
    relative = lane - 8 * i
    here = (relative >= 0) & (relative < 8)
    refs = [west_ref if east else east_ref for _, east in QUADRANTS]
    for lo, hi in ((0, 8), (8, PAIRS)):
        blocks = [None] * 4
        for jp in range(lo, hi):
            for q, (_, east) in enumerate(QUADRANTS):
                x = value_of(q, jp)
                shift = jp - lo + (0 if east else 1)
                x = pltpu.roll(x, shift, axis=1) if shift else x
                blocks[q] = x if jp == lo else jnp.where(lane == jp - lo, x, blocks[q])
        for q in range(4):
            place = edge_block(q, lo)
            moved = pltpu.roll(blocks[q], 8 * i, axis=1)
            refs[q][place, :] = jnp.where(here, moved, refs[q][place, :])


def pick_observations(count, cell, value, out_ref):
    sub = lax.broadcasted_iota(jnp.int32, (128, 128), 0)
    lane = lax.broadcasted_iota(jnp.int32, (128, 128), 1)
    counts = jnp.broadcast_to(count.astype(F32), (128, 128))
    starts = jnp.sum(jnp.where(lane < sub, counts, 0.0), axis=1, keepdims=True)
    mine = jnp.sum(jnp.where(lane == sub, counts, 0.0), axis=1, keepdims=True)
    local = (((cell >> 10) & (LAT - 1)) * LON + (cell & (LON - 1))).astype(F32)
    slots = cell.shape[1]
    slot = lax.broadcasted_iota(jnp.int32, (128, slots), 1).astype(F32)
    listed = jnp.zeros((128, 128), F32)
    for i in range(CAP):
        hit = slot == starts + float(i)
        index_i = jnp.sum(jnp.where(hit, local, 0.0), axis=1, keepdims=True)
        value_i = jnp.sum(jnp.where(hit, value, 0.0), axis=1, keepdims=True)
        value_i = jnp.where(mine > float(i), value_i, 0.0)
        listed = jnp.where(lane == i, index_i, listed)
        listed = jnp.where(lane == CAP + i, value_i, listed)
    out = listed
    for place, shift in enumerate((127, 1, 128 - N_LAT, N_LAT)):
        moved = pltpu.roll(listed, shift, axis=0)
        out = out + pltpu.roll(moved, 8 * (place + 1), axis=1)
    out_ref[...] = out


def fetch(sems, *pairs):
    copies = [pltpu.make_async_copy(src, dst, sems.at[n]) for n, (src, dst) in enumerate(pairs)]
    for copy in copies:
        copy.start()
    return copies


def start_kernel(
    where_ref, adj_hbm, saved_hbm, table_hbm, sea_hbm, count_hbm, cell_hbm, value_hbm,
    on_ref, off_ref, west_ref, east_ref, obs_ref, field_ref, sea8_ref, early_ref,
    adj_ref, final_ref, table_ref, sea_ref, count_ref, cell_ref, value_ref, sems,
):
    half = ROWS // 2
    final0 = STEPS * ROWS
    copies = fetch(
        sems,
        (count_hbm, count_ref),
        (cell_hbm, cell_ref),
        (value_hbm, value_ref),
        (sea_hbm, sea_ref),
        (table_hbm.at[pl.ds(0, BLOCK)], table_ref),
        (saved_hbm.at[pl.ds(final0, half)], final_ref.at[pl.ds(0, half)]),
        (saved_hbm.at[pl.ds(final0 + half, half)], final_ref.at[pl.ds(half, half)]),
        (adj_hbm.at[pl.ds(0, half)], adj_ref.at[pl.ds(0, half)]),
        (adj_hbm.at[pl.ds(half, half)], adj_ref.at[pl.ds(half, half)]),
        (saved_hbm.at[pl.ds(ROWS, ROWS)], early_ref.at[pl.ds(ROWS, ROWS)]),
        (saved_hbm.at[pl.ds(0, ROWS)], early_ref.at[pl.ds(0, ROWS)]),
    )
    par = where_ref[0] % 2
    sub, lane = iotas()
    for copy in copies[:3]:
        copy.wait()
    pick_observations(count_ref[...], cell_ref[...], value_ref[...], obs_ref)
    for copy in copies[3:7]:
        copy.wait()
    sea = sea_ref[...].astype(F32)
    sea8 = jnp.concatenate([sea, sea], axis=0)
    sea8_ref[...] = sea8

    def moment(i, odd, total):
        read = [spectrum_reader(final_ref, i + QUAD * q, (odd + q) % 2) for q in range(4)]
        for jp in range(PAIRS):
            both = (read[0](jp) + read[1](jp)) + (read[2](jp) + read[3](jp))
            total = total + weights(table_ref, jp) * both
        return total

    total = over_directions(moment, jnp.zeros((8, LON), F32))
    field = sea8 * 2.0 / jnp.sqrt(total + pltpu.roll(total, 4, axis=0))
    field_ref[...] = field
    for copy in copies[7:9]:
        copy.wait()
    send_rows(par, adj_ref, on_ref, off_ref, field_ref, sea8_ref)

    west_ref[...] = jnp.zeros_like(west_ref)
    east_ref[...] = jnp.zeros_like(east_ref)

    def pack(i, carry):
        pack_edges(west_ref, east_ref, i, lambda q, jp: adj_ref[direction_rows(i, q, jp), :], lane)
        return carry

    lax.fori_loop(0, QUAD, pack, 0)
    west_sea = jnp.broadcast_to(sea8[:, :1], (8, LON))
    east_sea = jnp.broadcast_to(sea8[:, LON - 1 :], (8, LON))
    for block in range(4):
        west_ref[tab(block), :] = west_ref[tab(block), :] * west_sea
        east_ref[tab(block), :] = east_ref[tab(block), :] * east_sea
    west_ref[32:40, :] = jnp.broadcast_to(field[:, :1], (8, LON))
    east_ref[32:40, :] = jnp.broadcast_to(field[:, LON - 1 :], (8, LON))
    for copy in copies[9:]:
        copy.wait()


def speeds_of(table_ref, stretch, i):
    cos_i = table_ref[pl.ds(pl.multiple_of(COS0 + 8 * i, 8), 8), :]
    sin_i = table_ref[pl.ds(pl.multiple_of(SIN0 + 8 * i, 8), 8), :]
    stretched = 0.7 * stretch
    return (cos_i * stretched, sin_i * stretched), (0.6 * sin_i, 0.6 * cos_i)


def turned_edges(lon_east_ref, lon_west_ref, i):
    turn = (LON - 8 * i) % LON
    out = {}
    for q, (_, east) in enumerate(QUADRANTS):
        for lo in (0, 8):
            ref = lon_east_ref if east else lon_west_ref
            out[q, lo] = pltpu.roll(ref[edge_block(q, lo), :], turn, axis=1)

    def edge(q, jp):
        shift = ((LON - 1 if QUADRANTS[q][1] else 0) - jp % 8) % LON
        block = out[q, 8 * (jp // 8)]
        return pltpu.roll(block, shift, axis=1) if shift else block

    return edge


def row_halo_of(north_ref, south_ref, i, q, jp):
    if QUADRANTS[q][0]:
        return north_ref[direction_rows(i, q, jp), :]
    row = (i + QUAD * q - NDIR // 2) * BLOCK + 8 * jp + 16
    return south_ref[pl.ds(pl.multiple_of(row, 8), 8), :]


def both_halves(total):
    return total + pltpu.roll(total, 4, axis=0)


def speed_of(table_ref, jp):
    return table_ref[SPEED0 + 8 * jp : SPEED0 + 8 * jp + 8, :]


def move(dst_ref, spectrum_ref, level, table_ref, stretch, sub, lane, value_of, lon_of, row_of):
    row = sub % LAT

    def body(i, odd, carry):
        coupling, energy = carry
        x_speed, y_speed = speeds_of(table_ref, stretch, i)
        read = [spectrum_reader(spectrum_ref, i + QUAD * q, (odd + q) % 2, level) for q in range(4)]
        lon_halo = lon_of(i)
        for jp in range(PAIRS):
            all_of = None
            for q, (north, east) in enumerate(QUADRANTS):
                spectrum = read[q](jp)
                mu = value_of(i, q, jp)
                turned = pltpu.roll(mu, LON - 1 if east else 1, axis=1)
                along = jnp.where(lane == (LON - 1 if east else 0), lon_halo(q, jp), turned)
                shifted = pltpu.roll(mu, 7 if north else 1, axis=0)
                across = jnp.where(row == (LAT - 1 if north else 0), row_of(i, q, jp), shifted)
                change = x_speed[q % 2] * (along - mu) + y_speed[q % 2] * (across - mu)
                nu = mu + speed_of(table_ref, jp) * change
                dst_ref[direction_rows(i, q, jp), :] = nu
                coupling = coupling + spectrum * nu
                all_of = spectrum if all_of is None else all_of + spectrum
            energy = energy + weights(table_ref, jp) * all_of
        return coupling, energy

    coupling, energy = over_directions(body, (jnp.zeros((8, LON), F32), jnp.zeros((8, LON), F32)))
    return both_halves(coupling), both_halves(energy)


def stretch_of(where_ref, table_ref):
    return table_ref[pl.ds(pl.multiple_of(STRETCH0 + 8 * where_ref[0], 8), 8), :]


def set_weighted(table_ref, field, dst_ref):
    for jp in range(PAIRS):
        dst_ref[tab(jp), :] = weights(table_ref, jp) * field


def rate_of(beta_ref, k, jp, upper):
    return jnp.where(upper, beta_ref[2 * jp + 1, k], beta_ref[2 * jp, k])


def edge_gains(
    spectrum_ref, level, table_ref, stretch, lon_east_ref, lon_west_ref, north_ref, south_ref,
    sub, lane, extra_of, keep,
):
    row = sub % LAT

    def body(i, odd, coupling):
        x_speed, y_speed = speeds_of(table_ref, stretch, i)
        read = [spectrum_reader(spectrum_ref, i + QUAD * q, (odd + q) % 2, level) for q in range(4)]
        edge = turned_edges(lon_east_ref, lon_west_ref, i)
        extra = [extra_of(q, x_speed[q % 2], y_speed[q % 2]) for q in range(4)]
        for jp in range(PAIRS):
            for q, (north, east) in enumerate(QUADRANTS):
                along = jnp.where(lane == (LON - 1 if east else 0), edge(q, jp), 0.0)
                halo = row_halo_of(north_ref, south_ref, i, q, jp)
                across = jnp.where(row == (LAT - 1 if north else 0), halo, 0.0)
                gain = speed_of(table_ref, jp) * (x_speed[q % 2] * along + y_speed[q % 2] * across)
                gain = keep(direction_rows(i, q, jp), jp, gain, extra[q])
                coupling = coupling + read[q](jp) * gain
        return coupling

    return both_halves(over_directions(body, jnp.zeros((8, LON), F32)))


def three_parts(x):
    parts = []
    for _ in range(3):
        part = x.astype(jnp.bfloat16)
        parts.append(part)
        x = x - part.astype(F32)
    return jnp.concatenate(parts, axis=0)


def sum_observations(obs_ref, sub, lane):
    listed = jnp.transpose(obs_ref[...])
    column = lax.broadcasted_iota(jnp.int32, (128, 128), 0).astype(F32)
    row8 = (sub % LAT).astype(F32)

    def slots(tile):
        for i in range(CAP):
            index = listed[8 * tile + i : 8 * tile + i + 1, :]
            value = listed[8 * tile + CAP + i : 8 * tile + CAP + i + 1, :]
            row = jnp.floor(index * (1.0 / LON))
            yield row, index - row * LON, value

    def spread(tile, takes):
        left, right = [], []
        for row, col, value in slots(tile):
            left.append(jnp.where(takes(row), value, jnp.zeros((8, LON), F32)))
            right.append(jnp.where(column == col, 1.0, 0.0).astype(jnp.bfloat16))
        parts = three_parts(jnp.concatenate(left, axis=1))
        out = lax.dot_general(
            parts, jnp.concatenate(right, axis=1), (((1,), (1,)), ((), ())), preferred_element_type=F32
        )
        return out[0:8, :] + out[8:16, :] + out[16:24, :]

    def line(tile, at):
        total = jnp.zeros((8, LON), F32)
        for row, col, value in slots(tile):
            total = total + jnp.where((row8 == row) & (col == at), value, 0.0)
        return jnp.sum(total, axis=1, keepdims=True)

    own = spread(0, lambda row: row8 == row)
    north = spread(1, lambda row: row8 * 0.0 == row)
    south = spread(2, lambda row: row8 * 0.0 + (LAT - 1.0) == row)
    return own, north, south, line(3, 0.0), line(4, LON - 1.0)


def middle_kernel(
    where_ref, beta_hbm, nu_ref, spectrum_ref, table_ref, sea8_ref, ice_ref, field_ref,
    coupling_ref, energy_ref, obs_ref, on_in, off_in, lon_east_ref, lon_west_ref,
    mu_ref, on_ref, off_ref, west_ref, east_ref,
    beta_ref, north_ref, south_ref, fields_ref, add_ref, sems,
):
    copies = fetch(sems, (beta_hbm, beta_ref))
    par = where_ref[0] % 2
    sub, lane = iotas()
    row = sub % LAT
    sea8 = sea8_ref[...]
    stretch = stretch_of(where_ref, table_ref)
    force, force_n, force_s, force_e, force_w = sum_observations(obs_ref, sub, lane)
    spread_rows(par, on_in, off_in, north_ref, south_ref, fields_ref)

    own = force * field_ref[...]
    set_weighted(table_ref, own, add_ref)
    first_weight = table_ref[WEIGHT0 : WEIGHT0 + 1, :]
    along_of, across_of = {}, {}
    for east, halo, ref in ((True, force_e, lon_east_ref), (False, force_w, lon_west_ref)):
        beside = halo * ref[32:40, :]
        turned = pltpu.roll(own, LON - 1 if east else 1, axis=1)
        here = jnp.where(lane == (LON - 1 if east else 0), beside, turned)
        along_of[east] = first_weight * (here - own)
    for north, halo, place in ((True, force_n, 0), (False, force_s, 8)):
        beside = halo * fields_ref[place : place + 8, :]
        shifted = pltpu.roll(own, 7 if north else 1, axis=0)
        here = jnp.where(row == (LAT - 1 if north else 0), beside, shifted)
        across_of[north] = first_weight * (here - own)

    def extra_of(q, x_speed, y_speed):
        north, east = QUADRANTS[q]
        return x_speed * along_of[east] + y_speed * across_of[north]

    def keep(place, jp, gain, extra):
        gain = gain + (add_ref[tab(jp), :] + extra)
        mu_ref[place, :] = nu_ref[place, :] + gain
        return gain

    gained = edge_gains(
        spectrum_ref, 1, table_ref, stretch, lon_east_ref, lon_west_ref, north_ref, south_ref,
        sub, lane, extra_of, keep,
    )
    coupling = coupling_ref[...] + gained
    energy = energy_ref[...]
    upper = sub >= LAT
    ice = ice_ref[...].astype(F32)
    rate = sea8 * (1.0 - jnp.concatenate([ice, ice], axis=0))
    base = sea8 - 0.2 * rate * energy
    set_weighted(table_ref, 0.2 * rate * coupling, add_ref)
    west_ref[...] = jnp.zeros_like(west_ref)
    east_ref[...] = jnp.zeros_like(east_ref)
    copies[0].wait()

    def source(i, carry):
        def value_of(q, jp):
            beta = rate_of(beta_ref, i + QUAD * q, jp, upper)
            place = direction_rows(i, q, jp)
            x = mu_ref[place, :] * (base + rate * beta) - add_ref[tab(jp), :]
            mu_ref[place, :] = x
            return x

        pack_edges(west_ref, east_ref, i, value_of, lane)
        return carry

    lax.fori_loop(0, QUAD, source, 0)
    send_rows(par, mu_ref, on_ref, off_ref)


def inner_kernel(level, where_ref, mu_ref, spectrum_ref, table_ref, *rest):
    sub, lane = iotas()
    nu_ref, coupling_ref, energy_ref = rest[-3:]
    sea8 = rest[0][...] if len(rest) == 4 else None

    def value_of(i, q, jp):
        mu = mu_ref[direction_rows(i, q, jp), :]
        return mu if sea8 is None else mu * sea8

    coupling, energy = move(
        nu_ref, spectrum_ref, level, table_ref, stretch_of(where_ref, table_ref), sub, lane,
        value_of, lambda i: lambda q, jp: 0.0, lambda i, q, jp: 0.0,
    )
    coupling_ref[...] = coupling
    energy_ref[...] = energy


def last_kernel(
    where_ref, beta_hbm, nu_ref, spectrum_ref, table_ref, ice_ref, coupling_ref, energy_ref,
    on_in, off_in, lon_east_ref, lon_west_ref,
    out_hbm,
    beta_ref, north_ref, south_ref, add_ref, gain_ref, sems, out_sems,
):
    copies = fetch(sems, (beta_hbm, beta_ref))
    par = where_ref[0] % 2
    sub, lane = iotas()
    row = sub % LAT
    spread_rows(par, on_in, off_in, north_ref, south_ref)
    stretch = stretch_of(where_ref, table_ref)

    def keep(place, jp, gain, extra):
        gain_ref[place, :] = gain
        return gain

    gained = edge_gains(
        spectrum_ref, 0, table_ref, stretch, lon_east_ref, lon_west_ref, north_ref, south_ref,
        sub, lane, lambda q, x_speed, y_speed: None, keep,
    )
    coupling = coupling_ref[...] + gained
    upper = sub >= LAT
    ice = ice_ref[...].astype(F32)
    rate = 1.0 - jnp.concatenate([ice, ice], axis=0)
    base = 1.0 - 0.2 * rate * energy_ref[...]
    set_weighted(table_ref, 0.2 * rate * coupling, add_ref)
    copies[0].wait()

    def chunk(g):
        rows = pl.ds(pl.multiple_of(g * 4 * BLOCK, 8), 4 * BLOCK)
        return pltpu.make_async_copy(gain_ref.at[rows], out_hbm.at[rows], out_sems.at[g])

    def body(g, carry):
        for jp in range(PAIRS):
            for h in range(4):
                beta = rate_of(beta_ref, 4 * g + h, jp, upper)
                place = pl.ds(pl.multiple_of((4 * g + h) * BLOCK + 8 * jp, 8), 8)
                x = (nu_ref[place, :] + gain_ref[place, :]) * (base + rate * beta)
                gain_ref[place, :] = x - add_ref[tab(jp), :]
        chunk(g).start()
        return carry

    lax.fori_loop(0, NDIR // 4, body, 0)
    for g in range(NDIR // 4):
        chunk(g).wait()


FIRST = 54


def params(limit=24):
    return pltpu.CompilerParams(vmem_limit_bytes=limit * MIB)


def f32(*shape):
    return jax.ShapeDtypeStruct(shape, F32)


def exchange(on, off, west, east):
    n_lon, n_lat = lax.axis_size("lon"), lax.axis_size("lat")
    near = [(i, i ^ 1) for i in range(n_lat)]
    far = [(i, ((i + 1) ^ 1) - 1) for i in range(1, n_lat - 1)]
    off = lax.ppermute(off, "lat", far)
    on = lax.ppermute(on, "lat", near)
    from_east = lax.ppermute(west, "lon", [(i, (i - 1) % n_lon) for i in range(n_lon)])
    from_west = lax.ppermute(east, "lon", [(i, (i + 1) % n_lon) for i in range(n_lon)])
    return on, off, from_east, from_west


def on_device(adj_final, saved, beta, sea_mask, ice_mask, obs_count, obs_cell, obs_value):
    table = jnp.asarray(constant_table())
    where = lax.axis_index("lat").astype(jnp.int32).reshape(1)
    adj = adj_final.reshape(ROWS, LON)
    saved = saved.reshape((STEPS + 1) * ROWS, LON)
    beta = beta.T
    tiles = lambda rows: pltpu.VMEM((rows, LON), F32)
    whole = lambda x: pltpu.VMEM(x.shape, x.dtype)
    level = pltpu.VMEM((ROWS, LON), jnp.bfloat16)
    payload = (f32(HALO, LON), f32(HALO, LON), f32(EDGE, LON), f32(EDGE, LON))
    dma = lambda *n: pltpu.SemaphoreType.DMA(n)

    on, off, west, east, obs, field, sea8, early = pl.pallas_call(
        start_kernel,
        out_shape=payload
        + (f32(128, 128), tiles(8), tiles(8))
        + (pltpu.VMEM((2 * ROWS, LON), jnp.bfloat16),),
        in_specs=[SMEM] + [HBM] * 7,
        out_specs=(VMEM,) * 8,
        scratch_shapes=[
            tiles(ROWS), level, tiles(BLOCK), whole(sea_mask), whole(obs_count), whole(obs_cell), whole(obs_value), dma(11),
        ],
        compiler_params=params(FIRST),
        name="edges_and_observations",
    )(where, adj, saved, table, sea_mask, obs_count, obs_cell, obs_value)

    on, off, from_east, from_west = exchange(on, off, west, east)
    obs = lax.all_to_all(obs.reshape(128, 1, 128), ("lon", "lat"), split_axis=0, concat_axis=0, tiled=True)
    obs = obs.reshape(128, 128)

    rates = pltpu.SMEM(beta.shape, F32)

    def inside(level, name, *operands):
        return pl.pallas_call(
            functools.partial(inner_kernel, level),
            out_shape=(f32(ROWS, LON), f32(8, LON), f32(8, LON)),
            in_specs=[SMEM] + [VMEM] * len(operands),
            out_specs=(VMEM,) * 3,
            compiler_params=params(),
            cost_estimate=pl.CostEstimate(flops=20_000_000, bytes_accessed=6_000_000, transcendentals=0),
            name=name,
        )(where, *operands)

    nu, coupling, energy = inside(1, "first_step_inside", adj, early, table, sea8)
    mu, on, off, west, east = pl.pallas_call(
        middle_kernel,
        out_shape=(f32(ROWS, LON),) + payload,
        in_specs=[SMEM, HBM] + [VMEM] * 13,
        out_specs=(VMEM,) * 5,
        scratch_shapes=[rates, tiles(SPREAD), tiles(SPREAD), tiles(16), tiles(BLOCK), dma(1)],
        compiler_params=params(),
        name="first_step_edges",
    )(
        where, beta, nu, early, table, sea8, ice_mask, field, coupling, energy, obs, on, off,
        from_east, from_west,
    )

    on, off, from_east, from_west = exchange(on, off, west, east)

    nu, coupling, energy = inside(0, "last_step_inside", mu, early, table)
    out = pl.pallas_call(
        last_kernel,
        out_shape=f32(ROWS, LON),
        in_specs=[SMEM, HBM] + [VMEM] * 10,
        out_specs=HBM,
        scratch_shapes=[rates, tiles(SPREAD), tiles(SPREAD), tiles(BLOCK), tiles(ROWS), dma(1), dma(NDIR // 4)],
        compiler_params=params(),
        name="last_step_edges",
    )(where, beta, nu, early, table, ice_mask, coupling, energy, on, off, from_east, from_west)
    return out.reshape(adj_final.shape)


def solution(mesh):
    return jax.shard_map(
        on_device,
        mesh=mesh,
        in_specs=(
            P(None, None, "lat", "lon"),
            P(None, None, None, "lat", "lon"),
            P(),
            P("lat", "lon"),
            P("lat", "lon"),
            P(("lon", "lat"), None),
            P(("lon", "lat"), None),
            P(("lon", "lat"), None),
        ),
        out_specs=P(None, None, "lat", "lon"),
        check_vma=False,
    )
```

```python
import math

import jax
import jax.numpy as jnp
import numpy as np
from jax import lax
from jax.experimental import pallas as pl
from jax.experimental.pallas import tpu as pltpu
from jax.sharding import PartitionSpec as P

STEPS = 2
CAP = 4
NDIR = 36
NFREQ = 30
QUAD = NDIR // 4
PAIRS = NFREQ // 2
LAT = 4
LON = 128
BLOCK = NFREQ * LAT
ROWS = NDIR * BLOCK
HALO = 552
SOUTH0 = 536
EDGE = 40
SPREAD = 2208
N_LAT = 16
N_LON = 8
MIB = 2**20
F32 = jnp.float32

HBM = pl.BlockSpec(memory_space=pltpu.HBM)
VMEM = pl.BlockSpec(memory_space=pltpu.VMEM)
SMEM = pl.BlockSpec(memory_space=pltpu.SMEM)

QUADRANTS = ((True, True), (True, False), (False, False), (False, True))

BOTH_WAYS = ((0, 1), (3, 2))

WEIGHT0 = 0
SPEED0 = BLOCK
COS0 = 2 * BLOCK
SIN0 = COS0 + 8 * QUAD
STRETCH0 = SIN0 + 8 * QUAD


def constant_table():
    angle = (np.arange(QUAD) + 0.5) * (2.0 * math.pi / NDIR)
    j = np.arange(NFREQ)
    speed = 1.1 ** (-j.astype(np.float64))
    growth = 1.1 ** j.astype(np.float64)
    weight = growth / (NDIR * growth.sum())
    rows = np.arange(N_LAT * LAT)
    latitude = (rows + 0.5 - N_LAT * LAT / 2.0) * (100.0 / (N_LAT * LAT))
    stretch = math.cos(50.0 * math.pi / 180.0) / np.cos(latitude * (math.pi / 180.0))
    stretch = np.tile(stretch.reshape(N_LAT, 1, LAT), (1, 2, 1)).reshape(-1)
    column = np.concatenate(
        [
            np.repeat(weight, LAT),
            np.repeat(speed, LAT),
            np.repeat(np.cos(angle), 8),
            np.repeat(np.sin(angle), 8),
            stretch,
        ]
    )
    return np.tile(column[:, None], (1, LON)).astype(np.float32)


def iotas():
    sub = lax.broadcasted_iota(jnp.int32, (8, LON), 0)
    lane = lax.broadcasted_iota(jnp.int32, (8, LON), 1)
    return sub, lane


def tab(jp):
    return slice(8 * jp, 8 * jp + 8)


def weights(table_ref, jp):
    return table_ref[WEIGHT0 + 8 * jp : WEIGHT0 + 8 * jp + 8, :]


def edge_block(quadrant, jp):
    first = 8 * (2 * (quadrant // 2) + jp // 8)
    return slice(first, first + 8)


def over_directions(body, carry):
    def two(v, carry):
        return body(2 * v + 1, 1, body(2 * v, 0, carry))

    carry = lax.fori_loop(0, QUAD // 2, two, carry)
    return body(QUAD - 1, (QUAD - 1) % 2, carry)


def spectrum_reader(ref, k, odd, level=0):
    first = level * ROWS + k * BLOCK - (8 if odd else 0)
    held = {}

    def read(jp):
        place, part = divmod(jp + odd, 2)
        if place not in held:
            held.clear()
            rows = pl.ds(pl.multiple_of(first + 16 * place, 16), 16)
            held[place] = ref[rows, :].astype(F32)
        return held[place][8 * part : 8 * part + 8, :]

    return read


def direction_rows(i, quadrant, jp=0, count=8):
    return pl.ds(pl.multiple_of((i + QUAD * quadrant) * BLOCK + 8 * jp, 8), count)


def piecewise(src, dst, sems, i):
    return [
        pltpu.make_async_copy(
            src.at[direction_rows(i, q, 0, BLOCK)], dst.at[direction_rows(i, q, 0, BLOCK)], sems.at[i, q]
        )
        for q in range(4)
    ]


def over_pieces(src, dst, sems, act):
    def body(i, carry):
        for copy in piecewise(src, dst, sems, i):
            act(copy)
        return carry

    lax.fori_loop(0, QUAD, body, 0)


def extract_rows(src, r, first, dst, scale):
    def body(m, carry):
        for u in range(4):
            start = (first + 8 * (4 * m + u)) * LAT + r
            value = src[pl.ds(start, 8, stride=LAT), :]
            if scale is not None:
                value = value * scale
            dst[pl.ds(pl.multiple_of(8 * (4 * m + u), 8), 8), :] = value
        return carry

    lax.fori_loop(0, 17, body, 0)


def send_rows(par, src, on_ref, off_ref, field=None, scale8=None):
    def put(dst, r, first):
        extract_rows(src, r, first, dst, None if scale8 is None else scale8[r : r + 1, :])
        if field is not None:
            dst[pl.ds(544, 8), :] = jnp.broadcast_to(field[r : r + 1, :], (8, LON))

    @pl.when(par == 0)
    def _():
        put(on_ref, LAT - 1, SOUTH0)
        put(off_ref, 0, 0)

    @pl.when(par == 1)
    def _():
        put(on_ref, 0, 0)
        put(off_ref, LAT - 1, SOUTH0)


def spread_rows(par, on_ref, off_ref, north_ref, south_ref, field_ref=None):
    def spread(src, dst, r):
        def body(m, carry):
            for u in range(4):
                first = 8 * (4 * m + u)
                dst[pl.ds(first * LAT + r, 8, stride=LAT), :] = src[pl.ds(pl.multiple_of(first, 8), 8), :]
            return carry

        lax.fori_loop(0, 17, body, 0)

    for parity, (north, south) in enumerate(((on_ref, off_ref), (off_ref, on_ref))):

        @pl.when(par == parity)
        def _():
            spread(north, north_ref, LAT - 1)
            spread(south, south_ref, 0)
            if field_ref is not None:
                field_ref[0:8, :] = north[544:552, :]
                field_ref[8:16, :] = south[544:552, :]


def pack_edges(west_ref, east_ref, i, value_of, lane):
    relative = lane - 8 * i
    here = (relative >= 0) & (relative < 8)
    for lo, hi in ((0, 8), (8, PAIRS)):
        blocks = [None] * 4
        for jp in range(lo, hi):
            c = jp - lo
            for eastward, westward in BOTH_WAYS:
                ends = jnp.where(lane == LON - 1, value_of(westward, jp), value_of(eastward, jp))
                ends = pltpu.roll(ends, c, axis=1) if c else ends
                for q, at in ((eastward, c), (westward, (c - 1) % LON)):
                    blocks[q] = jnp.where(lane == at, ends, blocks[q]) if c else ends
        for q, (_, east) in enumerate(QUADRANTS):
            ref = west_ref if east else east_ref
            place = edge_block(q, lo)
            moved = pltpu.roll(blocks[q], 8 * i + (0 if east else 1), axis=1)
            ref[place, :] = jnp.where(here, moved, ref[place, :])


def pick_observations(count, cell, value, out_ref):
    sub = lax.broadcasted_iota(jnp.int32, (128, 128), 0)
    lane = lax.broadcasted_iota(jnp.int32, (128, 128), 1)
    counts = jnp.broadcast_to(count.astype(F32), (128, 128))
    starts = jnp.sum(jnp.where(lane < sub, counts, 0.0), axis=1, keepdims=True)
    mine = jnp.sum(jnp.where(lane == sub, counts, 0.0), axis=1, keepdims=True)
    local = (((cell >> 10) & (LAT - 1)) * LON + (cell & (LON - 1))).astype(F32)
    slots = cell.shape[1]
    slot = lax.broadcasted_iota(jnp.int32, (128, slots), 1).astype(F32)
    listed = jnp.zeros((128, 128), F32)
    for i in range(CAP):
        hit = slot == starts + float(i)
        index_i = jnp.sum(jnp.where(hit, local, 0.0), axis=1, keepdims=True)
        value_i = jnp.sum(jnp.where(hit, value, 0.0), axis=1, keepdims=True)
        value_i = jnp.where(mine > float(i), value_i, 0.0)
        listed = jnp.where(lane == i, index_i, listed)
        listed = jnp.where(lane == CAP + i, value_i, listed)
    out = listed
    for place, shift in enumerate((127, 1, 128 - N_LAT, N_LAT)):
        moved = pltpu.roll(listed, shift, axis=0)
        out = out + pltpu.roll(moved, 8 * (place + 1), axis=1)
    out_ref[...] = out


def fetch(sems, *pairs, ahead=None):
    copies = [pltpu.make_async_copy(src, dst, sems.at[n]) for n, (src, dst) in enumerate(pairs)]
    for n, copy in enumerate(copies):
        if n == 5 and ahead is not None:
            ahead()
        copy.start()
    return copies


def start_kernel(
    where_ref, adj_hbm, saved_hbm, table_hbm, sea_hbm, count_hbm, cell_hbm, value_hbm,
    on_ref, off_ref, west_ref, east_ref, obs_ref, field_ref, sea8_ref, early_ref,
    adj_ref, final_ref, table_ref, sea_ref, count_ref, cell_ref, value_ref, sems, adj_sems,
):
    half = ROWS // 2
    final0 = STEPS * ROWS
    copies = fetch(
        sems,
        (count_hbm, count_ref),
        (cell_hbm, cell_ref),
        (value_hbm, value_ref),
        (sea_hbm, sea_ref),
        (table_hbm.at[pl.ds(0, BLOCK)], table_ref),
        (saved_hbm.at[pl.ds(final0, half)], final_ref.at[pl.ds(0, half)]),
        (saved_hbm.at[pl.ds(final0 + half, half)], final_ref.at[pl.ds(half, half)]),
        (saved_hbm.at[pl.ds(ROWS, ROWS)], early_ref.at[pl.ds(ROWS, ROWS)]),
        (saved_hbm.at[pl.ds(0, ROWS)], early_ref.at[pl.ds(0, ROWS)]),
        ahead=lambda: over_pieces(adj_hbm, adj_ref, adj_sems, lambda copy: copy.start()),
    )
    par = where_ref[0] % 2
    sub, lane = iotas()
    for copy in copies[:3]:
        copy.wait()
    pick_observations(count_ref[...], cell_ref[...], value_ref[...], obs_ref)
    for copy in copies[3:5]:
        copy.wait()
    sea = sea_ref[...].astype(F32)
    sea8 = jnp.concatenate([sea, sea], axis=0)
    sea8_ref[...] = sea8
    west_ref[...] = jnp.zeros_like(west_ref)
    east_ref[...] = jnp.zeros_like(east_ref)

    def pack(i, carry):
        for copy in piecewise(adj_hbm, adj_ref, adj_sems, i):
            copy.wait()
        pack_edges(west_ref, east_ref, i, lambda q, jp: adj_ref[direction_rows(i, q, jp), :], lane)
        return carry

    lax.fori_loop(0, QUAD, pack, 0)
    for copy in copies[5:7]:
        copy.wait()

    def moment(i, odd, total):
        read = [spectrum_reader(final_ref, i + QUAD * q, (odd + q) % 2) for q in range(4)]
        for jp in range(PAIRS):
            both = (read[0](jp) + read[1](jp)) + (read[2](jp) + read[3](jp))
            total = total + weights(table_ref, jp) * both
        return total

    total = over_directions(moment, jnp.zeros((8, LON), F32))
    field = sea8 * 2.0 / jnp.sqrt(both_halves(total))
    field_ref[...] = field
    send_rows(par, adj_ref, on_ref, off_ref, field_ref, sea8_ref)
    west_sea = jnp.broadcast_to(sea8[:, :1], (8, LON))
    east_sea = jnp.broadcast_to(sea8[:, LON - 1 :], (8, LON))
    for block in range(4):
        west_ref[tab(block), :] = west_ref[tab(block), :] * west_sea
        east_ref[tab(block), :] = east_ref[tab(block), :] * east_sea
    west_ref[32:40, :] = jnp.broadcast_to(field[:, :1], (8, LON))
    east_ref[32:40, :] = jnp.broadcast_to(field[:, LON - 1 :], (8, LON))
    for copy in copies[7:]:
        copy.wait()


def speeds_of(table_ref, stretch, i):
    cos_i = table_ref[pl.ds(pl.multiple_of(COS0 + 8 * i, 8), 8), :]
    sin_i = table_ref[pl.ds(pl.multiple_of(SIN0 + 8 * i, 8), 8), :]
    stretched = 0.7 * stretch
    return (cos_i * stretched, sin_i * stretched), (0.6 * sin_i, 0.6 * cos_i)


def turned_edges(lon_east_ref, lon_west_ref, i, lane):
    turned = {}
    for q, (_, east) in enumerate(QUADRANTS):
        for lo in (0, 8):
            ref = lon_east_ref if east else lon_west_ref
            turn = (LON - 8 * i + (0 if east else 1)) % LON
            turned[q, lo] = pltpu.roll(ref[edge_block(q, lo), :], turn, axis=1)
    held = {}

    def edge(q, jp):
        pair = q // 2
        if held.get(pair, (None, None))[0] != jp:
            eastward, westward = BOTH_WAYS[pair]
            lo, c = 8 * (jp // 8), jp % 8
            ends = jnp.where(lane == c + 1, turned[westward, lo], turned[eastward, lo])
            held[pair] = (jp, pltpu.roll(ends, LON - 1 - c, axis=1))
        return held[pair][1]

    return edge


def row_halo_of(north_ref, south_ref, i, q, jp):
    if QUADRANTS[q][0]:
        return north_ref[direction_rows(i, q, jp), :]
    row = (i + QUAD * q - NDIR // 2) * BLOCK + 8 * jp + 16
    return south_ref[pl.ds(pl.multiple_of(row, 8), 8), :]


def both_halves(total):
    return total + pltpu.roll(total, 4, axis=0)


def speed_of(table_ref, jp):
    return table_ref[SPEED0 + 8 * jp : SPEED0 + 8 * jp + 8, :]


def move(
    dst_ref, spectrum_ref, level, table_ref, stretch, sub, lane, value_of, lon_of, row_of,
    before=lambda i: None, after=lambda i: None,
):
    row = sub % LAT

    def body(i, odd, carry):
        before(i)
        coupling, energy = carry
        x_speed, y_speed = speeds_of(table_ref, stretch, i)
        read = [spectrum_reader(spectrum_ref, i + QUAD * q, (odd + q) % 2, level) for q in range(4)]
        lon_halo = lon_of(i)
        for jp in range(PAIRS):
            all_of = None
            for q, (north, east) in enumerate(QUADRANTS):
                spectrum = read[q](jp)
                mu = value_of(i, q, jp)
                turned = pltpu.roll(mu, LON - 1 if east else 1, axis=1)
                along = jnp.where(lane == (LON - 1 if east else 0), lon_halo(q, jp), turned)
                shifted = pltpu.roll(mu, 7 if north else 1, axis=0)
                across = jnp.where(row == (LAT - 1 if north else 0), row_of(i, q, jp), shifted)
                change = x_speed[q % 2] * (along - mu) + y_speed[q % 2] * (across - mu)
                nu = mu + speed_of(table_ref, jp) * change
                dst_ref[direction_rows(i, q, jp), :] = nu
                coupling = coupling + spectrum * nu
                all_of = spectrum if all_of is None else all_of + spectrum
            energy = energy + weights(table_ref, jp) * all_of
        after(i)
        return coupling, energy

    coupling, energy = over_directions(body, (jnp.zeros((8, LON), F32), jnp.zeros((8, LON), F32)))
    return both_halves(coupling), both_halves(energy)


def stretch_of(where_ref, table_ref):
    return table_ref[pl.ds(pl.multiple_of(STRETCH0 + 8 * where_ref[0], 8), 8), :]


def set_weighted(table_ref, field, dst_ref):
    for jp in range(PAIRS):
        dst_ref[tab(jp), :] = weights(table_ref, jp) * field


def rate_of(beta_ref, k, jp, upper):
    return jnp.where(upper, beta_ref[2 * jp + 1, k], beta_ref[2 * jp, k])


def edge_gains(
    spectrum_ref, level, table_ref, stretch, lon_east_ref, lon_west_ref, north_ref, south_ref,
    sub, lane, extra_of, keep,
):
    row = sub % LAT

    def body(i, odd, coupling):
        x_speed, y_speed = speeds_of(table_ref, stretch, i)
        read = [spectrum_reader(spectrum_ref, i + QUAD * q, (odd + q) % 2, level) for q in range(4)]
        edge = turned_edges(lon_east_ref, lon_west_ref, i, lane)
        extra = [extra_of(q, x_speed[q % 2], y_speed[q % 2]) for q in range(4)]
        for jp in range(PAIRS):
            for q, (north, east) in enumerate(QUADRANTS):
                along = jnp.where(lane == (LON - 1 if east else 0), edge(q, jp), 0.0)
                halo = row_halo_of(north_ref, south_ref, i, q, jp)
                across = jnp.where(row == (LAT - 1 if north else 0), halo, 0.0)
                gain = speed_of(table_ref, jp) * (x_speed[q % 2] * along + y_speed[q % 2] * across)
                gain = keep(direction_rows(i, q, jp), jp, gain, extra[q])
                coupling = coupling + read[q](jp) * gain
        return coupling

    return both_halves(over_directions(body, jnp.zeros((8, LON), F32)))


def three_parts(x):
    parts = []
    for _ in range(3):
        part = x.astype(jnp.bfloat16)
        parts.append(part)
        x = x - part.astype(F32)
    return jnp.concatenate(parts, axis=0)


def sum_observations(obs_ref, sub, lane):
    listed = jnp.transpose(obs_ref[...])
    column = lax.broadcasted_iota(jnp.int32, (128, 128), 0).astype(F32)
    row8 = (sub % LAT).astype(F32)

    def slots(tile):
        for i in range(CAP):
            index = listed[8 * tile + i : 8 * tile + i + 1, :]
            value = listed[8 * tile + CAP + i : 8 * tile + CAP + i + 1, :]
            row = jnp.floor(index * (1.0 / LON))
            yield row, index - row * LON, value

    def spread(tile, takes):
        left, right = [], []
        for row, col, value in slots(tile):
            left.append(jnp.where(takes(row), value, jnp.zeros((8, LON), F32)))
            right.append(jnp.where(column == col, 1.0, 0.0).astype(jnp.bfloat16))
        parts = three_parts(jnp.concatenate(left, axis=1))
        out = lax.dot_general(
            parts, jnp.concatenate(right, axis=1), (((1,), (1,)), ((), ())), preferred_element_type=F32
        )
        return out[0:8, :] + out[8:16, :] + out[16:24, :]

    def line(tile, at):
        total = jnp.zeros((8, LON), F32)
        for row, col, value in slots(tile):
            total = total + jnp.where((row8 == row) & (col == at), value, 0.0)
        return jnp.sum(total, axis=1, keepdims=True)

    own = spread(0, lambda row: row8 == row)
    north = spread(1, lambda row: row8 * 0.0 == row)
    south = spread(2, lambda row: row8 * 0.0 + (LAT - 1.0) == row)
    return own, north, south, line(3, 0.0), line(4, LON - 1.0)


def middle_kernel(
    where_ref, beta_hbm, nu_hbm, spectrum_ref, table_ref, sea8_ref, ice_ref, field_ref,
    coupling_ref, energy_ref, obs_ref, on_in, off_in, lon_east_ref, lon_west_ref,
    mu_ref, on_ref, off_ref, west_ref, east_ref,
    beta_ref, nu_ref, north_ref, south_ref, fields_ref, add_ref, sems,
):
    copies = fetch(sems, (beta_hbm, beta_ref), (nu_hbm, nu_ref))
    par = where_ref[0] % 2
    sub, lane = iotas()
    row = sub % LAT
    sea8 = sea8_ref[...]
    stretch = stretch_of(where_ref, table_ref)
    force, force_n, force_s, force_e, force_w = sum_observations(obs_ref, sub, lane)
    spread_rows(par, on_in, off_in, north_ref, south_ref, fields_ref)

    own = force * field_ref[...]
    set_weighted(table_ref, own, add_ref)
    first_weight = table_ref[WEIGHT0 : WEIGHT0 + 1, :]
    along_of, across_of = {}, {}
    for east, halo, ref in ((True, force_e, lon_east_ref), (False, force_w, lon_west_ref)):
        beside = halo * ref[32:40, :]
        turned = pltpu.roll(own, LON - 1 if east else 1, axis=1)
        here = jnp.where(lane == (LON - 1 if east else 0), beside, turned)
        along_of[east] = first_weight * (here - own)
    for north, halo, place in ((True, force_n, 0), (False, force_s, 8)):
        beside = halo * fields_ref[place : place + 8, :]
        shifted = pltpu.roll(own, 7 if north else 1, axis=0)
        here = jnp.where(row == (LAT - 1 if north else 0), beside, shifted)
        across_of[north] = first_weight * (here - own)

    def extra_of(q, x_speed, y_speed):
        north, east = QUADRANTS[q]
        return x_speed * along_of[east] + y_speed * across_of[north]

    def keep(place, jp, gain, extra):
        gain = gain + (add_ref[tab(jp), :] + extra)
        mu_ref[place, :] = gain
        return gain

    gained = edge_gains(
        spectrum_ref, 1, table_ref, stretch, lon_east_ref, lon_west_ref, north_ref, south_ref,
        sub, lane, extra_of, keep,
    )
    coupling = coupling_ref[...] + gained
    energy = energy_ref[...]
    upper = sub >= LAT
    ice = ice_ref[...].astype(F32)
    rate = sea8 * (1.0 - jnp.concatenate([ice, ice], axis=0))
    base = sea8 - 0.2 * rate * energy
    set_weighted(table_ref, 0.2 * rate * coupling, add_ref)
    west_ref[...] = jnp.zeros_like(west_ref)
    east_ref[...] = jnp.zeros_like(east_ref)
    for copy in copies:
        copy.wait()

    def source(i, carry):
        def value_of(q, jp):
            beta = rate_of(beta_ref, i + QUAD * q, jp, upper)
            place = direction_rows(i, q, jp)
            x = (nu_ref[place, :] + mu_ref[place, :]) * (base + rate * beta) - add_ref[tab(jp), :]
            mu_ref[place, :] = x
            return x

        pack_edges(west_ref, east_ref, i, value_of, lane)
        return carry

    lax.fori_loop(0, QUAD, source, 0)
    send_rows(par, mu_ref, on_ref, off_ref)


def first_inner_kernel(
    where_ref, adj_hbm, spectrum_ref, table_ref, sea8_ref, nu_hbm, coupling_ref, energy_ref,
    adj_ref, nu_ref, adj_sems, nu_sems,
):
    over_pieces(adj_hbm, adj_ref, adj_sems, lambda copy: copy.start())
    sub, lane = iotas()
    sea8 = sea8_ref[...]

    def before(i):
        for copy in piecewise(adj_hbm, adj_ref, adj_sems, i):
            copy.wait()

    def after(i):
        for copy in piecewise(nu_ref, nu_hbm, nu_sems, i):
            copy.start()

    coupling_ref[...], energy_ref[...] = move(
        nu_ref, spectrum_ref, 1, table_ref, stretch_of(where_ref, table_ref), sub, lane,
        lambda i, q, jp: adj_ref[direction_rows(i, q, jp), :] * sea8,
        lambda i: lambda q, jp: 0.0, lambda i, q, jp: 0.0, before, after,
    )
    over_pieces(nu_ref, nu_hbm, nu_sems, lambda copy: copy.wait())


def inner_kernel(where_ref, mu_ref, spectrum_ref, table_ref, nu_ref, coupling_ref, energy_ref):
    sub, lane = iotas()
    coupling_ref[...], energy_ref[...] = move(
        nu_ref, spectrum_ref, 0, table_ref, stretch_of(where_ref, table_ref), sub, lane,
        lambda i, q, jp: mu_ref[direction_rows(i, q, jp), :],
        lambda i: lambda q, jp: 0.0, lambda i, q, jp: 0.0,
    )


def last_kernel(
    where_ref, beta_hbm, nu_ref, spectrum_ref, table_ref, ice_ref, coupling_ref, energy_ref,
    on_in, off_in, lon_east_ref, lon_west_ref,
    out_hbm,
    beta_ref, north_ref, south_ref, add_ref, gain_ref, sems, out_sems,
):
    copies = fetch(sems, (beta_hbm, beta_ref))
    par = where_ref[0] % 2
    sub, lane = iotas()
    row = sub % LAT
    spread_rows(par, on_in, off_in, north_ref, south_ref)
    stretch = stretch_of(where_ref, table_ref)

    def keep(place, jp, gain, extra):
        gain_ref[place, :] = gain
        return gain

    gained = edge_gains(
        spectrum_ref, 0, table_ref, stretch, lon_east_ref, lon_west_ref, north_ref, south_ref,
        sub, lane, lambda q, x_speed, y_speed: None, keep,
    )
    coupling = coupling_ref[...] + gained
    upper = sub >= LAT
    ice = ice_ref[...].astype(F32)
    rate = 1.0 - jnp.concatenate([ice, ice], axis=0)
    base = 1.0 - 0.2 * rate * energy_ref[...]
    set_weighted(table_ref, 0.2 * rate * coupling, add_ref)
    copies[0].wait()

    def chunk(g):
        rows = pl.ds(pl.multiple_of(g * 4 * BLOCK, 8), 4 * BLOCK)
        return pltpu.make_async_copy(gain_ref.at[rows], out_hbm.at[rows], out_sems.at[g])

    def body(g, carry):
        for jp in range(PAIRS):
            for h in range(4):
                beta = rate_of(beta_ref, 4 * g + h, jp, upper)
                place = pl.ds(pl.multiple_of((4 * g + h) * BLOCK + 8 * jp, 8), 8)
                x = (nu_ref[place, :] + gain_ref[place, :]) * (base + rate * beta)
                gain_ref[place, :] = x - add_ref[tab(jp), :]
        chunk(g).start()
        return carry

    lax.fori_loop(0, NDIR // 4, body, 0)
    for g in range(NDIR // 4):
        chunk(g).wait()


FIRST = 54


def params(limit=24):
    return pltpu.CompilerParams(vmem_limit_bytes=limit * MIB)


def f32(*shape):
    return jax.ShapeDtypeStruct(shape, F32)


def exchange(on, off, west, east):
    n_lon, n_lat = lax.axis_size("lon"), lax.axis_size("lat")
    near = [(i, i ^ 1) for i in range(n_lat)]
    far = [(i, ((i + 1) ^ 1) - 1) for i in range(1, n_lat - 1)]
    off = lax.ppermute(off, "lat", far)
    on = lax.ppermute(on, "lat", near)
    from_east = lax.ppermute(west, "lon", [(i, (i - 1) % n_lon) for i in range(n_lon)])
    from_west = lax.ppermute(east, "lon", [(i, (i + 1) % n_lon) for i in range(n_lon)])
    return on, off, from_east, from_west


def on_device(adj_final, saved, beta, sea_mask, ice_mask, obs_count, obs_cell, obs_value):
    table = jnp.asarray(constant_table())
    where = lax.axis_index("lat").astype(jnp.int32).reshape(1)
    adj = adj_final.reshape(ROWS, LON)
    saved = saved.reshape((STEPS + 1) * ROWS, LON)
    beta = beta.T
    tiles = lambda rows: pltpu.VMEM((rows, LON), F32)
    whole = lambda x: pltpu.VMEM(x.shape, x.dtype)
    level = pltpu.VMEM((ROWS, LON), jnp.bfloat16)
    payload = (f32(HALO, LON), f32(HALO, LON), f32(EDGE, LON), f32(EDGE, LON))
    dma = lambda *n: pltpu.SemaphoreType.DMA(n)

    on, off, west, east, obs, field, sea8, early = pl.pallas_call(
        start_kernel,
        out_shape=payload
        + (f32(128, 128), tiles(8), tiles(8))
        + (pltpu.VMEM((2 * ROWS, LON), jnp.bfloat16),),
        in_specs=[SMEM] + [HBM] * 7,
        out_specs=(VMEM,) * 8,
        scratch_shapes=[
            tiles(ROWS), level, tiles(BLOCK), whole(sea_mask), whole(obs_count), whole(obs_cell), whole(obs_value), dma(9),
            dma(QUAD, 4),
        ],
        compiler_params=params(FIRST),
        name="edges_and_observations",
    )(where, adj, saved, table, sea_mask, obs_count, obs_cell, obs_value)

    on, off, from_east, from_west = exchange(on, off, west, east)
    obs = lax.all_to_all(obs.reshape(128, 1, 128), ("lon", "lat"), split_axis=0, concat_axis=0, tiled=True)
    obs = obs.reshape(128, 128)

    rates = pltpu.SMEM(beta.shape, F32)

    hint = pl.CostEstimate(flops=20_000_000, bytes_accessed=6_000_000, transcendentals=0)
    nu, coupling, energy = pl.pallas_call(
        first_inner_kernel,
        out_shape=(pltpu.HBM((ROWS, LON), F32), tiles(8), tiles(8)),
        in_specs=[SMEM, HBM] + [VMEM] * 3,
        out_specs=(HBM, VMEM, VMEM),
        scratch_shapes=[tiles(ROWS), tiles(ROWS), dma(QUAD, 4), dma(QUAD, 4)],
        compiler_params=params(),
        cost_estimate=hint,
        name="first_step_inside",
    )(where, pltpu.with_memory_space_constraint(adj, pltpu.HBM), early, table, sea8)
    mu, on, off, west, east = pl.pallas_call(
        middle_kernel,
        out_shape=(f32(ROWS, LON),) + payload,
        in_specs=[SMEM, HBM, HBM] + [VMEM] * 12,
        out_specs=(VMEM,) * 5,
        scratch_shapes=[rates, tiles(ROWS), tiles(SPREAD), tiles(SPREAD), tiles(16), tiles(BLOCK), dma(2)],
        compiler_params=params(),
        name="first_step_edges",
    )(
        where, beta, pltpu.with_memory_space_constraint(nu, pltpu.HBM), early, table, sea8, ice_mask, field, coupling, energy, obs, on, off,
        from_east, from_west,
    )

    on, off, from_east, from_west = exchange(on, off, west, east)

    nu, coupling, energy = pl.pallas_call(
        inner_kernel,
        out_shape=(f32(ROWS, LON), f32(8, LON), f32(8, LON)),
        in_specs=[SMEM] + [VMEM] * 3,
        out_specs=(VMEM,) * 3,
        compiler_params=params(),
        cost_estimate=hint,
        name="last_step_inside",
    )(where, mu, early, table)
    out = pl.pallas_call(
        last_kernel,
        out_shape=f32(ROWS, LON),
        in_specs=[SMEM, HBM] + [VMEM] * 10,
        out_specs=HBM,
        scratch_shapes=[rates, tiles(SPREAD), tiles(SPREAD), tiles(BLOCK), tiles(ROWS), dma(1), dma(NDIR // 4)],
        compiler_params=params(),
        name="last_step_edges",
    )(where, beta, nu, early, table, ice_mask, coupling, energy, on, off, from_east, from_west)
    return out.reshape(adj_final.shape)


def solution(mesh):
    return jax.shard_map(
        on_device,
        mesh=mesh,
        in_specs=(
            P(None, None, "lat", "lon"),
            P(None, None, None, "lat", "lon"),
            P(),
            P("lat", "lon"),
            P("lat", "lon"),
            P(("lon", "lat"), None),
            P(("lon", "lat"), None),
            P(("lon", "lat"), None),
        ),
        out_specs=P(None, None, "lat", "lon"),
        check_vma=False,
    )
```

```python
import math

import jax
import jax.numpy as jnp
import numpy as np
from jax import lax
from jax.experimental import pallas as pl
from jax.experimental.pallas import tpu as pltpu
from jax.sharding import PartitionSpec as P

STEPS = 2
CAP = 4
NDIR = 36
NFREQ = 30
QUAD = NDIR // 4
PAIRS = NFREQ // 2
LAT = 4
LON = 128
BLOCK = NFREQ * LAT
ROWS = NDIR * BLOCK
HALO = 552
SOUTH0 = 536
EDGE = 40
SPREAD = 2208
N_LAT = 16
N_LON = 8
MIB = 2**20
F32 = jnp.float32

HBM = pl.BlockSpec(memory_space=pltpu.HBM)
VMEM = pl.BlockSpec(memory_space=pltpu.VMEM)
SMEM = pl.BlockSpec(memory_space=pltpu.SMEM)

QUADRANTS = ((True, True), (True, False), (False, False), (False, True))

BOTH_WAYS = ((0, 1), (3, 2))

WEIGHT0 = 0
SPEED0 = BLOCK
COS0 = 2 * BLOCK
SIN0 = COS0 + 8 * QUAD
STRETCH0 = SIN0 + 8 * QUAD


def constant_table():
    angle = (np.arange(QUAD) + 0.5) * (2.0 * math.pi / NDIR)
    j = np.arange(NFREQ)
    speed = 1.1 ** (-j.astype(np.float64))
    growth = 1.1 ** j.astype(np.float64)
    weight = growth / (NDIR * growth.sum())
    rows = np.arange(N_LAT * LAT)
    latitude = (rows + 0.5 - N_LAT * LAT / 2.0) * (100.0 / (N_LAT * LAT))
    stretch = math.cos(50.0 * math.pi / 180.0) / np.cos(latitude * (math.pi / 180.0))
    stretch = np.tile(stretch.reshape(N_LAT, 1, LAT), (1, 2, 1)).reshape(-1)
    column = np.concatenate(
        [
            np.repeat(weight, LAT),
            np.repeat(speed, LAT),
            np.repeat(np.cos(angle), 8),
            np.repeat(np.sin(angle), 8),
            stretch,
        ]
    )
    return np.tile(column[:, None], (1, LON)).astype(np.float32)


def iotas():
    sub = lax.broadcasted_iota(jnp.int32, (8, LON), 0)
    lane = lax.broadcasted_iota(jnp.int32, (8, LON), 1)
    return sub, lane


def tab(jp):
    return slice(8 * jp, 8 * jp + 8)


def weights(table_ref, jp):
    return table_ref[WEIGHT0 + 8 * jp : WEIGHT0 + 8 * jp + 8, :]


def edge_block(quadrant, jp):
    first = 8 * (2 * (quadrant // 2) + jp // 8)
    return slice(first, first + 8)


def over_directions(body, carry):
    def two(v, carry):
        return body(2 * v + 1, 1, body(2 * v, 0, carry))

    carry = lax.fori_loop(0, QUAD // 2, two, carry)
    return body(QUAD - 1, (QUAD - 1) % 2, carry)


def spectrum_reader(ref, k, odd, level=0):
    first = level * ROWS + k * BLOCK - (8 if odd else 0)
    held = {}

    def read(jp):
        place, part = divmod(jp + odd, 2)
        if place not in held:
            held.clear()
            rows = pl.ds(pl.multiple_of(first + 16 * place, 16), 16)
            held[place] = ref[rows, :].astype(F32)
        return held[place][8 * part : 8 * part + 8, :]

    return read


def direction_rows(i, quadrant, jp=0, count=8):
    return pl.ds(pl.multiple_of((i + QUAD * quadrant) * BLOCK + 8 * jp, 8), count)


def piecewise(src, dst, sems, i):
    return [
        pltpu.make_async_copy(
            src.at[direction_rows(i, q, 0, BLOCK)], dst.at[direction_rows(i, q, 0, BLOCK)], sems.at[i, q]
        )
        for q in range(4)
    ]


def over_pieces(src, dst, sems, act):
    def body(i, carry):
        for copy in piecewise(src, dst, sems, i):
            act(copy)
        return carry

    lax.fori_loop(0, QUAD, body, 0)


def extract_rows(src, r, first, dst, scale):
    def body(m, carry):
        for u in range(4):
            start = (first + 8 * (4 * m + u)) * LAT + r
            value = src[pl.ds(start, 8, stride=LAT), :]
            if scale is not None:
                value = value * scale
            dst[pl.ds(pl.multiple_of(8 * (4 * m + u), 8), 8), :] = value
        return carry

    lax.fori_loop(0, 17, body, 0)


def send_rows(par, src, on_ref, off_ref, field=None, scale8=None):
    def put(dst, r, first):
        extract_rows(src, r, first, dst, None if scale8 is None else scale8[r : r + 1, :])
        if field is not None:
            dst[pl.ds(544, 8), :] = jnp.broadcast_to(field[r : r + 1, :], (8, LON))

    @pl.when(par == 0)
    def _():
        put(on_ref, LAT - 1, SOUTH0)
        put(off_ref, 0, 0)

    @pl.when(par == 1)
    def _():
        put(on_ref, 0, 0)
        put(off_ref, LAT - 1, SOUTH0)


def spread_rows(par, on_ref, off_ref, north_ref, south_ref, field_ref=None):
    def spread(src, dst, r):
        def body(m, carry):
            for u in range(4):
                first = 8 * (4 * m + u)
                dst[pl.ds(first * LAT + r, 8, stride=LAT), :] = src[pl.ds(pl.multiple_of(first, 8), 8), :]
            return carry

        lax.fori_loop(0, 17, body, 0)

    for parity, (north, south) in enumerate(((on_ref, off_ref), (off_ref, on_ref))):

        @pl.when(par == parity)
        def _():
            spread(north, north_ref, LAT - 1)
            spread(south, south_ref, 0)
            if field_ref is not None:
                field_ref[0:8, :] = north[544:552, :]
                field_ref[8:16, :] = south[544:552, :]


def pack_edges(west_ref, east_ref, i, value_of, lane):
    relative = lane - 8 * i
    here = (relative >= 0) & (relative < 8)
    for lo, hi in ((0, 8), (8, PAIRS)):
        blocks = [None] * 4
        for jp in range(lo, hi):
            c = jp - lo
            for eastward, westward in BOTH_WAYS:
                ends = jnp.where(lane == LON - 1, value_of(westward, jp), value_of(eastward, jp))
                ends = pltpu.roll(ends, c, axis=1) if c else ends
                for q, at in ((eastward, c), (westward, (c - 1) % LON)):
                    blocks[q] = jnp.where(lane == at, ends, blocks[q]) if c else ends
        for q, (_, east) in enumerate(QUADRANTS):
            ref = west_ref if east else east_ref
            place = edge_block(q, lo)
            moved = pltpu.roll(blocks[q], 8 * i + (0 if east else 1), axis=1)
            ref[place, :] = jnp.where(here, moved, ref[place, :])


def pick_observations(count, cell, value, out_ref):
    sub = lax.broadcasted_iota(jnp.int32, (128, 128), 0)
    lane = lax.broadcasted_iota(jnp.int32, (128, 128), 1)
    counts = jnp.broadcast_to(count.astype(F32), (128, 128))
    starts = jnp.sum(jnp.where(lane < sub, counts, 0.0), axis=1, keepdims=True)
    mine = jnp.sum(jnp.where(lane == sub, counts, 0.0), axis=1, keepdims=True)
    local = (((cell >> 10) & (LAT - 1)) * LON + (cell & (LON - 1))).astype(F32)
    slots = cell.shape[1]
    slot = lax.broadcasted_iota(jnp.int32, (128, slots), 1).astype(F32)
    listed = jnp.zeros((128, 128), F32)
    for i in range(CAP):
        hit = slot == starts + float(i)
        index_i = jnp.sum(jnp.where(hit, local, 0.0), axis=1, keepdims=True)
        value_i = jnp.sum(jnp.where(hit, value, 0.0), axis=1, keepdims=True)
        value_i = jnp.where(mine > float(i), value_i, 0.0)
        listed = jnp.where(lane == i, index_i, listed)
        listed = jnp.where(lane == CAP + i, value_i, listed)
    out = listed
    for place, shift in enumerate((127, 1, 128 - N_LAT, N_LAT)):
        moved = pltpu.roll(listed, shift, axis=0)
        out = out + pltpu.roll(moved, 8 * (place + 1), axis=1)
    out_ref[...] = out


def fetch(sems, *pairs, ahead=None):
    copies = [pltpu.make_async_copy(src, dst, sems.at[n]) for n, (src, dst) in enumerate(pairs)]
    for n, copy in enumerate(copies):
        if n == 5 and ahead is not None:
            ahead()
        copy.start()
    return copies


def start_kernel(
    where_ref, adj_hbm, saved_hbm, table_hbm, sea_hbm, count_hbm, cell_hbm, value_hbm,
    on_ref, off_ref, west_ref, east_ref, obs_ref, field_ref, sea8_ref, early_ref,
    adj_ref, final_ref, table_ref, sea_ref, count_ref, cell_ref, value_ref, sems, adj_sems,
):
    half = ROWS // 2
    final0 = STEPS * ROWS
    copies = fetch(
        sems,
        (count_hbm, count_ref),
        (cell_hbm, cell_ref),
        (value_hbm, value_ref),
        (sea_hbm, sea_ref),
        (table_hbm.at[pl.ds(0, BLOCK)], table_ref),
        (saved_hbm.at[pl.ds(final0, half)], final_ref.at[pl.ds(0, half)]),
        (saved_hbm.at[pl.ds(final0 + half, half)], final_ref.at[pl.ds(half, half)]),
        (saved_hbm.at[pl.ds(ROWS, ROWS)], early_ref.at[pl.ds(ROWS, ROWS)]),
        (saved_hbm.at[pl.ds(0, ROWS)], early_ref.at[pl.ds(0, ROWS)]),
        ahead=lambda: over_pieces(adj_hbm, adj_ref, adj_sems, lambda copy: copy.start()),
    )
    par = where_ref[0] % 2
    sub, lane = iotas()
    for copy in copies[:3]:
        copy.wait()
    pick_observations(count_ref[...], cell_ref[...], value_ref[...], obs_ref)
    for copy in copies[3:5]:
        copy.wait()
    sea = sea_ref[...].astype(F32)
    sea8 = jnp.concatenate([sea, sea], axis=0)
    sea8_ref[...] = sea8
    west_ref[...] = jnp.zeros_like(west_ref)
    east_ref[...] = jnp.zeros_like(east_ref)

    def pack(i, carry):
        for copy in piecewise(adj_hbm, adj_ref, adj_sems, i):
            copy.wait()
        pack_edges(west_ref, east_ref, i, lambda q, jp: adj_ref[direction_rows(i, q, jp), :], lane)
        return carry

    lax.fori_loop(0, QUAD, pack, 0)
    for copy in copies[5:7]:
        copy.wait()

    def moment(i, odd, total):
        read = [spectrum_reader(final_ref, i + QUAD * q, (odd + q) % 2) for q in range(4)]
        for jp in range(PAIRS):
            both = (read[0](jp) + read[1](jp)) + (read[2](jp) + read[3](jp))
            total = total + weights(table_ref, jp) * both
        return total

    total = over_directions(moment, jnp.zeros((8, LON), F32))
    field = sea8 * 2.0 / jnp.sqrt(both_halves(total))
    field_ref[...] = field
    send_rows(par, adj_ref, on_ref, off_ref, field_ref, sea8_ref)
    west_sea = jnp.broadcast_to(sea8[:, :1], (8, LON))
    east_sea = jnp.broadcast_to(sea8[:, LON - 1 :], (8, LON))
    for block in range(4):
        west_ref[tab(block), :] = west_ref[tab(block), :] * west_sea
        east_ref[tab(block), :] = east_ref[tab(block), :] * east_sea
    west_ref[32:40, :] = jnp.broadcast_to(field[:, :1], (8, LON))
    east_ref[32:40, :] = jnp.broadcast_to(field[:, LON - 1 :], (8, LON))
    for copy in copies[7:]:
        copy.wait()


def speeds_of(table_ref, stretch, i):
    cos_i = table_ref[pl.ds(pl.multiple_of(COS0 + 8 * i, 8), 8), :]
    sin_i = table_ref[pl.ds(pl.multiple_of(SIN0 + 8 * i, 8), 8), :]
    stretched = 0.7 * stretch
    return (cos_i * stretched, sin_i * stretched), (0.6 * sin_i, 0.6 * cos_i)


def turned_edges(lon_east_ref, lon_west_ref, i, lane):
    turned = {}
    for q, (_, east) in enumerate(QUADRANTS):
        for lo in (0, 8):
            ref = lon_east_ref if east else lon_west_ref
            turn = (LON - 8 * i + (0 if east else 1)) % LON
            turned[q, lo] = pltpu.roll(ref[edge_block(q, lo), :], turn, axis=1)
    held = {}

    def edge(q, jp):
        pair = q // 2
        if held.get(pair, (None, None))[0] != jp:
            eastward, westward = BOTH_WAYS[pair]
            lo, c = 8 * (jp // 8), jp % 8
            ends = jnp.where(lane == c + 1, turned[westward, lo], turned[eastward, lo])
            held[pair] = (jp, pltpu.roll(ends, LON - 1 - c, axis=1))
        return held[pair][1]

    return edge


def row_halo_of(north_ref, south_ref, i, q, jp):
    if QUADRANTS[q][0]:
        return north_ref[direction_rows(i, q, jp), :]
    row = (i + QUAD * q - NDIR // 2) * BLOCK + 8 * jp + 16
    return south_ref[pl.ds(pl.multiple_of(row, 8), 8), :]


def both_halves(total):
    return total + pltpu.roll(total, 4, axis=0)


def speed_of(table_ref, jp):
    return table_ref[SPEED0 + 8 * jp : SPEED0 + 8 * jp + 8, :]


def move(
    dst_ref, spectrum_ref, level, table_ref, stretch, sub, lane, value_of, lon_of, row_of,
    before=lambda i: None, after=lambda i: None,
):
    row = sub % LAT

    def body(i, odd, carry):
        before(i)
        coupling, energy = carry
        x_speed, y_speed = speeds_of(table_ref, stretch, i)
        read = [spectrum_reader(spectrum_ref, i + QUAD * q, (odd + q) % 2, level) for q in range(4)]
        lon_halo = lon_of(i)
        for jp in range(PAIRS):
            all_of = None
            for q, (north, east) in enumerate(QUADRANTS):
                spectrum = read[q](jp)
                mu = value_of(i, q, jp)
                turned = pltpu.roll(mu, LON - 1 if east else 1, axis=1)
                along = jnp.where(lane == (LON - 1 if east else 0), lon_halo(q, jp), turned)
                shifted = pltpu.roll(mu, 7 if north else 1, axis=0)
                across = jnp.where(row == (LAT - 1 if north else 0), row_of(i, q, jp), shifted)
                change = x_speed[q % 2] * (along - mu) + y_speed[q % 2] * (across - mu)
                nu = mu + speed_of(table_ref, jp) * change
                dst_ref[direction_rows(i, q, jp), :] = nu
                coupling = coupling + spectrum * nu
                all_of = spectrum if all_of is None else all_of + spectrum
            energy = energy + weights(table_ref, jp) * all_of
        after(i)
        return coupling, energy

    coupling, energy = over_directions(body, (jnp.zeros((8, LON), F32), jnp.zeros((8, LON), F32)))
    return both_halves(coupling), both_halves(energy)


def stretch_of(where_ref, table_ref):
    return table_ref[pl.ds(pl.multiple_of(STRETCH0 + 8 * where_ref[0], 8), 8), :]


def set_weighted(table_ref, field, dst_ref):
    for jp in range(PAIRS):
        dst_ref[tab(jp), :] = weights(table_ref, jp) * field


def rate_of(beta_ref, k, jp, upper):
    return jnp.where(upper, beta_ref[2 * jp + 1, k], beta_ref[2 * jp, k])


def edge_gains(
    spectrum_ref, level, table_ref, stretch, lon_east_ref, lon_west_ref, north_ref, south_ref,
    sub, lane, extra_of, keep,
):
    row = sub % LAT

    def body(i, odd, coupling):
        x_speed, y_speed = speeds_of(table_ref, stretch, i)
        read = [spectrum_reader(spectrum_ref, i + QUAD * q, (odd + q) % 2, level) for q in range(4)]
        edge = turned_edges(lon_east_ref, lon_west_ref, i, lane)
        extra = [extra_of(q, x_speed[q % 2], y_speed[q % 2]) for q in range(4)]
        for jp in range(PAIRS):
            for q, (north, east) in enumerate(QUADRANTS):
                along = jnp.where(lane == (LON - 1 if east else 0), edge(q, jp), 0.0)
                halo = row_halo_of(north_ref, south_ref, i, q, jp)
                across = jnp.where(row == (LAT - 1 if north else 0), halo, 0.0)
                gain = speed_of(table_ref, jp) * (x_speed[q % 2] * along + y_speed[q % 2] * across)
                gain = keep(direction_rows(i, q, jp), jp, gain, extra[q])
                coupling = coupling + read[q](jp) * gain
        return coupling

    return both_halves(over_directions(body, jnp.zeros((8, LON), F32)))


def three_parts(x):
    parts = []
    for _ in range(3):
        part = x.astype(jnp.bfloat16)
        parts.append(part)
        x = x - part.astype(F32)
    return jnp.concatenate(parts, axis=0)


def sum_observations(obs_ref, sub, lane):
    listed = jnp.transpose(obs_ref[...])
    column = lax.broadcasted_iota(jnp.int32, (128, 128), 0).astype(F32)
    row8 = (sub % LAT).astype(F32)

    def slots(tile):
        for i in range(CAP):
            index = listed[8 * tile + i : 8 * tile + i + 1, :]
            value = listed[8 * tile + CAP + i : 8 * tile + CAP + i + 1, :]
            row = jnp.floor(index * (1.0 / LON))
            yield row, index - row * LON, value

    def spread(tile, takes):
        left, right = [], []
        for row, col, value in slots(tile):
            left.append(jnp.where(takes(row), value, jnp.zeros((8, LON), F32)))
            right.append(jnp.where(column == col, 1.0, 0.0).astype(jnp.bfloat16))
        parts = three_parts(jnp.concatenate(left, axis=1))
        out = lax.dot_general(
            parts, jnp.concatenate(right, axis=1), (((1,), (1,)), ((), ())), preferred_element_type=F32
        )
        return out[0:8, :] + out[8:16, :] + out[16:24, :]

    def line(tile, at):
        total = jnp.zeros((8, LON), F32)
        for row, col, value in slots(tile):
            total = total + jnp.where((row8 == row) & (col == at), value, 0.0)
        return jnp.sum(total, axis=1, keepdims=True)

    own = spread(0, lambda row: row8 == row)
    north = spread(1, lambda row: row8 * 0.0 == row)
    south = spread(2, lambda row: row8 * 0.0 + (LAT - 1.0) == row)
    return own, north, south, line(3, 0.0), line(4, LON - 1.0)


def middle_kernel(
    where_ref, beta_hbm, nu_hbm, spectrum_ref, table_ref, sea8_ref, ice_ref, field_ref,
    coupling_ref, energy_ref, obs_ref, on_in, off_in, lon_east_ref, lon_west_ref,
    mu_ref, on_ref, off_ref,
    beta_ref, nu_ref, north_ref, south_ref, fields_ref, add_ref, sems,
):
    copies = fetch(sems, (beta_hbm, beta_ref), (nu_hbm, nu_ref))
    par = where_ref[0] % 2
    sub, lane = iotas()
    row = sub % LAT
    sea8 = sea8_ref[...]
    stretch = stretch_of(where_ref, table_ref)
    force, force_n, force_s, force_e, force_w = sum_observations(obs_ref, sub, lane)
    spread_rows(par, on_in, off_in, north_ref, south_ref, fields_ref)

    own = force * field_ref[...]
    set_weighted(table_ref, own, add_ref)
    first_weight = table_ref[WEIGHT0 : WEIGHT0 + 1, :]
    along_of, across_of = {}, {}
    for east, halo, ref in ((True, force_e, lon_east_ref), (False, force_w, lon_west_ref)):
        beside = halo * ref[32:40, :]
        turned = pltpu.roll(own, LON - 1 if east else 1, axis=1)
        here = jnp.where(lane == (LON - 1 if east else 0), beside, turned)
        along_of[east] = first_weight * (here - own)
    for north, halo, place in ((True, force_n, 0), (False, force_s, 8)):
        beside = halo * fields_ref[place : place + 8, :]
        shifted = pltpu.roll(own, 7 if north else 1, axis=0)
        here = jnp.where(row == (LAT - 1 if north else 0), beside, shifted)
        across_of[north] = first_weight * (here - own)

    def extra_of(q, x_speed, y_speed):
        north, east = QUADRANTS[q]
        return x_speed * along_of[east] + y_speed * across_of[north]

    def keep(place, jp, gain, extra):
        gain = gain + (add_ref[tab(jp), :] + extra)
        mu_ref[place, :] = gain
        return gain

    gained = edge_gains(
        spectrum_ref, 1, table_ref, stretch, lon_east_ref, lon_west_ref, north_ref, south_ref,
        sub, lane, extra_of, keep,
    )
    coupling = coupling_ref[...] + gained
    energy = energy_ref[...]
    upper = sub >= LAT
    ice = ice_ref[...].astype(F32)
    rate = sea8 * (1.0 - jnp.concatenate([ice, ice], axis=0))
    base = sea8 - 0.2 * rate * energy
    set_weighted(table_ref, 0.2 * rate * coupling, add_ref)
    for copy in copies:
        copy.wait()

    def source(i, carry):
        for jp in range(PAIRS):
            for q in range(4):
                beta = rate_of(beta_ref, i + QUAD * q, jp, upper)
                place = direction_rows(i, q, jp)
                x = (nu_ref[place, :] + mu_ref[place, :]) * (base + rate * beta)
                mu_ref[place, :] = x - add_ref[tab(jp), :]
        return carry

    lax.fori_loop(0, QUAD, source, 0)
    send_rows(par, mu_ref, on_ref, off_ref)


def pack_kernel(mu_ref, west_ref, east_ref):
    _, lane = iotas()
    west_ref[...] = jnp.zeros_like(west_ref)
    east_ref[...] = jnp.zeros_like(east_ref)

    def pack(i, carry):
        pack_edges(west_ref, east_ref, i, lambda q, jp: mu_ref[direction_rows(i, q, jp), :], lane)
        return carry

    lax.fori_loop(0, QUAD, pack, 0)


def first_inner_kernel(
    where_ref, adj_hbm, spectrum_ref, table_ref, sea8_ref, nu_hbm, coupling_ref, energy_ref,
    adj_ref, nu_ref, adj_sems, nu_sems,
):
    over_pieces(adj_hbm, adj_ref, adj_sems, lambda copy: copy.start())
    sub, lane = iotas()
    sea8 = sea8_ref[...]

    def before(i):
        for copy in piecewise(adj_hbm, adj_ref, adj_sems, i):
            copy.wait()

    def after(i):
        for copy in piecewise(nu_ref, nu_hbm, nu_sems, i):
            copy.start()

    coupling_ref[...], energy_ref[...] = move(
        nu_ref, spectrum_ref, 1, table_ref, stretch_of(where_ref, table_ref), sub, lane,
        lambda i, q, jp: adj_ref[direction_rows(i, q, jp), :] * sea8,
        lambda i: lambda q, jp: 0.0, lambda i, q, jp: 0.0, before, after,
    )
    over_pieces(nu_ref, nu_hbm, nu_sems, lambda copy: copy.wait())


def inner_kernel(where_ref, mu_ref, spectrum_ref, table_ref, nu_ref, coupling_ref, energy_ref):
    sub, lane = iotas()
    coupling_ref[...], energy_ref[...] = move(
        nu_ref, spectrum_ref, 0, table_ref, stretch_of(where_ref, table_ref), sub, lane,
        lambda i, q, jp: mu_ref[direction_rows(i, q, jp), :],
        lambda i: lambda q, jp: 0.0, lambda i, q, jp: 0.0,
    )


def last_kernel(
    where_ref, beta_hbm, nu_ref, spectrum_ref, table_ref, ice_ref, coupling_ref, energy_ref,
    on_in, off_in, lon_east_ref, lon_west_ref,
    out_hbm,
    beta_ref, north_ref, south_ref, add_ref, gain_ref, sems, out_sems,
):
    copies = fetch(sems, (beta_hbm, beta_ref))
    par = where_ref[0] % 2
    sub, lane = iotas()
    row = sub % LAT
    spread_rows(par, on_in, off_in, north_ref, south_ref)
    stretch = stretch_of(where_ref, table_ref)

    def keep(place, jp, gain, extra):
        gain_ref[place, :] = gain
        return gain

    gained = edge_gains(
        spectrum_ref, 0, table_ref, stretch, lon_east_ref, lon_west_ref, north_ref, south_ref,
        sub, lane, lambda q, x_speed, y_speed: None, keep,
    )
    coupling = coupling_ref[...] + gained
    upper = sub >= LAT
    ice = ice_ref[...].astype(F32)
    rate = 1.0 - jnp.concatenate([ice, ice], axis=0)
    base = 1.0 - 0.2 * rate * energy_ref[...]
    set_weighted(table_ref, 0.2 * rate * coupling, add_ref)
    copies[0].wait()

    def chunk(g):
        rows = pl.ds(pl.multiple_of(g * 4 * BLOCK, 8), 4 * BLOCK)
        return pltpu.make_async_copy(gain_ref.at[rows], out_hbm.at[rows], out_sems.at[g])

    def body(g, carry):
        for jp in range(PAIRS):
            for h in range(4):
                beta = rate_of(beta_ref, 4 * g + h, jp, upper)
                place = pl.ds(pl.multiple_of((4 * g + h) * BLOCK + 8 * jp, 8), 8)
                x = (nu_ref[place, :] + gain_ref[place, :]) * (base + rate * beta)
                gain_ref[place, :] = x - add_ref[tab(jp), :]
        chunk(g).start()
        return carry

    lax.fori_loop(0, NDIR // 4, body, 0)
    for g in range(NDIR // 4):
        chunk(g).wait()


FIRST = 54


def params(limit=24):
    return pltpu.CompilerParams(vmem_limit_bytes=limit * MIB)


def f32(*shape):
    return jax.ShapeDtypeStruct(shape, F32)


def exchange(on, off, west, east):
    n_lon, n_lat = lax.axis_size("lon"), lax.axis_size("lat")
    near = [(i, i ^ 1) for i in range(n_lat)]
    far = [(i, ((i + 1) ^ 1) - 1) for i in range(1, n_lat - 1)]
    off = lax.ppermute(off, "lat", far)
    on = lax.ppermute(on, "lat", near)
    from_east = lax.ppermute(west, "lon", [(i, (i - 1) % n_lon) for i in range(n_lon)])
    from_west = lax.ppermute(east, "lon", [(i, (i + 1) % n_lon) for i in range(n_lon)])
    return on, off, from_east, from_west


def on_device(adj_final, saved, beta, sea_mask, ice_mask, obs_count, obs_cell, obs_value):
    table = jnp.asarray(constant_table())
    where = lax.axis_index("lat").astype(jnp.int32).reshape(1)
    adj = adj_final.reshape(ROWS, LON)
    saved = saved.reshape((STEPS + 1) * ROWS, LON)
    beta = beta.T
    tiles = lambda rows: pltpu.VMEM((rows, LON), F32)
    whole = lambda x: pltpu.VMEM(x.shape, x.dtype)
    level = pltpu.VMEM((ROWS, LON), jnp.bfloat16)
    payload = (f32(HALO, LON), f32(HALO, LON), f32(EDGE, LON), f32(EDGE, LON))
    dma = lambda *n: pltpu.SemaphoreType.DMA(n)

    on, off, west, east, obs, field, sea8, early = pl.pallas_call(
        start_kernel,
        out_shape=payload
        + (f32(128, 128), tiles(8), tiles(8))
        + (pltpu.VMEM((2 * ROWS, LON), jnp.bfloat16),),
        in_specs=[SMEM] + [HBM] * 7,
        out_specs=(VMEM,) * 8,
        scratch_shapes=[
            tiles(ROWS), level, tiles(BLOCK), whole(sea_mask), whole(obs_count), whole(obs_cell), whole(obs_value), dma(9),
            dma(QUAD, 4),
        ],
        compiler_params=params(FIRST),
        name="edges_and_observations",
    )(where, adj, saved, table, sea_mask, obs_count, obs_cell, obs_value)

    on, off, from_east, from_west = exchange(on, off, west, east)
    obs = lax.all_to_all(obs.reshape(128, 1, 128), ("lon", "lat"), split_axis=0, concat_axis=0, tiled=True)
    obs = obs.reshape(128, 128)

    rates = pltpu.SMEM(beta.shape, F32)

    hint = pl.CostEstimate(flops=20_000_000, bytes_accessed=6_000_000, transcendentals=0)
    nu, coupling, energy = pl.pallas_call(
        first_inner_kernel,
        out_shape=(pltpu.HBM((ROWS, LON), F32), tiles(8), tiles(8)),
        in_specs=[SMEM, HBM] + [VMEM] * 3,
        out_specs=(HBM, VMEM, VMEM),
        scratch_shapes=[tiles(ROWS), tiles(ROWS), dma(QUAD, 4), dma(QUAD, 4)],
        compiler_params=params(),
        cost_estimate=hint,
        name="first_step_inside",
    )(where, pltpu.with_memory_space_constraint(adj, pltpu.HBM), early, table, sea8)
    mu, on, off = pl.pallas_call(
        middle_kernel,
        out_shape=(f32(ROWS, LON),) + payload[:2],
        in_specs=[SMEM, HBM, HBM] + [VMEM] * 12,
        out_specs=(VMEM,) * 3,
        scratch_shapes=[rates, tiles(ROWS), tiles(SPREAD), tiles(SPREAD), tiles(16), tiles(BLOCK), dma(2)],
        compiler_params=params(),
        name="first_step_edges",
    )(
        where, beta, pltpu.with_memory_space_constraint(nu, pltpu.HBM), early, table, sea8, ice_mask, field, coupling, energy, obs, on, off,
        from_east, from_west,
    )

    west, east = pl.pallas_call(
        pack_kernel,
        out_shape=payload[2:],
        in_specs=[VMEM],
        out_specs=(VMEM,) * 2,
        compiler_params=params(),
        cost_estimate=pl.CostEstimate(flops=3_000_000, bytes_accessed=2_200_000, transcendentals=0),
        name="edges_of_first_step",
    )(mu)
    on, off, from_east, from_west = exchange(on, off, west, east)

    nu, coupling, energy = pl.pallas_call(
        inner_kernel,
        out_shape=(f32(ROWS, LON), f32(8, LON), f32(8, LON)),
        in_specs=[SMEM] + [VMEM] * 3,
        out_specs=(VMEM,) * 3,
        compiler_params=params(),
        cost_estimate=hint,
        name="last_step_inside",
    )(where, mu, early, table)
    out = pl.pallas_call(
        last_kernel,
        out_shape=f32(ROWS, LON),
        in_specs=[SMEM, HBM] + [VMEM] * 10,
        out_specs=HBM,
        scratch_shapes=[rates, tiles(SPREAD), tiles(SPREAD), tiles(BLOCK), tiles(ROWS), dma(1), dma(NDIR // 4)],
        compiler_params=params(),
        name="last_step_edges",
    )(where, beta, nu, early, table, ice_mask, coupling, energy, on, off, from_east, from_west)
    return out.reshape(adj_final.shape)


def solution(mesh):
    return jax.shard_map(
        on_device,
        mesh=mesh,
        in_specs=(
            P(None, None, "lat", "lon"),
            P(None, None, None, "lat", "lon"),
            P(),
            P("lat", "lon"),
            P("lat", "lon"),
            P(("lon", "lat"), None),
            P(("lon", "lat"), None),
            P(("lon", "lat"), None),
        ),
        out_specs=P(None, None, "lat", "lon"),
        check_vma=False,
    )
```

```python
import math

import jax
import jax.numpy as jnp
import numpy as np
from jax import lax
from jax.experimental import pallas as pl
from jax.experimental.pallas import tpu as pltpu
from jax.sharding import PartitionSpec as P

STEPS = 2
CAP = 4
NDIR = 36
NFREQ = 30
QUAD = NDIR // 4
PAIRS = NFREQ // 2
LAT = 4
LON = 128
BLOCK = NFREQ * LAT
ROWS = NDIR * BLOCK
HALO = 552
SOUTH0 = 536
EDGE = 40
SPREAD = 2208
N_LAT = 16
N_LON = 8
MIB = 2**20
F32 = jnp.float32

HBM = pl.BlockSpec(memory_space=pltpu.HBM)
VMEM = pl.BlockSpec(memory_space=pltpu.VMEM)
SMEM = pl.BlockSpec(memory_space=pltpu.SMEM)

QUADRANTS = ((True, True), (True, False), (False, False), (False, True))

BOTH_WAYS = ((0, 1), (3, 2))

WEIGHT0 = 0
SPEED0 = BLOCK
COS0 = 2 * BLOCK
SIN0 = COS0 + 8 * QUAD
STRETCH0 = SIN0 + 8 * QUAD


def constant_table():
    angle = (np.arange(QUAD) + 0.5) * (2.0 * math.pi / NDIR)
    j = np.arange(NFREQ)
    speed = 1.1 ** (-j.astype(np.float64))
    growth = 1.1 ** j.astype(np.float64)
    weight = growth / (NDIR * growth.sum())
    rows = np.arange(N_LAT * LAT)
    latitude = (rows + 0.5 - N_LAT * LAT / 2.0) * (100.0 / (N_LAT * LAT))
    stretch = math.cos(50.0 * math.pi / 180.0) / np.cos(latitude * (math.pi / 180.0))
    stretch = np.tile(stretch.reshape(N_LAT, 1, LAT), (1, 2, 1)).reshape(-1)
    column = np.concatenate(
        [
            np.repeat(weight, LAT),
            np.repeat(speed, LAT),
            np.repeat(np.cos(angle), 8),
            np.repeat(np.sin(angle), 8),
            stretch,
        ]
    )
    return np.tile(column[:, None], (1, LON)).astype(np.float32)


def iotas():
    sub = lax.broadcasted_iota(jnp.int32, (8, LON), 0)
    lane = lax.broadcasted_iota(jnp.int32, (8, LON), 1)
    return sub, lane


def tab(jp):
    return slice(8 * jp, 8 * jp + 8)


def weights(table_ref, jp):
    return table_ref[WEIGHT0 + 8 * jp : WEIGHT0 + 8 * jp + 8, :]


def edge_block(quadrant, jp):
    first = 8 * (2 * (quadrant // 2) + jp // 8)
    return slice(first, first + 8)


def over_directions(body, carry):
    def two(v, carry):
        return body(2 * v + 1, 1, body(2 * v, 0, carry))

    carry = lax.fori_loop(0, QUAD // 2, two, carry)
    return body(QUAD - 1, (QUAD - 1) % 2, carry)


def spectrum_reader(ref, k, odd, level=0):
    first = level * ROWS + k * BLOCK - (8 if odd else 0)
    held = {}

    def read(jp):
        place, part = divmod(jp + odd, 2)
        if place not in held:
            held.clear()
            rows = pl.ds(pl.multiple_of(first + 16 * place, 16), 16)
            held[place] = ref[rows, :].astype(F32)
        return held[place][8 * part : 8 * part + 8, :]

    return read


def direction_rows(i, quadrant, jp=0, count=8):
    return pl.ds(pl.multiple_of((i + QUAD * quadrant) * BLOCK + 8 * jp, 8), count)


def piecewise(src, dst, sems, i):
    return [
        pltpu.make_async_copy(
            src.at[direction_rows(i, q, 0, BLOCK)], dst.at[direction_rows(i, q, 0, BLOCK)], sems.at[i, q]
        )
        for q in range(4)
    ]


def over_pieces(src, dst, sems, act):
    def body(i, carry):
        for copy in piecewise(src, dst, sems, i):
            act(copy)
        return carry

    lax.fori_loop(0, QUAD, body, 0)


def extract_rows(src, r, first, dst, scale):
    def body(m, carry):
        for u in range(4):
            start = (first + 8 * (4 * m + u)) * LAT + r
            value = src[pl.ds(start, 8, stride=LAT), :]
            if scale is not None:
                value = value * scale
            dst[pl.ds(pl.multiple_of(8 * (4 * m + u), 8), 8), :] = value
        return carry

    lax.fori_loop(0, 17, body, 0)


def send_rows(par, src, on_ref, off_ref, field=None, scale8=None):
    def put(dst, r, first):
        extract_rows(src, r, first, dst, None if scale8 is None else scale8[r : r + 1, :])
        if field is not None:
            dst[pl.ds(544, 8), :] = jnp.broadcast_to(field[r : r + 1, :], (8, LON))

    @pl.when(par == 0)
    def _():
        put(on_ref, LAT - 1, SOUTH0)
        put(off_ref, 0, 0)

    @pl.when(par == 1)
    def _():
        put(on_ref, 0, 0)
        put(off_ref, LAT - 1, SOUTH0)


def spread_rows(par, on_ref, off_ref, north_ref, south_ref, field_ref=None):
    def spread(src, dst, r):
        def body(m, carry):
            for u in range(4):
                first = 8 * (4 * m + u)
                dst[pl.ds(first * LAT + r, 8, stride=LAT), :] = src[pl.ds(pl.multiple_of(first, 8), 8), :]
            return carry

        lax.fori_loop(0, 17, body, 0)

    for parity, (north, south) in enumerate(((on_ref, off_ref), (off_ref, on_ref))):

        @pl.when(par == parity)
        def _():
            spread(north, north_ref, LAT - 1)
            spread(south, south_ref, 0)
            if field_ref is not None:
                field_ref[0:8, :] = north[544:552, :]
                field_ref[8:16, :] = south[544:552, :]


def pack_edges(west_ref, east_ref, i, value_of, lane):
    relative = lane - 8 * i
    here = (relative >= 0) & (relative < 8)
    for lo, hi in ((0, 8), (8, PAIRS)):
        blocks = [None] * 4
        for jp in range(lo, hi):
            c = jp - lo
            for eastward, westward in BOTH_WAYS:
                ends = jnp.where(lane == LON - 1, value_of(westward, jp), value_of(eastward, jp))
                ends = pltpu.roll(ends, c, axis=1) if c else ends
                for q, at in ((eastward, c), (westward, (c - 1) % LON)):
                    blocks[q] = jnp.where(lane == at, ends, blocks[q]) if c else ends
        for q, (_, east) in enumerate(QUADRANTS):
            ref = west_ref if east else east_ref
            place = edge_block(q, lo)
            moved = pltpu.roll(blocks[q], 8 * i + (0 if east else 1), axis=1)
            ref[place, :] = jnp.where(here, moved, ref[place, :])


def pick_observations(count, cell, value, out_ref):
    sub = lax.broadcasted_iota(jnp.int32, (128, 128), 0)
    lane = lax.broadcasted_iota(jnp.int32, (128, 128), 1)
    counts = jnp.broadcast_to(count.astype(F32), (128, 128))
    starts = jnp.sum(jnp.where(lane < sub, counts, 0.0), axis=1, keepdims=True)
    mine = jnp.sum(jnp.where(lane == sub, counts, 0.0), axis=1, keepdims=True)
    local = (((cell >> 10) & (LAT - 1)) * LON + (cell & (LON - 1))).astype(F32)
    slots = cell.shape[1]
    slot = lax.broadcasted_iota(jnp.int32, (128, slots), 1).astype(F32)
    listed = jnp.zeros((128, 128), F32)
    for i in range(CAP):
        hit = slot == starts + float(i)
        index_i = jnp.sum(jnp.where(hit, local, 0.0), axis=1, keepdims=True)
        value_i = jnp.sum(jnp.where(hit, value, 0.0), axis=1, keepdims=True)
        value_i = jnp.where(mine > float(i), value_i, 0.0)
        listed = jnp.where(lane == i, index_i, listed)
        listed = jnp.where(lane == CAP + i, value_i, listed)
    out = listed
    for place, shift in enumerate((127, 1, 128 - N_LAT, N_LAT)):
        moved = pltpu.roll(listed, shift, axis=0)
        out = out + pltpu.roll(moved, 8 * (place + 1), axis=1)
    out_ref[...] = out


def fetch(sems, *pairs, ahead=None):
    copies = [pltpu.make_async_copy(src, dst, sems.at[n]) for n, (src, dst) in enumerate(pairs)]
    for n, copy in enumerate(copies):
        if n == 5 and ahead is not None:
            ahead()
        copy.start()
    return copies


def start_kernel(
    where_ref, adj_hbm, saved_hbm, table_hbm, sea_hbm, count_hbm, cell_hbm, value_hbm,
    on_ref, off_ref, west_ref, east_ref, obs_ref, field_ref, sea8_ref, early_ref,
    adj_ref, final_ref, table_ref, sea_ref, count_ref, cell_ref, value_ref, sems, adj_sems,
):
    half = ROWS // 2
    final0 = STEPS * ROWS
    copies = fetch(
        sems,
        (count_hbm, count_ref),
        (cell_hbm, cell_ref),
        (value_hbm, value_ref),
        (sea_hbm, sea_ref),
        (table_hbm.at[pl.ds(0, BLOCK)], table_ref),
        (saved_hbm.at[pl.ds(final0, half)], final_ref.at[pl.ds(0, half)]),
        (saved_hbm.at[pl.ds(final0 + half, half)], final_ref.at[pl.ds(half, half)]),
        (saved_hbm.at[pl.ds(ROWS, ROWS)], early_ref.at[pl.ds(ROWS, ROWS)]),
        (saved_hbm.at[pl.ds(0, ROWS)], early_ref.at[pl.ds(0, ROWS)]),
        ahead=lambda: over_pieces(adj_hbm, adj_ref, adj_sems, lambda copy: copy.start()),
    )
    par = where_ref[0] % 2
    sub, lane = iotas()
    for copy in copies[:3]:
        copy.wait()
    pick_observations(count_ref[...], cell_ref[...], value_ref[...], obs_ref)
    for copy in copies[3:5]:
        copy.wait()
    sea = sea_ref[...].astype(F32)
    sea8 = jnp.concatenate([sea, sea], axis=0)
    sea8_ref[...] = sea8
    west_ref[...] = jnp.zeros_like(west_ref)
    east_ref[...] = jnp.zeros_like(east_ref)

    def pack(i, carry):
        for copy in piecewise(adj_hbm, adj_ref, adj_sems, i):
            copy.wait()
        pack_edges(west_ref, east_ref, i, lambda q, jp: adj_ref[direction_rows(i, q, jp), :], lane)
        return carry

    lax.fori_loop(0, QUAD, pack, 0)
    for copy in copies[5:7]:
        copy.wait()

    def moment(i, odd, total):
        read = [spectrum_reader(final_ref, i + QUAD * q, (odd + q) % 2) for q in range(4)]
        for jp in range(PAIRS):
            both = (read[0](jp) + read[1](jp)) + (read[2](jp) + read[3](jp))
            total = total + weights(table_ref, jp) * both
        return total

    total = over_directions(moment, jnp.zeros((8, LON), F32))
    field = sea8 * 2.0 / jnp.sqrt(both_halves(total))
    field_ref[...] = field
    send_rows(par, adj_ref, on_ref, off_ref, field_ref, sea8_ref)
    west_sea = jnp.broadcast_to(sea8[:, :1], (8, LON))
    east_sea = jnp.broadcast_to(sea8[:, LON - 1 :], (8, LON))
    for block in range(4):
        west_ref[tab(block), :] = west_ref[tab(block), :] * west_sea
        east_ref[tab(block), :] = east_ref[tab(block), :] * east_sea
    west_ref[32:40, :] = jnp.broadcast_to(field[:, :1], (8, LON))
    east_ref[32:40, :] = jnp.broadcast_to(field[:, LON - 1 :], (8, LON))
    for copy in copies[7:]:
        copy.wait()


def speeds_of(table_ref, stretch, i):
    cos_i = table_ref[pl.ds(pl.multiple_of(COS0 + 8 * i, 8), 8), :]
    sin_i = table_ref[pl.ds(pl.multiple_of(SIN0 + 8 * i, 8), 8), :]
    stretched = 0.7 * stretch
    return (cos_i * stretched, sin_i * stretched), (0.6 * sin_i, 0.6 * cos_i)


def turned_edges(lon_east_ref, lon_west_ref, i, lane):
    turned = {}
    for q, (_, east) in enumerate(QUADRANTS):
        for lo in (0, 8):
            ref = lon_east_ref if east else lon_west_ref
            turn = (LON - 8 * i + (0 if east else 1)) % LON
            turned[q, lo] = pltpu.roll(ref[edge_block(q, lo), :], turn, axis=1)
    held = {}

    def edge(q, jp):
        pair = q // 2
        if held.get(pair, (None, None))[0] != jp:
            eastward, westward = BOTH_WAYS[pair]
            lo, c = 8 * (jp // 8), jp % 8
            ends = jnp.where(lane == c + 1, turned[westward, lo], turned[eastward, lo])
            held[pair] = (jp, pltpu.roll(ends, LON - 1 - c, axis=1))
        return held[pair][1]

    return edge


def row_halo_of(north_ref, south_ref, i, q, jp):
    if QUADRANTS[q][0]:
        return north_ref[direction_rows(i, q, jp), :]
    row = (i + QUAD * q - NDIR // 2) * BLOCK + 8 * jp + 16
    return south_ref[pl.ds(pl.multiple_of(row, 8), 8), :]


def both_halves(total):
    return total + pltpu.roll(total, 4, axis=0)


def speed_of(table_ref, jp):
    return table_ref[SPEED0 + 8 * jp : SPEED0 + 8 * jp + 8, :]


def move(
    dst_ref, spectrum_ref, level, table_ref, stretch, sub, lane, value_of, lon_of, row_of,
    before=lambda i: None, after=lambda i: None,
):
    row = sub % LAT

    def body(i, odd, carry):
        before(i)
        coupling, energy = carry
        x_speed, y_speed = speeds_of(table_ref, stretch, i)
        read = [spectrum_reader(spectrum_ref, i + QUAD * q, (odd + q) % 2, level) for q in range(4)]
        lon_halo = lon_of(i)
        for jp in range(PAIRS):
            all_of = None
            for q, (north, east) in enumerate(QUADRANTS):
                spectrum = read[q](jp)
                mu = value_of(i, q, jp)
                turned = pltpu.roll(mu, LON - 1 if east else 1, axis=1)
                along = jnp.where(lane == (LON - 1 if east else 0), lon_halo(q, jp), turned)
                shifted = pltpu.roll(mu, 7 if north else 1, axis=0)
                across = jnp.where(row == (LAT - 1 if north else 0), row_of(i, q, jp), shifted)
                change = x_speed[q % 2] * (along - mu) + y_speed[q % 2] * (across - mu)
                nu = mu + speed_of(table_ref, jp) * change
                dst_ref[direction_rows(i, q, jp), :] = nu
                coupling = coupling + spectrum * nu
                all_of = spectrum if all_of is None else all_of + spectrum
            energy = energy + weights(table_ref, jp) * all_of
        after(i)
        return coupling, energy

    coupling, energy = over_directions(body, (jnp.zeros((8, LON), F32), jnp.zeros((8, LON), F32)))
    return both_halves(coupling), both_halves(energy)


def stretch_of(where_ref, table_ref):
    return table_ref[pl.ds(pl.multiple_of(STRETCH0 + 8 * where_ref[0], 8), 8), :]


def set_weighted(table_ref, field, dst_ref):
    for jp in range(PAIRS):
        dst_ref[tab(jp), :] = weights(table_ref, jp) * field


def rate_of(beta_ref, k, jp, upper):
    return jnp.where(upper, beta_ref[2 * jp + 1, k], beta_ref[2 * jp, k])


def edge_gains(
    spectrum_ref, level, table_ref, stretch, lon_east_ref, lon_west_ref, north_ref, south_ref,
    sub, lane, extra_of, keep,
):
    row = sub % LAT

    def body(i, odd, coupling):
        x_speed, y_speed = speeds_of(table_ref, stretch, i)
        read = [spectrum_reader(spectrum_ref, i + QUAD * q, (odd + q) % 2, level) for q in range(4)]
        edge = turned_edges(lon_east_ref, lon_west_ref, i, lane)
        extra = [extra_of(q, x_speed[q % 2], y_speed[q % 2]) for q in range(4)]
        for jp in range(PAIRS):
            for q, (north, east) in enumerate(QUADRANTS):
                along = jnp.where(lane == (LON - 1 if east else 0), edge(q, jp), 0.0)
                halo = row_halo_of(north_ref, south_ref, i, q, jp)
                across = jnp.where(row == (LAT - 1 if north else 0), halo, 0.0)
                gain = speed_of(table_ref, jp) * (x_speed[q % 2] * along + y_speed[q % 2] * across)
                gain = keep(direction_rows(i, q, jp), jp, gain, extra[q])
                coupling = coupling + read[q](jp) * gain
        return coupling

    return both_halves(over_directions(body, jnp.zeros((8, LON), F32)))


def three_parts(x):
    parts = []
    for _ in range(3):
        part = x.astype(jnp.bfloat16)
        parts.append(part)
        x = x - part.astype(F32)
    return jnp.concatenate(parts, axis=0)


def sum_observations(obs_ref, sub, lane):
    listed = jnp.transpose(obs_ref[...])
    column = lax.broadcasted_iota(jnp.int32, (128, 128), 0).astype(F32)
    row8 = (sub % LAT).astype(F32)

    def slots(tile):
        for i in range(CAP):
            index = listed[8 * tile + i : 8 * tile + i + 1, :]
            value = listed[8 * tile + CAP + i : 8 * tile + CAP + i + 1, :]
            row = jnp.floor(index * (1.0 / LON))
            yield row, index - row * LON, value

    def spread(tile, takes):
        left, right = [], []
        for row, col, value in slots(tile):
            left.append(jnp.where(takes(row), value, jnp.zeros((8, LON), F32)))
            right.append(jnp.where(column == col, 1.0, 0.0).astype(jnp.bfloat16))
        parts = three_parts(jnp.concatenate(left, axis=1))
        out = lax.dot_general(
            parts, jnp.concatenate(right, axis=1), (((1,), (1,)), ((), ())), preferred_element_type=F32
        )
        return out[0:8, :] + out[8:16, :] + out[16:24, :]

    def line(tile, at):
        total = jnp.zeros((8, LON), F32)
        for row, col, value in slots(tile):
            total = total + jnp.where((row8 == row) & (col == at), value, 0.0)
        return jnp.sum(total, axis=1, keepdims=True)

    own = spread(0, lambda row: row8 == row)
    north = spread(1, lambda row: row8 * 0.0 == row)
    south = spread(2, lambda row: row8 * 0.0 + (LAT - 1.0) == row)
    return own, north, south, line(3, 0.0), line(4, LON - 1.0)


def middle_kernel(
    where_ref, beta_hbm, nu_hbm, spectrum_ref, table_ref, sea8_ref, ice_ref, field_ref,
    coupling_ref, energy_ref, obs_ref, on_in, off_in, lon_east_ref, lon_west_ref,
    mu_ref, on_ref, off_ref,
    beta_ref, nu_ref, north_ref, south_ref, fields_ref, add_ref, sems,
):
    copies = fetch(sems, (beta_hbm, beta_ref), (nu_hbm, nu_ref))
    par = where_ref[0] % 2
    sub, lane = iotas()
    row = sub % LAT
    sea8 = sea8_ref[...]
    stretch = stretch_of(where_ref, table_ref)
    force, force_n, force_s, force_e, force_w = sum_observations(obs_ref, sub, lane)
    spread_rows(par, on_in, off_in, north_ref, south_ref, fields_ref)

    own = force * field_ref[...]
    set_weighted(table_ref, own, add_ref)
    first_weight = table_ref[WEIGHT0 : WEIGHT0 + 1, :]
    along_of, across_of = {}, {}
    for east, halo, ref in ((True, force_e, lon_east_ref), (False, force_w, lon_west_ref)):
        beside = halo * ref[32:40, :]
        turned = pltpu.roll(own, LON - 1 if east else 1, axis=1)
        here = jnp.where(lane == (LON - 1 if east else 0), beside, turned)
        along_of[east] = first_weight * (here - own)
    for north, halo, place in ((True, force_n, 0), (False, force_s, 8)):
        beside = halo * fields_ref[place : place + 8, :]
        shifted = pltpu.roll(own, 7 if north else 1, axis=0)
        here = jnp.where(row == (LAT - 1 if north else 0), beside, shifted)
        across_of[north] = first_weight * (here - own)

    def extra_of(q, x_speed, y_speed):
        north, east = QUADRANTS[q]
        return x_speed * along_of[east] + y_speed * across_of[north]

    def keep(place, jp, gain, extra):
        gain = gain + (add_ref[tab(jp), :] + extra)
        mu_ref[place, :] = gain
        return gain

    gained = edge_gains(
        spectrum_ref, 1, table_ref, stretch, lon_east_ref, lon_west_ref, north_ref, south_ref,
        sub, lane, extra_of, keep,
    )
    coupling = coupling_ref[...] + gained
    energy = energy_ref[...]
    upper = sub >= LAT
    ice = ice_ref[...].astype(F32)
    rate = sea8 * (1.0 - jnp.concatenate([ice, ice], axis=0))
    base = sea8 - 0.2 * rate * energy
    set_weighted(table_ref, 0.2 * rate * coupling, add_ref)
    for copy in copies:
        copy.wait()

    def source(i, carry):
        for jp in range(PAIRS):
            for q in range(4):
                beta = rate_of(beta_ref, i + QUAD * q, jp, upper)
                place = direction_rows(i, q, jp)
                x = (nu_ref[place, :] + mu_ref[place, :]) * (base + rate * beta)
                mu_ref[place, :] = x - add_ref[tab(jp), :]
        return carry

    lax.fori_loop(0, QUAD, source, 0)
    send_rows(par, mu_ref, on_ref, off_ref)


def pack_kernel(mu_ref, west_ref, east_ref):
    _, lane = iotas()
    west_ref[...] = jnp.zeros_like(west_ref)
    east_ref[...] = jnp.zeros_like(east_ref)

    def pack(i, carry):
        pack_edges(west_ref, east_ref, i, lambda q, jp: mu_ref[direction_rows(i, q, jp), :], lane)
        return carry

    lax.fori_loop(0, QUAD, pack, 0)


def first_inner_kernel(
    where_ref, adj_hbm, spectrum_ref, table_ref, sea8_ref, nu_hbm, coupling_ref, energy_ref,
    adj_ref, nu_ref, adj_sems, nu_sems,
):
    over_pieces(adj_hbm, adj_ref, adj_sems, lambda copy: copy.start())
    sub, lane = iotas()
    sea8 = sea8_ref[...]

    def before(i):
        for copy in piecewise(adj_hbm, adj_ref, adj_sems, i):
            copy.wait()

    def after(i):
        for copy in piecewise(nu_ref, nu_hbm, nu_sems, i):
            copy.start()

    coupling_ref[...], energy_ref[...] = move(
        nu_ref, spectrum_ref, 1, table_ref, stretch_of(where_ref, table_ref), sub, lane,
        lambda i, q, jp: adj_ref[direction_rows(i, q, jp), :] * sea8,
        lambda i: lambda q, jp: 0.0, lambda i, q, jp: 0.0, before, after,
    )
    over_pieces(nu_ref, nu_hbm, nu_sems, lambda copy: copy.wait())


def inner_kernel(where_ref, mu_ref, spectrum_ref, table_ref, nu_ref, coupling_ref, energy_ref):
    sub, lane = iotas()
    coupling_ref[...], energy_ref[...] = move(
        nu_ref, spectrum_ref, 0, table_ref, stretch_of(where_ref, table_ref), sub, lane,
        lambda i, q, jp: mu_ref[direction_rows(i, q, jp), :],
        lambda i: lambda q, jp: 0.0, lambda i, q, jp: 0.0,
    )


def last_kernel(
    where_ref, beta_hbm, nu_ref, spectrum_ref, table_ref, ice_ref, coupling_ref, energy_ref,
    on_in, off_in, lon_east_ref, lon_west_ref,
    out_hbm,
    beta_ref, north_ref, south_ref, add_ref, gain_ref, sems, out_sems,
):
    copies = fetch(sems, (beta_hbm, beta_ref))
    par = where_ref[0] % 2
    sub, lane = iotas()
    row = sub % LAT
    spread_rows(par, on_in, off_in, north_ref, south_ref)
    stretch = stretch_of(where_ref, table_ref)

    def keep(place, jp, gain, extra):
        gain_ref[place, :] = gain
        return gain

    gained = edge_gains(
        spectrum_ref, 0, table_ref, stretch, lon_east_ref, lon_west_ref, north_ref, south_ref,
        sub, lane, lambda q, x_speed, y_speed: None, keep,
    )
    coupling = coupling_ref[...] + gained
    upper = sub >= LAT
    ice = ice_ref[...].astype(F32)
    rate = 1.0 - jnp.concatenate([ice, ice], axis=0)
    base = 1.0 - 0.2 * rate * energy_ref[...]
    set_weighted(table_ref, 0.2 * rate * coupling, add_ref)
    copies[0].wait()

    def chunk(g):
        rows = pl.ds(pl.multiple_of(g * 4 * BLOCK, 8), 4 * BLOCK)
        return pltpu.make_async_copy(gain_ref.at[rows], out_hbm.at[rows], out_sems.at[g])

    def body(g, carry):
        for jp in range(PAIRS):
            for h in range(4):
                beta = rate_of(beta_ref, 4 * g + h, jp, upper)
                place = pl.ds(pl.multiple_of((4 * g + h) * BLOCK + 8 * jp, 8), 8)
                x = (nu_ref[place, :] + gain_ref[place, :]) * (base + rate * beta)
                gain_ref[place, :] = x - add_ref[tab(jp), :]
        chunk(g).start()
        return carry

    lax.fori_loop(0, NDIR // 4, body, 0)
    for g in range(NDIR // 4):
        chunk(g).wait()


FIRST = 54


def params(limit=24):
    return pltpu.CompilerParams(vmem_limit_bytes=limit * MIB)


def f32(*shape):
    return jax.ShapeDtypeStruct(shape, F32)


def exchange(on, off, west, east):
    n_lon, n_lat = lax.axis_size("lon"), lax.axis_size("lat")
    near = [(i, i ^ 1) for i in range(n_lat)]
    far = [(i, ((i + 1) ^ 1) - 1) for i in range(1, n_lat - 1)]
    off = lax.ppermute(off, "lat", far)
    on = lax.ppermute(on, "lat", near)
    from_east = lax.ppermute(west, "lon", [(i, (i - 1) % n_lon) for i in range(n_lon)])
    from_west = lax.ppermute(east, "lon", [(i, (i + 1) % n_lon) for i in range(n_lon)])
    return on, off, from_east, from_west


def on_device(adj_final, saved, beta, sea_mask, ice_mask, obs_count, obs_cell, obs_value):
    table = jnp.asarray(constant_table())
    where = lax.axis_index("lat").astype(jnp.int32).reshape(1)
    adj = adj_final.reshape(ROWS, LON)
    saved = saved.reshape((STEPS + 1) * ROWS, LON)
    beta = beta.T
    tiles = lambda rows: pltpu.VMEM((rows, LON), F32)
    whole = lambda x: pltpu.VMEM(x.shape, x.dtype)
    level = pltpu.VMEM((ROWS, LON), jnp.bfloat16)
    payload = (f32(HALO, LON), f32(HALO, LON), f32(EDGE, LON), f32(EDGE, LON))
    dma = lambda *n: pltpu.SemaphoreType.DMA(n)

    on, off, west, east, obs, field, sea8, early = pl.pallas_call(
        start_kernel,
        out_shape=payload
        + (f32(128, 128), tiles(8), tiles(8))
        + (pltpu.VMEM((2 * ROWS, LON), jnp.bfloat16),),
        in_specs=[SMEM] + [HBM] * 7,
        out_specs=(VMEM,) * 8,
        scratch_shapes=[
            tiles(ROWS + 8), level, tiles(BLOCK), whole(sea_mask), whole(obs_count), whole(obs_cell), whole(obs_value), dma(9),
            dma(QUAD, 4),
        ],
        compiler_params=params(FIRST),
        name="edges_and_observations",
    )(where, adj, saved, table, sea_mask, obs_count, obs_cell, obs_value)

    on, off, from_east, from_west = exchange(on, off, west, east)
    obs = lax.all_to_all(obs.reshape(128, 1, 128), ("lon", "lat"), split_axis=0, concat_axis=0, tiled=True)
    obs = obs.reshape(128, 128)

    rates = pltpu.SMEM(beta.shape, F32)

    hint = pl.CostEstimate(flops=20_000_000, bytes_accessed=6_000_000, transcendentals=0)
    nu, coupling, energy = pl.pallas_call(
        first_inner_kernel,
        out_shape=(pltpu.HBM((ROWS, LON), F32), tiles(8), tiles(8)),
        in_specs=[SMEM, HBM] + [VMEM] * 3,
        out_specs=(HBM, VMEM, VMEM),
        scratch_shapes=[tiles(ROWS), tiles(ROWS), dma(QUAD, 4), dma(QUAD, 4)],
        compiler_params=params(),
        cost_estimate=hint,
        name="first_step_inside",
    )(where, pltpu.with_memory_space_constraint(adj, pltpu.HBM), early, table, sea8)
    mu, on, off = pl.pallas_call(
        middle_kernel,
        out_shape=(f32(ROWS + 8, LON),) + payload[:2],
        in_specs=[SMEM, HBM, HBM] + [VMEM] * 12,
        out_specs=(VMEM,) * 3,
        scratch_shapes=[rates, tiles(ROWS), tiles(SPREAD), tiles(SPREAD), tiles(16), tiles(BLOCK), dma(2)],
        compiler_params=params(),
        name="first_step_edges",
    )(
        where, beta, pltpu.with_memory_space_constraint(nu, pltpu.HBM), early, table, sea8, ice_mask, field, coupling, energy, obs, on, off,
        from_east, from_west,
    )

    west, east = pl.pallas_call(
        pack_kernel,
        out_shape=payload[2:],
        in_specs=[VMEM],
        out_specs=(VMEM,) * 2,
        compiler_params=params(),
        cost_estimate=pl.CostEstimate(flops=3_000_000, bytes_accessed=2_200_000, transcendentals=0),
        name="edges_of_first_step",
    )(mu)
    on, off, from_east, from_west = exchange(on, off, west, east)

    nu, coupling, energy = pl.pallas_call(
        inner_kernel,
        out_shape=(f32(ROWS, LON), f32(8, LON), f32(8, LON)),
        in_specs=[SMEM] + [VMEM] * 3,
        out_specs=(VMEM,) * 3,
        compiler_params=params(),
        cost_estimate=hint,
        name="last_step_inside",
    )(where, mu, early, table)
    out = pl.pallas_call(
        last_kernel,
        out_shape=f32(ROWS, LON),
        in_specs=[SMEM, HBM] + [VMEM] * 10,
        out_specs=HBM,
        scratch_shapes=[rates, tiles(SPREAD), tiles(SPREAD), tiles(BLOCK), tiles(ROWS), dma(1), dma(NDIR // 4)],
        compiler_params=params(),
        name="last_step_edges",
    )(where, beta, nu, early, table, ice_mask, coupling, energy, on, off, from_east, from_west)
    return out.reshape(adj_final.shape)


def solution(mesh):
    return jax.shard_map(
        on_device,
        mesh=mesh,
        in_specs=(
            P(None, None, "lat", "lon"),
            P(None, None, None, "lat", "lon"),
            P(),
            P("lat", "lon"),
            P("lat", "lon"),
            P(("lon", "lat"), None),
            P(("lon", "lat"), None),
            P(("lon", "lat"), None),
        ),
        out_specs=P(None, None, "lat", "lon"),
        check_vma=False,
    )
```

```python
import math

import jax
import jax.numpy as jnp
import numpy as np
from jax import lax
from jax.experimental import pallas as pl
from jax.experimental.pallas import tpu as pltpu
from jax.sharding import PartitionSpec as P

STEPS = 2
CAP = 4
NDIR = 36
NFREQ = 30
QUAD = NDIR // 4
PAIRS = NFREQ // 2
LAT = 4
LON = 128
BLOCK = NFREQ * LAT
ROWS = NDIR * BLOCK
HALO = 552
SOUTH0 = 536
EDGE = 40
SPREAD = 2208
N_LAT = 16
N_LON = 8
MIB = 2**20
F32 = jnp.float32

HBM = pl.BlockSpec(memory_space=pltpu.HBM)
VMEM = pl.BlockSpec(memory_space=pltpu.VMEM)
SMEM = pl.BlockSpec(memory_space=pltpu.SMEM)

QUADRANTS = ((True, True), (True, False), (False, False), (False, True))

BOTH_WAYS = ((0, 1), (3, 2))

WEIGHT0 = 0
SPEED0 = BLOCK
COS0 = 2 * BLOCK
SIN0 = COS0 + 8 * QUAD
STRETCH0 = SIN0 + 8 * QUAD


def constant_table():
    angle = (np.arange(QUAD) + 0.5) * (2.0 * math.pi / NDIR)
    j = np.arange(NFREQ)
    speed = 1.1 ** (-j.astype(np.float64))
    growth = 1.1 ** j.astype(np.float64)
    weight = growth / (NDIR * growth.sum())
    rows = np.arange(N_LAT * LAT)
    latitude = (rows + 0.5 - N_LAT * LAT / 2.0) * (100.0 / (N_LAT * LAT))
    stretch = math.cos(50.0 * math.pi / 180.0) / np.cos(latitude * (math.pi / 180.0))
    stretch = np.tile(stretch.reshape(N_LAT, 1, LAT), (1, 2, 1)).reshape(-1)
    column = np.concatenate(
        [
            np.repeat(weight, LAT),
            np.repeat(speed, LAT),
            np.repeat(np.cos(angle), 8),
            np.repeat(np.sin(angle), 8),
            stretch,
        ]
    )
    return np.tile(column[:, None], (1, LON)).astype(np.float32)


def iotas():
    sub = lax.broadcasted_iota(jnp.int32, (8, LON), 0)
    lane = lax.broadcasted_iota(jnp.int32, (8, LON), 1)
    return sub, lane


def tab(jp):
    return slice(8 * jp, 8 * jp + 8)


def weights(table_ref, jp):
    return table_ref[WEIGHT0 + 8 * jp : WEIGHT0 + 8 * jp + 8, :]


def edge_block(quadrant, jp):
    first = 8 * (2 * (quadrant // 2) + jp // 8)
    return slice(first, first + 8)


def over_directions(body, carry):
    def two(v, carry):
        return body(2 * v + 1, 1, body(2 * v, 0, carry))

    carry = lax.fori_loop(0, QUAD // 2, two, carry)
    return body(QUAD - 1, (QUAD - 1) % 2, carry)


def spectrum_reader(ref, k, odd, level=0):
    first = level * ROWS + k * BLOCK - (8 if odd else 0)
    held = {}

    def read(jp):
        place, part = divmod(jp + odd, 2)
        if place not in held:
            held.clear()
            rows = pl.ds(pl.multiple_of(first + 16 * place, 16), 16)
            held[place] = ref[rows, :].astype(F32)
        return held[place][8 * part : 8 * part + 8, :]

    return read


def direction_rows(i, quadrant, jp=0, count=8):
    return pl.ds(pl.multiple_of((i + QUAD * quadrant) * BLOCK + 8 * jp, 8), count)


def piecewise(src, dst, sems, i):
    return [
        pltpu.make_async_copy(
            src.at[direction_rows(i, q, 0, BLOCK)], dst.at[direction_rows(i, q, 0, BLOCK)], sems.at[i, q]
        )
        for q in range(4)
    ]


def over_pieces(src, dst, sems, act):
    def body(i, carry):
        for copy in piecewise(src, dst, sems, i):
            act(copy)
        return carry

    lax.fori_loop(0, QUAD, body, 0)


def extract_rows(src, r, first, dst, scale):
    def body(m, carry):
        for u in range(4):
            start = (first + 8 * (4 * m + u)) * LAT + r
            value = src[pl.ds(start, 8, stride=LAT), :]
            if scale is not None:
                value = value * scale
            dst[pl.ds(pl.multiple_of(8 * (4 * m + u), 8), 8), :] = value
        return carry

    lax.fori_loop(0, 17, body, 0)


def send_rows(par, src, on_ref, off_ref, field=None, scale8=None):
    def put(dst, r, first):
        extract_rows(src, r, first, dst, None if scale8 is None else scale8[r : r + 1, :])
        if field is not None:
            dst[pl.ds(544, 8), :] = jnp.broadcast_to(field[r : r + 1, :], (8, LON))

    @pl.when(par == 0)
    def _():
        put(on_ref, LAT - 1, SOUTH0)
        put(off_ref, 0, 0)

    @pl.when(par == 1)
    def _():
        put(on_ref, 0, 0)
        put(off_ref, LAT - 1, SOUTH0)


def spread_rows(par, on_ref, off_ref, north_ref, south_ref, field_ref=None):
    def spread(src, dst, r):
        def body(m, carry):
            for u in range(4):
                first = 8 * (4 * m + u)
                dst[pl.ds(first * LAT + r, 8, stride=LAT), :] = src[pl.ds(pl.multiple_of(first, 8), 8), :]
            return carry

        lax.fori_loop(0, 17, body, 0)

    for parity, (north, south) in enumerate(((on_ref, off_ref), (off_ref, on_ref))):

        @pl.when(par == parity)
        def _():
            spread(north, north_ref, LAT - 1)
            spread(south, south_ref, 0)
            if field_ref is not None:
                field_ref[0:8, :] = north[544:552, :]
                field_ref[8:16, :] = south[544:552, :]


def pack_edges(west_ref, east_ref, i, value_of, lane):
    relative = lane - 8 * i
    here = (relative >= 0) & (relative < 8)
    for lo, hi in ((0, 8), (8, PAIRS)):
        blocks = [None] * 4
        for jp in range(lo, hi):
            c = jp - lo
            for eastward, westward in BOTH_WAYS:
                ends = jnp.where(lane == LON - 1, value_of(westward, jp), value_of(eastward, jp))
                ends = pltpu.roll(ends, c, axis=1) if c else ends
                for q, at in ((eastward, c), (westward, (c - 1) % LON)):
                    blocks[q] = jnp.where(lane == at, ends, blocks[q]) if c else ends
        for q, (_, east) in enumerate(QUADRANTS):
            ref = west_ref if east else east_ref
            place = edge_block(q, lo)
            moved = pltpu.roll(blocks[q], 8 * i + (0 if east else 1), axis=1)
            ref[place, :] = jnp.where(here, moved, ref[place, :])


def pick_observations(count, cell, value, out_ref):
    sub = lax.broadcasted_iota(jnp.int32, (128, 128), 0)
    lane = lax.broadcasted_iota(jnp.int32, (128, 128), 1)
    counts = jnp.broadcast_to(count.astype(F32), (128, 128))
    starts = jnp.sum(jnp.where(lane < sub, counts, 0.0), axis=1, keepdims=True)
    mine = jnp.sum(jnp.where(lane == sub, counts, 0.0), axis=1, keepdims=True)
    local = (((cell >> 10) & (LAT - 1)) * LON + (cell & (LON - 1))).astype(F32)
    slots = cell.shape[1]
    slot = lax.broadcasted_iota(jnp.int32, (128, slots), 1).astype(F32)
    listed = jnp.zeros((128, 128), F32)
    for i in range(CAP):
        hit = slot == starts + float(i)
        index_i = jnp.sum(jnp.where(hit, local, 0.0), axis=1, keepdims=True)
        value_i = jnp.sum(jnp.where(hit, value, 0.0), axis=1, keepdims=True)
        value_i = jnp.where(mine > float(i), value_i, 0.0)
        listed = jnp.where(lane == i, index_i, listed)
        listed = jnp.where(lane == CAP + i, value_i, listed)
    out = listed
    for place, shift in enumerate((127, 1, 128 - N_LAT, N_LAT)):
        moved = pltpu.roll(listed, shift, axis=0)
        out = out + pltpu.roll(moved, 8 * (place + 1), axis=1)
    out_ref[...] = out


def fetch(sems, *pairs, ahead=None):
    copies = [pltpu.make_async_copy(src, dst, sems.at[n]) for n, (src, dst) in enumerate(pairs)]
    for n, copy in enumerate(copies):
        if n == 5 and ahead is not None:
            ahead()
        copy.start()
    return copies


def start_kernel(
    where_ref, adj_hbm, saved_hbm, table_hbm, sea_hbm, count_hbm, cell_hbm, value_hbm,
    on_ref, off_ref, west_ref, east_ref, obs_ref, field_ref, sea8_ref, early_ref,
    adj_ref, final_ref, table_ref, sea_ref, count_ref, cell_ref, value_ref, sems, adj_sems,
):
    half = ROWS // 2
    final0 = STEPS * ROWS
    copies = fetch(
        sems,
        (count_hbm, count_ref),
        (cell_hbm, cell_ref),
        (value_hbm, value_ref),
        (sea_hbm, sea_ref),
        (table_hbm.at[pl.ds(0, BLOCK)], table_ref),
        (saved_hbm.at[pl.ds(final0, half)], final_ref.at[pl.ds(0, half)]),
        (saved_hbm.at[pl.ds(final0 + half, half)], final_ref.at[pl.ds(half, half)]),
        (saved_hbm.at[pl.ds(ROWS, ROWS)], early_ref.at[pl.ds(ROWS, ROWS)]),
        (saved_hbm.at[pl.ds(0, ROWS)], early_ref.at[pl.ds(0, ROWS)]),
        ahead=lambda: over_pieces(adj_hbm, adj_ref, adj_sems, lambda copy: copy.start()),
    )
    par = where_ref[0] % 2
    sub, lane = iotas()
    for copy in copies[:3]:
        copy.wait()
    pick_observations(count_ref[...], cell_ref[...], value_ref[...], obs_ref)
    for copy in copies[3:5]:
        copy.wait()
    sea = sea_ref[...].astype(F32)
    sea8 = jnp.concatenate([sea, sea], axis=0)
    sea8_ref[...] = sea8
    west_ref[...] = jnp.zeros_like(west_ref)
    east_ref[...] = jnp.zeros_like(east_ref)

    def pack(i, carry):
        for copy in piecewise(adj_hbm, adj_ref, adj_sems, i):
            copy.wait()
        pack_edges(west_ref, east_ref, i, lambda q, jp: adj_ref[direction_rows(i, q, jp), :], lane)
        return carry

    lax.fori_loop(0, QUAD, pack, 0)
    for copy in copies[5:7]:
        copy.wait()

    def moment(i, odd, total):
        read = [spectrum_reader(final_ref, i + QUAD * q, (odd + q) % 2) for q in range(4)]
        for jp in range(PAIRS):
            both = (read[0](jp) + read[1](jp)) + (read[2](jp) + read[3](jp))
            total = total + weights(table_ref, jp) * both
        return total

    total = over_directions(moment, jnp.zeros((8, LON), F32))
    field = sea8 * 2.0 / jnp.sqrt(both_halves(total))
    field_ref[...] = field
    send_rows(par, adj_ref, on_ref, off_ref, field_ref, sea8_ref)
    west_sea = jnp.broadcast_to(sea8[:, :1], (8, LON))
    east_sea = jnp.broadcast_to(sea8[:, LON - 1 :], (8, LON))
    for block in range(4):
        west_ref[tab(block), :] = west_ref[tab(block), :] * west_sea
        east_ref[tab(block), :] = east_ref[tab(block), :] * east_sea
    west_ref[32:40, :] = jnp.broadcast_to(field[:, :1], (8, LON))
    east_ref[32:40, :] = jnp.broadcast_to(field[:, LON - 1 :], (8, LON))
    for copy in copies[7:]:
        copy.wait()


def speeds_of(table_ref, stretch, i):
    cos_i = table_ref[pl.ds(pl.multiple_of(COS0 + 8 * i, 8), 8), :]
    sin_i = table_ref[pl.ds(pl.multiple_of(SIN0 + 8 * i, 8), 8), :]
    stretched = 0.7 * stretch
    return (cos_i * stretched, sin_i * stretched), (0.6 * sin_i, 0.6 * cos_i)


def turned_edges(lon_east_ref, lon_west_ref, i, lane):
    turned = {}
    for q, (_, east) in enumerate(QUADRANTS):
        for lo in (0, 8):
            ref = lon_east_ref if east else lon_west_ref
            turn = (LON - 8 * i + (0 if east else 1)) % LON
            turned[q, lo] = pltpu.roll(ref[edge_block(q, lo), :], turn, axis=1)
    held = {}

    def edge(q, jp):
        pair = q // 2
        if held.get(pair, (None, None))[0] != jp:
            eastward, westward = BOTH_WAYS[pair]
            lo, c = 8 * (jp // 8), jp % 8
            ends = jnp.where(lane == c + 1, turned[westward, lo], turned[eastward, lo])
            held[pair] = (jp, pltpu.roll(ends, LON - 1 - c, axis=1))
        return held[pair][1]

    return edge


def row_halo_of(north_ref, south_ref, i, q, jp):
    if QUADRANTS[q][0]:
        return north_ref[direction_rows(i, q, jp), :]
    row = (i + QUAD * q - NDIR // 2) * BLOCK + 8 * jp + 16
    return south_ref[pl.ds(pl.multiple_of(row, 8), 8), :]


def both_halves(total):
    return total + pltpu.roll(total, 4, axis=0)


def speed_of(table_ref, jp):
    return table_ref[SPEED0 + 8 * jp : SPEED0 + 8 * jp + 8, :]


def move(
    dst_ref, spectrum_ref, level, table_ref, stretch, sub, lane, value_of, lon_of, row_of,
    before=lambda i: None, after=lambda i: None,
):
    row = sub % LAT

    def body(i, odd, carry):
        before(i)
        coupling, energy = carry
        x_speed, y_speed = speeds_of(table_ref, stretch, i)
        read = [spectrum_reader(spectrum_ref, i + QUAD * q, (odd + q) % 2, level) for q in range(4)]
        lon_halo = lon_of(i)
        for jp in range(PAIRS):
            all_of = None
            for q, (north, east) in enumerate(QUADRANTS):
                spectrum = read[q](jp)
                mu = value_of(i, q, jp)
                turned = pltpu.roll(mu, LON - 1 if east else 1, axis=1)
                along = jnp.where(lane == (LON - 1 if east else 0), lon_halo(q, jp), turned)
                shifted = pltpu.roll(mu, 7 if north else 1, axis=0)
                across = jnp.where(row == (LAT - 1 if north else 0), row_of(i, q, jp), shifted)
                change = x_speed[q % 2] * (along - mu) + y_speed[q % 2] * (across - mu)
                nu = mu + speed_of(table_ref, jp) * change
                dst_ref[direction_rows(i, q, jp), :] = nu
                coupling = coupling + spectrum * nu
                all_of = spectrum if all_of is None else all_of + spectrum
            energy = energy + weights(table_ref, jp) * all_of
        after(i)
        return coupling, energy

    coupling, energy = over_directions(body, (jnp.zeros((8, LON), F32), jnp.zeros((8, LON), F32)))
    return both_halves(coupling), both_halves(energy)


def stretch_of(where_ref, table_ref):
    return table_ref[pl.ds(pl.multiple_of(STRETCH0 + 8 * where_ref[0], 8), 8), :]


def set_weighted(table_ref, field, dst_ref):
    for jp in range(PAIRS):
        dst_ref[tab(jp), :] = weights(table_ref, jp) * field


def rate_of(beta_ref, k, jp, upper):
    return jnp.where(upper, beta_ref[2 * jp + 1, k], beta_ref[2 * jp, k])


def edge_gains(
    spectrum_ref, level, table_ref, stretch, lon_east_ref, lon_west_ref, north_ref, south_ref,
    sub, lane, extra_of, keep,
):
    row = sub % LAT

    def body(i, odd, coupling):
        x_speed, y_speed = speeds_of(table_ref, stretch, i)
        read = [spectrum_reader(spectrum_ref, i + QUAD * q, (odd + q) % 2, level) for q in range(4)]
        edge = turned_edges(lon_east_ref, lon_west_ref, i, lane)
        extra = [extra_of(q, x_speed[q % 2], y_speed[q % 2]) for q in range(4)]
        for jp in range(PAIRS):
            for q, (north, east) in enumerate(QUADRANTS):
                along = jnp.where(lane == (LON - 1 if east else 0), edge(q, jp), 0.0)
                halo = row_halo_of(north_ref, south_ref, i, q, jp)
                across = jnp.where(row == (LAT - 1 if north else 0), halo, 0.0)
                gain = speed_of(table_ref, jp) * (x_speed[q % 2] * along + y_speed[q % 2] * across)
                gain = keep(direction_rows(i, q, jp), jp, gain, extra[q])
                coupling = coupling + read[q](jp) * gain
        return coupling

    return both_halves(over_directions(body, jnp.zeros((8, LON), F32)))


def three_parts(x):
    parts = []
    for _ in range(3):
        part = x.astype(jnp.bfloat16)
        parts.append(part)
        x = x - part.astype(F32)
    return jnp.concatenate(parts, axis=0)


def sum_observations(obs_ref, sub, lane):
    listed = jnp.transpose(obs_ref[...])
    column = lax.broadcasted_iota(jnp.int32, (128, 128), 0).astype(F32)
    row8 = (sub % LAT).astype(F32)

    def slots(tile):
        for i in range(CAP):
            index = listed[8 * tile + i : 8 * tile + i + 1, :]
            value = listed[8 * tile + CAP + i : 8 * tile + CAP + i + 1, :]
            row = jnp.floor(index * (1.0 / LON))
            yield row, index - row * LON, value

    def spread(tile, takes):
        left, right = [], []
        for row, col, value in slots(tile):
            left.append(jnp.where(takes(row), value, jnp.zeros((8, LON), F32)))
            right.append(jnp.where(column == col, 1.0, 0.0).astype(jnp.bfloat16))
        parts = three_parts(jnp.concatenate(left, axis=1))
        out = lax.dot_general(
            parts, jnp.concatenate(right, axis=1), (((1,), (1,)), ((), ())), preferred_element_type=F32
        )
        return out[0:8, :] + out[8:16, :] + out[16:24, :]

    def line(tile, at):
        total = jnp.zeros((8, LON), F32)
        for row, col, value in slots(tile):
            total = total + jnp.where((row8 == row) & (col == at), value, 0.0)
        return jnp.sum(total, axis=1, keepdims=True)

    own = spread(0, lambda row: row8 == row)
    north = spread(1, lambda row: row8 * 0.0 == row)
    south = spread(2, lambda row: row8 * 0.0 + (LAT - 1.0) == row)
    return own, north, south, line(3, 0.0), line(4, LON - 1.0)


def middle_kernel(
    where_ref, beta_hbm, nu_hbm, spectrum_ref, table_ref, sea8_ref, ice_ref, field_ref,
    coupling_ref, energy_ref, obs_ref, on_in, off_in, lon_east_ref, lon_west_ref,
    mu_ref, on_ref, off_ref,
    beta_ref, nu_ref, north_ref, south_ref, fields_ref, add_ref, sems,
):
    copies = fetch(sems, (beta_hbm, beta_ref), (nu_hbm, nu_ref))
    par = where_ref[0] % 2
    sub, lane = iotas()
    row = sub % LAT
    sea8 = sea8_ref[...]
    stretch = stretch_of(where_ref, table_ref)
    force, force_n, force_s, force_e, force_w = sum_observations(obs_ref, sub, lane)
    spread_rows(par, on_in, off_in, north_ref, south_ref, fields_ref)

    own = force * field_ref[...]
    set_weighted(table_ref, own, add_ref)
    first_weight = table_ref[WEIGHT0 : WEIGHT0 + 1, :]
    along_of, across_of = {}, {}
    for east, halo, ref in ((True, force_e, lon_east_ref), (False, force_w, lon_west_ref)):
        beside = halo * ref[32:40, :]
        turned = pltpu.roll(own, LON - 1 if east else 1, axis=1)
        here = jnp.where(lane == (LON - 1 if east else 0), beside, turned)
        along_of[east] = first_weight * (here - own)
    for north, halo, place in ((True, force_n, 0), (False, force_s, 8)):
        beside = halo * fields_ref[place : place + 8, :]
        shifted = pltpu.roll(own, 7 if north else 1, axis=0)
        here = jnp.where(row == (LAT - 1 if north else 0), beside, shifted)
        across_of[north] = first_weight * (here - own)

    def extra_of(q, x_speed, y_speed):
        north, east = QUADRANTS[q]
        return x_speed * along_of[east] + y_speed * across_of[north]

    def keep(place, jp, gain, extra):
        gain = gain + (add_ref[tab(jp), :] + extra)
        mu_ref[place, :] = gain
        return gain

    gained = edge_gains(
        spectrum_ref, 1, table_ref, stretch, lon_east_ref, lon_west_ref, north_ref, south_ref,
        sub, lane, extra_of, keep,
    )
    coupling = coupling_ref[...] + gained
    energy = energy_ref[...]
    upper = sub >= LAT
    ice = ice_ref[...].astype(F32)
    rate = sea8 * (1.0 - jnp.concatenate([ice, ice], axis=0))
    base = sea8 - 0.2 * rate * energy
    set_weighted(table_ref, 0.2 * rate * coupling, add_ref)
    for copy in copies:
        copy.wait()

    def source(i, carry):
        for jp in range(PAIRS):
            for q in range(4):
                beta = rate_of(beta_ref, i + QUAD * q, jp, upper)
                place = direction_rows(i, q, jp)
                x = (nu_ref[place, :] + mu_ref[place, :]) * (base + rate * beta)
                mu_ref[place, :] = x - add_ref[tab(jp), :]
        return carry

    lax.fori_loop(0, QUAD, source, 0)
    send_rows(par, mu_ref, on_ref, off_ref)


def pack_kernel(mu_ref, west_ref, east_ref):
    _, lane = iotas()
    west_ref[...] = jnp.zeros_like(west_ref)
    east_ref[...] = jnp.zeros_like(east_ref)

    def pack(i, carry):
        pack_edges(west_ref, east_ref, i, lambda q, jp: mu_ref[direction_rows(i, q, jp), :], lane)
        return carry

    lax.fori_loop(0, QUAD, pack, 0)


def first_inner_kernel(
    where_ref, adj_hbm, spectrum_ref, table_ref, sea8_ref, nu_hbm, coupling_ref, energy_ref,
    adj_ref, nu_ref, adj_sems, nu_sems,
):
    over_pieces(adj_hbm, adj_ref, adj_sems, lambda copy: copy.start())
    sub, lane = iotas()
    sea8 = sea8_ref[...]

    def before(i):
        for copy in piecewise(adj_hbm, adj_ref, adj_sems, i):
            copy.wait()

    def after(i):
        for copy in piecewise(nu_ref, nu_hbm, nu_sems, i):
            copy.start()

    coupling_ref[...], energy_ref[...] = move(
        nu_ref, spectrum_ref, 1, table_ref, stretch_of(where_ref, table_ref), sub, lane,
        lambda i, q, jp: adj_ref[direction_rows(i, q, jp), :] * sea8,
        lambda i: lambda q, jp: 0.0, lambda i, q, jp: 0.0, before, after,
    )
    over_pieces(nu_ref, nu_hbm, nu_sems, lambda copy: copy.wait())


def inner_kernel(where_ref, mu_ref, spectrum_ref, table_ref, nu_ref, coupling_ref, energy_ref):
    sub, lane = iotas()
    coupling_ref[...], energy_ref[...] = move(
        nu_ref, spectrum_ref, 0, table_ref, stretch_of(where_ref, table_ref), sub, lane,
        lambda i, q, jp: mu_ref[direction_rows(i, q, jp), :],
        lambda i: lambda q, jp: 0.0, lambda i, q, jp: 0.0,
    )


def last_kernel(
    where_ref, beta_hbm, nu_ref, spectrum_ref, table_ref, ice_ref, coupling_ref, energy_ref,
    on_in, off_in, lon_east_ref, lon_west_ref,
    out_hbm,
    beta_ref, north_ref, south_ref, add_ref, gain_ref, sems, out_sems,
):
    copies = fetch(sems, (beta_hbm, beta_ref))
    par = where_ref[0] % 2
    sub, lane = iotas()
    row = sub % LAT
    spread_rows(par, on_in, off_in, north_ref, south_ref)
    stretch = stretch_of(where_ref, table_ref)

    def keep(place, jp, gain, extra):
        gain_ref[place, :] = gain
        return gain

    gained = edge_gains(
        spectrum_ref, 0, table_ref, stretch, lon_east_ref, lon_west_ref, north_ref, south_ref,
        sub, lane, lambda q, x_speed, y_speed: None, keep,
    )
    coupling = coupling_ref[...] + gained
    upper = sub >= LAT
    ice = ice_ref[...].astype(F32)
    rate = 1.0 - jnp.concatenate([ice, ice], axis=0)
    base = 1.0 - 0.2 * rate * energy_ref[...]
    set_weighted(table_ref, 0.2 * rate * coupling, add_ref)
    copies[0].wait()

    def chunk(g):
        rows = pl.ds(pl.multiple_of(g * 4 * BLOCK, 8), 4 * BLOCK)
        return pltpu.make_async_copy(gain_ref.at[rows], out_hbm.at[rows], out_sems.at[g])

    def body(g, carry):
        for jp in range(PAIRS):
            for h in range(4):
                beta = rate_of(beta_ref, 4 * g + h, jp, upper)
                place = pl.ds(pl.multiple_of((4 * g + h) * BLOCK + 8 * jp, 8), 8)
                x = (nu_ref[place, :] + gain_ref[place, :]) * (base + rate * beta)
                gain_ref[place, :] = x - add_ref[tab(jp), :]
        chunk(g).start()
        return carry

    lax.fori_loop(0, NDIR // 4, body, 0)
    for g in range(NDIR // 4):
        chunk(g).wait()


FIRST = 54


def params(limit=24):
    return pltpu.CompilerParams(vmem_limit_bytes=limit * MIB)


def f32(*shape):
    return jax.ShapeDtypeStruct(shape, F32)


def exchange(on, off, west, east):
    n_lon, n_lat = lax.axis_size("lon"), lax.axis_size("lat")
    near = [(i, i ^ 1) for i in range(n_lat)]
    far = [(i, ((i + 1) ^ 1) - 1) for i in range(1, n_lat - 1)]
    off = lax.ppermute(off, "lat", far)
    on = lax.ppermute(on, "lat", near)
    from_east = lax.ppermute(west, "lon", [(i, (i - 1) % n_lon) for i in range(n_lon)])
    from_west = lax.ppermute(east, "lon", [(i, (i + 1) % n_lon) for i in range(n_lon)])
    return on, off, from_east, from_west


def on_device(adj_final, saved, beta, sea_mask, ice_mask, obs_count, obs_cell, obs_value):
    table = jnp.asarray(constant_table())
    where = lax.axis_index("lat").astype(jnp.int32).reshape(1)
    adj = adj_final.reshape(ROWS, LON)
    saved = saved.reshape((STEPS + 1) * ROWS, LON)
    beta = beta.T
    tiles = lambda rows: pltpu.VMEM((rows, LON), F32)
    whole = lambda x: pltpu.VMEM(x.shape, x.dtype)
    level = pltpu.VMEM((ROWS, LON), jnp.bfloat16)
    payload = (f32(HALO, LON), f32(HALO, LON), f32(EDGE, LON), f32(EDGE, LON))
    dma = lambda *n: pltpu.SemaphoreType.DMA(n)

    on, off, west, east, obs, field, sea8, early = pl.pallas_call(
        start_kernel,
        out_shape=(tiles(HALO), tiles(HALO), tiles(EDGE), tiles(EDGE))
        + (tiles(128), tiles(8), tiles(8))
        + (pltpu.VMEM((2 * ROWS, LON), jnp.bfloat16),),
        in_specs=[SMEM] + [HBM] * 7,
        out_specs=(VMEM,) * 8,
        scratch_shapes=[
            tiles(ROWS + 8), level, tiles(BLOCK), whole(sea_mask), whole(obs_count), whole(obs_cell), whole(obs_value), dma(9),
            dma(QUAD, 4),
        ],
        compiler_params=params(FIRST),
        name="edges_and_observations",
    )(where, adj, saved, table, sea_mask, obs_count, obs_cell, obs_value)

    on, off, from_east, from_west = exchange(on, off, west, east)
    obs = lax.all_to_all(obs.reshape(128, 1, 128), ("lon", "lat"), split_axis=0, concat_axis=0, tiled=True)
    obs = obs.reshape(128, 128)

    rates = pltpu.SMEM(beta.shape, F32)

    hint = pl.CostEstimate(flops=20_000_000, bytes_accessed=6_000_000, transcendentals=0)
    nu, coupling, energy = pl.pallas_call(
        first_inner_kernel,
        out_shape=(pltpu.HBM((ROWS, LON), F32), tiles(8), tiles(8)),
        in_specs=[SMEM, HBM] + [VMEM] * 3,
        out_specs=(HBM, VMEM, VMEM),
        scratch_shapes=[tiles(ROWS), tiles(ROWS), dma(QUAD, 4), dma(QUAD, 4)],
        compiler_params=params(),
        cost_estimate=hint,
        name="first_step_inside",
    )(where, pltpu.with_memory_space_constraint(adj, pltpu.HBM), early, table, sea8)
    mu, on, off = pl.pallas_call(
        middle_kernel,
        out_shape=(f32(ROWS + 8, LON),) + payload[:2],
        in_specs=[SMEM, HBM, HBM] + [VMEM] * 12,
        out_specs=(VMEM,) * 3,
        scratch_shapes=[rates, tiles(ROWS), tiles(SPREAD), tiles(SPREAD), tiles(16), tiles(BLOCK), dma(2)],
        compiler_params=params(),
        name="first_step_edges",
    )(
        where, beta, pltpu.with_memory_space_constraint(nu, pltpu.HBM), early, table, sea8, ice_mask, field, coupling, energy, obs, on, off,
        from_east, from_west,
    )

    west, east = pl.pallas_call(
        pack_kernel,
        out_shape=payload[2:],
        in_specs=[VMEM],
        out_specs=(VMEM,) * 2,
        compiler_params=params(),
        cost_estimate=pl.CostEstimate(flops=3_000_000, bytes_accessed=2_200_000, transcendentals=0),
        name="edges_of_first_step",
    )(mu)
    on, off, from_east, from_west = exchange(on, off, west, east)

    nu, coupling, energy = pl.pallas_call(
        inner_kernel,
        out_shape=(f32(ROWS, LON), f32(8, LON), f32(8, LON)),
        in_specs=[SMEM] + [VMEM] * 3,
        out_specs=(VMEM,) * 3,
        compiler_params=params(),
        cost_estimate=hint,
        name="last_step_inside",
    )(where, mu, early, table)
    out = pl.pallas_call(
        last_kernel,
        out_shape=f32(ROWS, LON),
        in_specs=[SMEM, HBM] + [VMEM] * 10,
        out_specs=HBM,
        scratch_shapes=[rates, tiles(SPREAD), tiles(SPREAD), tiles(BLOCK), tiles(ROWS), dma(1), dma(NDIR // 4)],
        compiler_params=params(),
        name="last_step_edges",
    )(where, beta, nu, early, table, ice_mask, coupling, energy, on, off, from_east, from_west)
    return out.reshape(adj_final.shape)


def solution(mesh):
    return jax.shard_map(
        on_device,
        mesh=mesh,
        in_specs=(
            P(None, None, "lat", "lon"),
            P(None, None, None, "lat", "lon"),
            P(),
            P("lat", "lon"),
            P("lat", "lon"),
            P(("lon", "lat"), None),
            P(("lon", "lat"), None),
            P(("lon", "lat"), None),
        ),
        out_specs=P(None, None, "lat", "lon"),
        check_vma=False,
    )
```
